128 devices in a mesh: seq: 32 (over z, x_hi, y), head: 4 (over x_lo, core).
Axes of the slice: x: 4 (x_hi: 2, x_lo: 2; x = x_hi * 2 + x_lo), y: 4, z: 4, core: 2. Of those that a mesh axis runs over, the one named last changes fastest.
Arguments:
- queries: bfloat16 [32768, 2048], P('seq', 'head'), may hold values from -4.5 to 4.5
- keys: bfloat16 [32768, 2048], P('seq', 'head'), may hold values from -4.5 to 4.5
- values: bfloat16 [32768, 2048], P('seq', 'head'), may hold values from -6 to 6
- out_grad: bfloat16 [32768, 2048], P('seq', 'head'), may hold values from -6 to 6
Outputs:
- query_grad: bfloat16 [32768, 2048], P(('seq', 'head'))
- key_grad: bfloat16 [32768, 2048], P(('seq', 'head'))
- value_grad: bfloat16 [32768, 2048], P(('seq', 'head'))
- summary_key_grad: float32 [512, 2048], P('seq', 'head')
- summary_value_grad: float32 [512, 2048], P('seq', 'head')
The draws below stay inside these ranges and needn't reach their ends.
All inputs are finite; a program needn't handle non-finite values.
Results may differ from the reference program's by a relative error of at most 0.006.
Values may be sent and summed in bfloat16 or wider, within the bound.
A program may use at most 128 MiB of HBM per device.

```python
import jax
import jax.numpy as jnp
from jax import lax

HEADS = 16
HEAD_DIM = 128
SPAN = 64
SEQ = 32768


def draw_queries(key, part):
    key = jax.random.fold_in(key, 7)
    shape = (SEQ, HEADS * HEAD_DIM)
    base = jnp.clip(jax.random.normal(key, shape), -4.5, 4.5)
    return base.astype(jnp.bfloat16)


def draw_keys(key, part):
    key = jax.random.fold_in(key, 13)
    shape = (SEQ, HEADS * HEAD_DIM)
    base = jnp.clip(jax.random.normal(key, shape), -4.5, 4.5)
    return base.astype(jnp.bfloat16)


def block_scale(rng, extent, cuts, smallest, top_value):
    gain, own = 1.0, jax.random.fold_in(rng, 6)
    for dim, shards_of in cuts:
        heights = jnp.exp(jax.random.uniform(jax.random.fold_in(own, dim), (shards_of,), jnp.float32, smallest / len(cuts), top_value / len(cuts)))
        gain = gain * jnp.repeat(heights, extent[dim] // shards_of).reshape([-1 if axis == dim else 1 for axis in range(len(extent))])
    return gain


def bell_draw(key, shape, scale, bound, cuts=(), kind=jnp.bfloat16):
    entries = jax.random.normal(key, shape, jnp.float32) * scale
    if len(cuts) > 0:
        entries = block_scale(key, shape, cuts, -0.22, 0.18) * entries
    return jnp.clip(entries, min=-bound, max=bound).astype(kind)


def setup_inputs(seed: int = 0) -> dict:
    splits = jax.random.split(jax.random.key(seed), 5)
    queries = draw_queries(jax.random.fold_in(splits[4], 71), 0)
    keys = draw_keys(jax.random.fold_in(splits[4], 71), 0)
    values = bell_draw(splits[2], (SEQ, HEADS * HEAD_DIM), 1.0, 6.0, ((0, 32), (1, 4)))
    out_grad = bell_draw(splits[3], (SEQ, HEADS * HEAD_DIM), 1.0, 6.0, ((0, 32), (1, 4)))
    return {"queries": queries, "keys": keys, "values": values, "out_grad": out_grad}


def rounded(value):
    return lax.optimization_barrier(value.astype(jnp.bfloat16)).astype(jnp.float32)


def reference(queries, keys, values, out_grad):
    f32 = jnp.float32
    full = lax.Precision.HIGHEST
    seq_len, cols = queries.shape
    heads = cols // HEAD_DIM
    scale = HEAD_DIM ** -0.5
    nch = seq_len // SPAN
    summ_k = (jnp.sum(keys.astype(f32).reshape(nch, SPAN, cols), axis=1) / SPAN).astype(jnp.bfloat16)
    summ_v = (jnp.sum(values.astype(f32).reshape(nch, SPAN, cols), axis=1) / SPAN).astype(jnp.bfloat16)
    sum_keys = summ_k.astype(f32).reshape(nch, heads, HEAD_DIM)
    sum_vals = summ_v.astype(f32).reshape(nch, heads, HEAD_DIM)
    qrows = min(512, seq_len)
    nblk = seq_len // qrows
    ncks = qrows // SPAN
    lane = jnp.arange(SPAN, dtype=jnp.int32)
    causal = lane[:, None] >= lane[None, :]

    def to_rows(local):
        return local.transpose(1, 0, 2).reshape(heads, qrows)

    def from_rows(stats):
        return stats.reshape(heads, ncks, SPAN).transpose(1, 0, 2)

    def block(carry, index):
        acc_k, acc_v = carry
        start = index * qrows
        q_rows = lax.dynamic_slice_in_dim(queries, start, qrows, 0).astype(f32).reshape(qrows, heads, HEAD_DIM)
        k_rows = lax.dynamic_slice_in_dim(keys, start, qrows, 0).astype(f32).reshape(qrows, heads, HEAD_DIM)
        v_rows = lax.dynamic_slice_in_dim(values, start, qrows, 0).astype(f32).reshape(qrows, heads, HEAD_DIM)
        d_rows = lax.dynamic_slice_in_dim(out_grad, start, qrows, 0).astype(f32).reshape(qrows, heads, HEAD_DIM)
        q_ck = q_rows.reshape(ncks, SPAN, heads, HEAD_DIM)
        k_ck = k_rows.reshape(ncks, SPAN, heads, HEAD_DIM)
        v_ck = v_rows.reshape(ncks, SPAN, heads, HEAD_DIM)
        d_ck = d_rows.reshape(ncks, SPAN, heads, HEAD_DIM)
        row_span = (start // SPAN + jnp.arange(qrows, dtype=jnp.int32) // SPAN).astype(jnp.int32)
        local = jnp.einsum('nqhe,nkhe->nhqk', q_ck, k_ck) * scale
        local = jnp.where(causal, local, -jnp.inf)
        summed = jnp.einsum('qhe,jhe->hqj', q_rows, sum_keys) * scale
        seen = jnp.arange(nch, dtype=jnp.int32)[None, :] < row_span[:, None]
        summed = jnp.where(seen[None], summed, -jnp.inf)
        top = jnp.maximum(to_rows(jnp.max(local, axis=-1)), jnp.max(summed, axis=-1))
        total = to_rows(jnp.sum(jnp.exp(local - from_rows(top)[..., None]), axis=-1))
        total = total + jnp.sum(jnp.exp(summed - top[..., None]), axis=-1)
        lse = top + jnp.log(total)
        p_loc = jnp.exp(local - from_rows(lse)[..., None])
        p_sum = jnp.exp(summed - lse[..., None])
        dp_loc = jnp.einsum('nqhe,nkhe->nhqk', d_ck, v_ck)
        dp_sum = jnp.einsum('qhe,jhe->hqj', d_rows, sum_vals)
        delta = to_rows(jnp.sum(p_loc * dp_loc, axis=-1)) + jnp.sum(p_sum * dp_sum, axis=-1)
        g_loc = rounded(p_loc * (dp_loc - from_rows(delta)[..., None]))
        g_sum = p_sum * (dp_sum - delta[..., None])
        pb_loc = rounded(p_loc)
        pb_sum = p_sum
        dq_part = jnp.einsum('nhqk,nkhe->nqhe', g_loc, k_ck).reshape(qrows, heads, HEAD_DIM)
        dq_rows = scale * (dq_part + jnp.einsum('hqj,jhe->qhe', g_sum, sum_keys, precision=full))
        dk_rows = scale * jnp.einsum('nhqk,nqhe->nkhe', g_loc, q_ck)
        dv_rows = jnp.einsum('nhqk,nqhe->nkhe', pb_loc, d_ck)
        acc_k = acc_k + scale * jnp.einsum('hqj,qhe->jhe', g_sum, q_rows, precision=full)
        acc_v = acc_v + jnp.einsum('hqj,qhe->jhe', pb_sum, d_rows, precision=full)
        outs = (dq_rows.reshape(qrows, cols), dk_rows.reshape(qrows, cols), dv_rows.reshape(qrows, cols))
        return (acc_k, acc_v), outs

    empty = jnp.zeros((nch, heads, HEAD_DIM), f32)
    (acc_k, acc_v), (dq_all, dk_all, dv_all) = lax.scan(block, (empty, empty), jnp.arange(nblk, dtype=jnp.int32))
    grad_k = acc_k.reshape(nch, cols)
    grad_v = acc_v.reshape(nch, cols)
    dq_all = dq_all.reshape(seq_len, cols)
    dk_all = dk_all.reshape(seq_len, cols) + jnp.repeat(grad_k, SPAN, axis=0) / SPAN
    dv_all = dv_all.reshape(seq_len, cols) + jnp.repeat(grad_v, SPAN, axis=0) / SPAN
    return (dq_all.astype(jnp.bfloat16), dk_all.astype(jnp.bfloat16), dv_all.astype(jnp.bfloat16), grad_k, grad_v)
```

```python
import functools

import jax
import jax.numpy as jnp
from jax import lax
from jax.experimental import pallas as pl
from jax.experimental.pallas import tpu as pltpu
from jax.sharding import PartitionSpec as P

HEAD_DIM = 128
SPAN = 64
MESH = pl.DeviceIdType.MESH
LOG2E = 1.4426950408889634
F32 = jnp.float32
BF16 = jnp.bfloat16
NT = (((1,), (1,)), ((), ()))
NN = (((1,), (0,)), ((), ()))
TN = (((0,), (0,)), ((), ()))


def dot(a, b, dims):
    return lax.dot_general(a, b, dims, preferred_element_type=F32)


def tile_order(hd, j):
    chip = lax.rem(hd // 2 + 1 + j // 2, 2)
    core = lax.rem(lax.rem(hd, 2) + j + j // 2, 2)
    return chip * 2 + core


def main_kernel(
    nseq,
    nhead,
    q_hbm, k_hbm, v_hbm, d_hbm,
    out, gk_out, gv_out, shared,
    q_ref, k_ref, v_ref, d_ref,
    summ, summ_t, acc, term, rterm, own, sgs, stage, s_scr, e_scr, dp_scr,
    load_sem, gsend, grecv, rsend, rrecv, asend, arecv, local_sem, ssend, srecv, own_sem,
):
    me = lax.axis_index("seq")
    hd = lax.axis_index("head")
    count = q_ref.shape[0]
    heads = q_ref.shape[1] // HEAD_DIM
    per_dev = count // SPAN
    total = per_dev * nseq
    tile = count // nhead
    scale = HEAD_DIM ** (-0.5)
    c2 = scale * LOG2E

    loads = [
        pltpu.make_async_copy(src, dst, load_sem.at[i])
        for i, (src, dst) in enumerate(
            ((k_hbm, k_ref), (v_hbm, v_ref), (q_hbm, q_ref), (d_hbm, d_ref))
        )
    ]
    for load in loads:
        load.start()
    summ[...] = jnp.zeros(summ.shape, summ.dtype)

    barrier = pltpu.get_barrier_semaphore()

    def greet(i, _):
        pl.semaphore_signal(
            barrier, inc=1, device_id={"seq": lax.rem(me + i, nseq)}, device_id_type=MESH
        )
        return 0

    lax.fori_loop(1, nseq, greet, 0)
    for i in range(1, nhead):
        pl.semaphore_signal(
            barrier, inc=1, device_id={"head": lax.rem(hd + i, nhead)}, device_id_type=MESH
        )

    pool = (
        lax.broadcasted_iota(jnp.int32, (per_dev, count), 1) // SPAN
        == lax.broadcasted_iota(jnp.int32, (per_dev, count), 0)
    ).astype(BF16)
    loads[0].wait()
    mean_k = (dot(pool, k_ref[...], NN) * (1.0 / SPAN)).astype(BF16)
    loads[1].wait()
    mean_v = (dot(pool, v_ref[...], NN) * (1.0 / SPAN)).astype(BF16)
    summ[me, 0] = mean_k
    summ[me, 1] = mean_v

    pl.semaphore_wait(barrier, nseq - 1 + nhead - 1)

    def gather_copy(src, dst):
        return pltpu.make_async_remote_copy(
            src_ref=summ.at[src],
            dst_ref=summ.at[src],
            send_sem=gsend.at[dst],
            recv_sem=grecv.at[src],
            device_id={"seq": dst},
            device_id_type=MESH,
        )

    def gather_start(dst, _):
        gather_copy(me, dst).start()
        return 0

    lax.fori_loop(me + 1, nseq, gather_start, 0)
    loads[2].wait()
    loads[3].wait()

    def gather_wait(src, _):
        gather_copy(src, 0).wait_recv()
        return 0

    lax.fori_loop(0, me, gather_wait, 0)

    rows = 128
    nchunk = total // rows
    shards = rows // per_dev
    lane = lax.broadcasted_iota(jnp.int32, (SPAN, tile), 1)
    low_lane = lax.rem(lane, 2 * SPAN) < SPAN
    causal = lax.broadcasted_iota(jnp.int32, (SPAN, tile), 0) <= lax.rem(lane, SPAN)
    low128 = low_lane[:, : 2 * SPAN]

    def fold(x, op):
        parts = [x[8 * i : 8 * i + 8] for i in range(x.shape[0] // 8)]
        while len(parts) > 1:
            parts = [
                op(parts[i], parts[i + 1]) if i + 1 < len(parts) else parts[i]
                for i in range(0, len(parts), 2)
            ]
        return parts[0]

    def step(n, _):
        h = n // nhead
        j = lax.rem(n, nhead)
        i = tile_order(hd, j)
        cols = pl.ds(pl.multiple_of(h * HEAD_DIM, HEAD_DIM), HEAD_DIM)
        trow = pl.ds(pl.multiple_of(i * tile, tile), tile)

        def sk(c):
            return summ[c * shards : (c + 1) * shards, 0, :, cols].reshape(rows, HEAD_DIM)

        def sv(c):
            return summ[c * shards : (c + 1) * shards, 1, :, cols].reshape(rows, HEAD_DIM)

        @pl.when(j == 0)
        def _():
            for c in range(nchunk):
                summ_t[:, c * rows : (c + 1) * rows] = sk(c).astype(F32).T.astype(BF16)
            acc[...] = jnp.zeros(acc.shape, F32)

        qt = q_ref[trow, cols]
        kt = k_ref[trow, cols]
        vt = v_ref[trow, cols]
        dt = d_ref[trow, cols]

        def local(a, b):
            picked = []
            for p in range(tile // (2 * SPAN)):
                sl = slice(p * 2 * SPAN, (p + 1) * 2 * SPAN)
                full = dot(a[sl], b[sl], NT)
                picked.append(jnp.where(low128, full[:SPAN], full[SPAN:]))
            return jnp.concatenate(picked, axis=1)

        a_loc = jnp.where(causal, local(kt, qt), -jnp.inf)
        dp_loc = local(vt, dt)
        span_of = (
            me * per_dev
            + i * (tile // SPAN)
            + lax.broadcasted_iota(jnp.int32, (rows, tile), 1) // SPAN
        )
        row_id = lax.broadcasted_iota(jnp.int32, (rows, tile), 0)
        top = fold(a_loc, jnp.maximum)
        for c in range(nchunk):
            s = dot(sk(c), qt, NT)
            s = jnp.where(row_id + c * rows < span_of, s, -jnp.inf)
            s_scr[c * rows : (c + 1) * rows] = s
            top = jnp.maximum(top, fold(s, jnp.maximum))
        top = jnp.max(top, axis=0, keepdims=True)
        base = top * c2

        e_loc = jnp.exp2(a_loc * c2 - base)
        mass = fold(e_loc, jnp.add)
        weighted = fold(e_loc * dp_loc, jnp.add)
        for c in range(nchunk):
            sl = slice(c * rows, (c + 1) * rows)
            dp = dot(sv(c), dt, NT)
            e = jnp.exp2(s_scr[sl] * c2 - base)
            e_scr[sl] = e
            dp_scr[sl] = dp
            mass = mass + fold(e, jnp.add)
            weighted = weighted + fold(e * dp, jnp.add)
        inv = 1.0 / jnp.sum(mass, axis=0, keepdims=True)
        delta = jnp.sum(weighted, axis=0, keepdims=True) * inv

        p_loc = e_loc * inv
        g_loc = p_loc * (dp_loc - delta)
        zero = jnp.zeros((SPAN, 2 * SPAN), F32)
        dqt_parts = []
        for p in range(tile // (2 * SPAN)):
            sl = slice(p * 2 * SPAN, (p + 1) * 2 * SPAN)
            g = g_loc[:, sl]
            w = p_loc[:, sl]
            g2 = jnp.concatenate(
                [jnp.where(low128, g, zero), jnp.where(low128, zero, g)], axis=0
            ).astype(BF16)
            w2 = jnp.concatenate(
                [jnp.where(low128, w, zero), jnp.where(low128, zero, w)], axis=0
            ).astype(BF16)
            stage[n, 1, sl] = (dot(g2, qt[sl], NN) * scale).astype(BF16)
            stage[n, 2, sl] = dot(w2, dt[sl], NN).astype(BF16)
            dqt_parts.append(dot(kt[sl], g2, TN))
        dqt = jnp.concatenate(dqt_parts, axis=1)
        for c in range(nchunk):
            sl = slice(c * rows, (c + 1) * rows)
            r = e_scr[sl] * inv
            g = (r * (dp_scr[sl] - delta)).astype(BF16)
            acc[0, sl] += dot(g, qt, NN)
            acc[1, sl] += dot(r.astype(BF16), dt, NN)
            dqt = dqt + dot(summ_t[:, sl], g, NN)
        stage[n, 0] = (dqt * scale).T.astype(BF16)

        slot = hd * heads + h

        @pl.when(j < nhead - 1)
        def _():
            pltpu.make_async_remote_copy(
                src_ref=stage.at[n],
                dst_ref=out.at[slot],
                send_sem=asend.at[n],
                recv_sem=arecv.at[hd],
                device_id={"head": i},
                device_id_type=MESH,
            ).start()

        @pl.when(j == nhead - 1)
        def _():
            pltpu.make_async_copy(stage.at[n], out.at[slot], local_sem.at[h]).start()
            for w in range(2):
                term[:, h, w] = acc[w].reshape(nseq, per_dev, HEAD_DIM).astype(BF16)
                own[w, :, cols] = acc[w, pl.ds(pl.multiple_of(me * per_dev, per_dev), per_dev)]

            def send_term(k, _):
                dst = me - 1 - k
                pltpu.make_async_remote_copy(
                    src_ref=term.at[dst, h],
                    dst_ref=rterm.at[me, h],
                    send_sem=rsend.at[dst],
                    recv_sem=rrecv.at[me],
                    device_id={"seq": dst},
                    device_id_type=MESH,
                ).start()
                return 0

            lax.fori_loop(0, me, send_term, 0)

        return 0

    lax.fori_loop(0, heads * nhead, step, 0)

    def term_all(a, b):
        return pltpu.make_async_remote_copy(
            src_ref=term.at[a],
            dst_ref=rterm.at[b],
            send_sem=rsend.at[a],
            recv_sem=rrecv.at[b],
            device_id={"seq": a},
            device_id_type=MESH,
        )

    def add_term(src, _):
        term_all(0, src).wait_recv()
        for w in range(2):
            for h in range(heads):
                sl = slice(h * HEAD_DIM, (h + 1) * HEAD_DIM)
                own[w, :, sl] += rterm[src, h, w].astype(F32)
        return 0

    lax.fori_loop(me + 1, nseq, add_term, 0)
    grad_k = own[0] * scale
    grad_v = own[1]
    gk_out[...] = grad_k
    gv_out[...] = grad_v
    part = per_dev // nhead
    for dst in range(nhead):
        sgs[dst, 0:part] = grad_k[dst * part : (dst + 1) * part] * (1.0 / SPAN)
        sgs[dst, part : 2 * part] = grad_v[dst * part : (dst + 1) * part] * (1.0 / SPAN)

    def shared_copy(src, dst, slot):
        return pltpu.make_async_remote_copy(
            src_ref=sgs.at[dst],
            dst_ref=shared.at[src],
            send_sem=ssend.at[slot],
            recv_sem=srecv.at[src],
            device_id={"head": dst},
            device_id_type=MESH,
        )

    for k in range(1, nhead):
        shared_copy(hd, lax.rem(hd + k, nhead), k).start()
    mine = pltpu.make_async_copy(sgs.at[hd], shared.at[hd], own_sem)
    mine.start()
    mine.wait()
    for k in range(1, nhead):
        other = lax.rem(hd + k, nhead)
        shared_copy(hd, other, k).wait_send()
        shared_copy(other, other, k).wait_recv()
        pltpu.make_async_remote_copy(
            src_ref=stage.at[0],
            dst_ref=out.at[pl.ds(other * heads, heads)],
            send_sem=asend.at[0],
            recv_sem=arecv.at[other],
            device_id={"head": other},
            device_id_type=MESH,
        ).wait_recv()

    def sent_all(n, _):
        @pl.when(lax.rem(n, nhead) < nhead - 1)
        def _():
            pltpu.make_async_remote_copy(
                src_ref=stage.at[n],
                dst_ref=out.at[0],
                send_sem=asend.at[n],
                recv_sem=arecv.at[hd],
                device_id={"head": lax.rem(hd + 1, nhead)},
                device_id_type=MESH,
            ).wait_send()

        return 0

    lax.fori_loop(0, heads * nhead, sent_all, 0)
    for h in range(heads):
        pltpu.make_async_copy(
            stage.at[h * nhead + nhead - 1], out.at[hd * heads + h], local_sem.at[h]
        ).wait()

    def gather_sent(dst, _):
        gather_copy(me, dst).wait_send()
        return 0

    lax.fori_loop(me + 1, nseq, gather_sent, 0)

    def terms_sent(dst, _):
        term_all(dst, me).wait_send()
        return 0

    lax.fori_loop(0, me, terms_sent, 0)


def finish_kernel(part, in_ref, shared_ref, q_out, k_out, v_out):
    heads = in_ref.shape[0]
    for h in range(heads):
        sl = slice(h * HEAD_DIM, (h + 1) * HEAD_DIM)
        q_out[:, sl] = in_ref[h, 0]
        for w, ref in ((0, k_out), (1, v_out)):
            for c in range(part):
                rows = slice(c * SPAN, (c + 1) * SPAN)
                add = shared_ref[0, w * part + c : w * part + c + 1, sl]
                ref[rows, sl] = (in_ref[h, 1 + w, rows].astype(F32) + add).astype(BF16)


def per_device(queries, keys, values, out_grad):
    count, cols = queries.shape
    nseq = lax.axis_size("seq")
    nhead = lax.axis_size("head")
    heads = cols // HEAD_DIM
    per_dev = count // SPAN
    total = per_dev * nseq
    tile = count // nhead
    part = per_dev // nhead
    steps = heads * nhead
    anyspace = pl.BlockSpec(memory_space=pl.ANY)
    vmem = pl.BlockSpec(memory_space=pltpu.VMEM)
    dma = pltpu.SemaphoreType.DMA
    pieces, grad_k, grad_v, shared = pl.pallas_call(
        functools.partial(main_kernel, nseq, nhead),
        out_shape=(
            jax.ShapeDtypeStruct((nhead * heads, 3, tile, HEAD_DIM), BF16),
            jax.ShapeDtypeStruct((per_dev, cols), F32),
            jax.ShapeDtypeStruct((per_dev, cols), F32),
            jax.ShapeDtypeStruct((nhead, 2 * part, cols), F32),
        ),
        in_specs=[anyspace] * 4,
        out_specs=(anyspace, vmem, vmem, anyspace),
        scratch_shapes=[pltpu.VMEM((count, cols), BF16)] * 4
        + [
            pltpu.VMEM((nseq, 2, per_dev, cols), BF16),
            pltpu.VMEM((HEAD_DIM, total), BF16),
            pltpu.VMEM((2, total, HEAD_DIM), F32),
            pltpu.VMEM((nseq, heads, 2, per_dev, HEAD_DIM), BF16),
            pltpu.VMEM((nseq, heads, 2, per_dev, HEAD_DIM), BF16),
            pltpu.VMEM((2, per_dev, cols), F32),
            pltpu.VMEM((nhead, 2 * part, cols), F32),
            pltpu.VMEM((steps, 3, tile, HEAD_DIM), BF16),
            pltpu.VMEM((total, tile), F32),
            pltpu.VMEM((total, tile), F32),
            pltpu.VMEM((total, tile), F32),
            dma((4,)),
            dma((nseq,)),
            dma((nseq,)),
            dma((nseq,)),
            dma((nseq,)),
            dma((steps,)),
            dma((nhead,)),
            dma((heads,)),
            dma((nhead,)),
            dma((nhead,)),
            dma,
        ],
        compiler_params=pltpu.CompilerParams(
            collective_id=0, has_side_effects=True, vmem_limit_bytes=40 * 1024 * 1024
        ),
        name="attend",
    )(queries, keys, values, out_grad)
    row = jax.ShapeDtypeStruct((tile, nhead * cols), BF16)
    col_block = pl.BlockSpec((tile, cols), lambda g: (0, g))
    query_grad, key_grad, value_grad = pl.pallas_call(
        functools.partial(finish_kernel, part),
        out_shape=(row, row, row),
        grid=(nhead,),
        in_specs=[
            pl.BlockSpec((heads, 3, tile, HEAD_DIM), lambda g: (g, 0, 0, 0)),
            pl.BlockSpec((1, 2 * part, cols), lambda g: (g, 0, 0)),
        ],
        out_specs=(col_block, col_block, col_block),
        name="finish",
    )(pieces, shared)
    return (query_grad, key_grad, value_grad, grad_k, grad_v)


def solution(mesh):
    placed = (P("seq", "head"), P("seq", "head"), P("seq", "head"), P("seq", "head"))
    return jax.shard_map(
        per_device,
        mesh=mesh,
        in_specs=placed,
        out_specs=(
            P(("seq", "head"), None),
            P(("seq", "head"), None),
            P(("seq", "head"), None),
            P("seq", "head"),
            P("seq", "head"),
        ),
        check_vma=False,
    )
```

```python
import functools

import jax
import jax.numpy as jnp
from jax import lax
from jax.experimental import pallas as pl
from jax.experimental.pallas import tpu as pltpu
from jax.sharding import PartitionSpec as P

HEAD_DIM = 128
SPAN = 64
PLACES = 4
SLAB = 8
MESH = pl.DeviceIdType.MESH
LOG2E = 1.4426950408889634
F32 = jnp.float32
BF16 = jnp.bfloat16
NT = (((1,), (1,)), ((), ()))
NN = (((1,), (0,)), ((), ()))
TN = (((0,), (0,)), ((), ()))


def dot(a, b, dims):
    return lax.dot_general(a, b, dims, preferred_element_type=F32)


def tile_order(hd, j):
    chip = lax.rem(hd // 2 + 1 + j // 2, 2)
    core = lax.rem(lax.rem(hd, 2) + j + j // 2, 2)
    return chip * 2 + core


def main_kernel(
    nseq,
    nhead,
    q_hbm, k_hbm, v_hbm, d_hbm,
    out, gk_out, gv_out, shared,
    q_ref, k_ref, v_ref, d_ref,
    summ, summ_t, acc, term, rterm, own, other_own, sgs, stage, s_scr, e_scr, dp_scr,
    load_sem, xsend, xrecv, gsend, grecv, rsend, rrecv, psend, precv,
    asend, arecv, local_sem, ssend, srecv, own_sem,
):
    me = lax.axis_index("seq")
    hd = lax.axis_index("head")
    count = q_ref.shape[0]
    heads = q_ref.shape[1] // HEAD_DIM
    per_dev = count // SPAN
    total = per_dev * nseq
    tile = count // nhead
    scale = HEAD_DIM ** (-0.5)
    c2 = scale * LOG2E
    slab = me // SLAB
    side = lax.rem(me, SLAB) // PLACES
    plane = slab * PLACES + lax.rem(me, PLACES)
    nplane = nseq // 2
    partner = me + PLACES - 2 * PLACES * side

    def shard_at(p):
        return (p // PLACES) * SLAB + side * PLACES + lax.rem(p, PLACES)

    loads = [
        [
            pltpu.make_async_copy(
                src.at[c * tile : (c + 1) * tile], dst.at[c * tile : (c + 1) * tile], load_sem.at[i, c]
            )
            for c in range(nhead)
        ]
        for i, (src, dst) in enumerate(
            ((k_hbm, k_ref), (v_hbm, v_ref), (q_hbm, q_ref), (d_hbm, d_ref))
        )
    ]
    for group in loads:
        for load in group:
            load.start()
    summ[...] = jnp.zeros(summ.shape, summ.dtype)

    barrier = pltpu.get_barrier_semaphore()

    def greet(i, _):
        pl.semaphore_signal(
            barrier,
            inc=1,
            device_id={"seq": shard_at(lax.rem(plane + i, nplane))},
            device_id_type=MESH,
        )
        return 0

    lax.fori_loop(1, nplane, greet, 0)
    pl.semaphore_signal(barrier, inc=1, device_id={"seq": partner}, device_id_type=MESH)
    for i in range(1, nhead):
        pl.semaphore_signal(
            barrier, inc=1, device_id={"head": lax.rem(hd + i, nhead)}, device_id_type=MESH
        )

    pool = (
        lax.broadcasted_iota(jnp.int32, (per_dev, count), 1) // SPAN
        == lax.broadcasted_iota(jnp.int32, (per_dev, count), 0)
    ).astype(BF16)
    for w, ref in ((0, k_ref), (1, v_ref)):
        for load in loads[w]:
            load.wait()
        mean = (dot(pool, ref[...], NN) * (1.0 / SPAN)).astype(BF16)
        for h in range(heads):
            summ[h, plane, side, w] = mean[:, h * HEAD_DIM : (h + 1) * HEAD_DIM]

    pl.semaphore_wait(barrier, nplane - 1 + 1 + nhead - 1)

    def swap_copy(h, to):
        return pltpu.make_async_remote_copy(
            src_ref=summ.at[h, plane, to],
            dst_ref=summ.at[h, plane, to],
            send_sem=xsend.at[h],
            recv_sem=xrecv.at[h],
            device_id={"seq": partner},
            device_id_type=MESH,
        )

    def gather_copy(h, src, dst):
        return pltpu.make_async_remote_copy(
            src_ref=summ.at[h, src],
            dst_ref=summ.at[h, src],
            send_sem=gsend.at[h, dst],
            recv_sem=grecv.at[h, src],
            device_id={"seq": shard_at(dst)},
            device_id_type=MESH,
        )

    first = slab * PLACES
    later = nplane - first
    earlier = first + PLACES

    def to_later(k):
        return first + lax.rem(plane - first + k, later)

    def to_earlier(k):
        return lax.rem(plane + k, earlier)

    for h in range(heads):
        swap_copy(h, side).start()
    for h in range(heads):
        swap_copy(h, 1 - side).wait_recv()

        def gather_start(k, _, h=h):
            gather_copy(h, plane, to_later(k)).start()
            return 0

        lax.fori_loop(1, later, gather_start, 0)
    for group in loads[2:]:
        for load in group:
            load.wait()

    rows = 128
    nchunk = total // rows
    group = rows // (2 * per_dev)
    lane = lax.broadcasted_iota(jnp.int32, (SPAN, tile), 1)
    low_lane = lax.rem(lane, 2 * SPAN) < SPAN
    causal = lax.broadcasted_iota(jnp.int32, (SPAN, tile), 0) <= lax.rem(lane, SPAN)
    low128 = low_lane[:, : 2 * SPAN]

    def fold(x, op):
        parts = [x[8 * i : 8 * i + 8] for i in range(x.shape[0] // 8)]
        while len(parts) > 1:
            parts = [
                op(parts[i], parts[i + 1]) if i + 1 < len(parts) else parts[i]
                for i in range(0, len(parts), 2)
            ]
        return parts[0]

    def term_copy(h, dst, src):
        return pltpu.make_async_remote_copy(
            src_ref=term.at[dst, h],
            dst_ref=rterm.at[src, h],
            send_sem=rsend.at[h, dst],
            recv_sem=rrecv.at[h, src],
            device_id={"seq": shard_at(dst)},
            device_id_type=MESH,
        )

    def step(n, _):
        h = n // nhead
        j = lax.rem(n, nhead)
        i = tile_order(hd, j)
        cols = pl.ds(pl.multiple_of(h * HEAD_DIM, HEAD_DIM), HEAD_DIM)
        trow = pl.ds(pl.multiple_of(i * tile, tile), tile)

        def sk(c):
            return summ[h, c * group : (c + 1) * group, :, 0].reshape(rows, HEAD_DIM)

        def sv(c):
            return summ[h, c * group : (c + 1) * group, :, 1].reshape(rows, HEAD_DIM)

        @pl.when(j == 0)
        def _():
            def gather_wait(k, _):
                gather_copy(h, to_earlier(k), plane).wait_recv()
                return 0

            lax.fori_loop(1, earlier, gather_wait, 0)
            for c in range(nchunk):
                summ_t[:, c * rows : (c + 1) * rows] = sk(c).astype(F32).T.astype(BF16)
            acc[...] = jnp.zeros(acc.shape, F32)

        qt = q_ref[trow, cols]
        kt = k_ref[trow, cols]
        vt = v_ref[trow, cols]
        dt = d_ref[trow, cols]

        def local(a, b):
            picked = []
            for p in range(tile // (2 * SPAN)):
                sl = slice(p * 2 * SPAN, (p + 1) * 2 * SPAN)
                full = dot(a[sl], b[sl], NT)
                picked.append(jnp.where(low128, full[:SPAN], full[SPAN:]))
            return jnp.concatenate(picked, axis=1)

        a_loc = jnp.where(causal, local(kt, qt), -jnp.inf)
        dp_loc = local(vt, dt)
        span_of = (
            me * per_dev
            + i * (tile // SPAN)
            + lax.broadcasted_iota(jnp.int32, (rows, tile), 1) // SPAN
        )
        place_row = lax.broadcasted_iota(jnp.int32, (rows, tile), 0)
        pair = place_row // per_dev
        row_id = (
            (lax.rem(pair, 2) * PLACES + pair // 2) * per_dev + lax.rem(place_row, per_dev)
        )
        top = fold(a_loc, jnp.maximum)
        for c in range(nchunk):
            s = dot(sk(c), qt, NT)
            s = jnp.where(row_id + c * rows < span_of, s, -jnp.inf)
            s_scr[c * rows : (c + 1) * rows] = s
            top = jnp.maximum(top, fold(s, jnp.maximum))
        top = jnp.max(top, axis=0, keepdims=True)
        base = top * c2

        e_loc = jnp.exp2(a_loc * c2 - base)
        mass = fold(e_loc, jnp.add)
        weighted = fold(e_loc * dp_loc, jnp.add)
        for c in range(nchunk):
            sl = slice(c * rows, (c + 1) * rows)
            dp = dot(sv(c), dt, NT)
            e = jnp.exp2(s_scr[sl] * c2 - base)
            e_scr[sl] = e
            dp_scr[sl] = dp
            mass = mass + fold(e, jnp.add)
            weighted = weighted + fold(e * dp, jnp.add)
        inv = 1.0 / jnp.sum(mass, axis=0, keepdims=True)
        delta = jnp.sum(weighted, axis=0, keepdims=True) * inv

        p_loc = e_loc * inv
        g_loc = p_loc * (dp_loc - delta)
        zero = jnp.zeros((SPAN, 2 * SPAN), F32)
        dqt_parts = []
        for p in range(tile // (2 * SPAN)):
            sl = slice(p * 2 * SPAN, (p + 1) * 2 * SPAN)
            g = g_loc[:, sl]
            w = p_loc[:, sl]
            g2 = jnp.concatenate(
                [jnp.where(low128, g, zero), jnp.where(low128, zero, g)], axis=0
            ).astype(BF16)
            w2 = jnp.concatenate(
                [jnp.where(low128, w, zero), jnp.where(low128, zero, w)], axis=0
            ).astype(BF16)
            stage[n, 1, sl] = (dot(g2, qt[sl], NN) * scale).astype(BF16)
            stage[n, 2, sl] = dot(w2, dt[sl], NN).astype(BF16)
            dqt_parts.append(dot(kt[sl], g2, TN))
        dqt = jnp.concatenate(dqt_parts, axis=1)
        for c in range(nchunk):
            sl = slice(c * rows, (c + 1) * rows)
            r = e_scr[sl] * inv
            g = (r * (dp_scr[sl] - delta)).astype(BF16)
            acc[0, sl] += dot(g, qt, NN)
            acc[1, sl] += dot(r.astype(BF16), dt, NN)
            dqt = dqt + dot(summ_t[:, sl], g, NN)
        stage[n, 0] = (dqt * scale).T.astype(BF16)

        slot = hd * heads + h

        @pl.when(j < nhead - 1)
        def _():
            pltpu.make_async_remote_copy(
                src_ref=stage.at[n],
                dst_ref=out.at[slot],
                send_sem=asend.at[n],
                recv_sem=arecv.at[hd],
                device_id={"head": i},
                device_id_type=MESH,
            ).start()

        @pl.when(j == nhead - 1)
        def _():
            pltpu.make_async_copy(stage.at[n], out.at[slot], local_sem.at[h]).start()
            mine = pl.ds(pl.multiple_of(plane * 2 * per_dev, 2 * per_dev), 2 * per_dev)
            for w in range(2):
                term[:, h, :, w] = acc[w].reshape(nplane, 2, per_dev, HEAD_DIM).astype(BF16)
                own[:, h, w] = acc[w, mine].reshape(2, per_dev, HEAD_DIM)

            def send_term(k, _):
                dst = to_earlier(k)
                term_copy(h, dst, plane).start()
                return 0

            lax.fori_loop(1, earlier, send_term, 0)

        return 0

    lax.fori_loop(0, heads * nhead, step, 0)

    for h in range(heads):

        def add_term(k, _, h=h):
            src = to_later(k)
            term_copy(h, plane, src).wait_recv()
            own[:, h] += rterm[src, h].astype(F32)
            return 0

        lax.fori_loop(1, later, add_term, 0)

    partial = pltpu.make_async_remote_copy(
        src_ref=own.at[1 - side],
        dst_ref=other_own,
        send_sem=psend,
        recv_sem=precv,
        device_id={"seq": partner},
        device_id_type=MESH,
    )
    partial.start()
    partial.wait()
    grads = [
        jnp.concatenate([own[side, h, w] + other_own[h, w] for h in range(heads)], axis=1)
        for w in range(2)
    ]
    grad_k = grads[0] * scale
    grad_v = grads[1]
    gk_out[...] = grad_k
    gv_out[...] = grad_v
    part = per_dev // nhead
    for dst in range(nhead):
        sgs[dst, 0:part] = grad_k[dst * part : (dst + 1) * part] * (1.0 / SPAN)
        sgs[dst, part : 2 * part] = grad_v[dst * part : (dst + 1) * part] * (1.0 / SPAN)

    def shared_copy(src, dst, slot):
        return pltpu.make_async_remote_copy(
            src_ref=sgs.at[dst],
            dst_ref=shared.at[src],
            send_sem=ssend.at[slot],
            recv_sem=srecv.at[src],
            device_id={"head": dst},
            device_id_type=MESH,
        )

    for k in range(1, nhead):
        shared_copy(hd, lax.rem(hd + k, nhead), k).start()
    mine = pltpu.make_async_copy(sgs.at[hd], shared.at[hd], own_sem)
    mine.start()
    mine.wait()
    for k in range(1, nhead):
        other = lax.rem(hd + k, nhead)
        shared_copy(hd, other, k).wait_send()
        shared_copy(other, other, k).wait_recv()
        pltpu.make_async_remote_copy(
            src_ref=stage.at[0],
            dst_ref=out.at[pl.ds(other * heads, heads)],
            send_sem=asend.at[0],
            recv_sem=arecv.at[other],
            device_id={"head": other},
            device_id_type=MESH,
        ).wait_recv()

    def sent_all(n, _):
        @pl.when(lax.rem(n, nhead) < nhead - 1)
        def _():
            pltpu.make_async_remote_copy(
                src_ref=stage.at[n],
                dst_ref=out.at[0],
                send_sem=asend.at[n],
                recv_sem=arecv.at[hd],
                device_id={"head": lax.rem(hd + 1, nhead)},
                device_id_type=MESH,
            ).wait_send()

        return 0

    lax.fori_loop(0, heads * nhead, sent_all, 0)
    for h in range(heads):
        pltpu.make_async_copy(
            stage.at[h * nhead + nhead - 1], out.at[hd * heads + h], local_sem.at[h]
        ).wait()

    for h in range(heads):
        swap_copy(h, side).wait_send()

        def gather_sent(k, _, h=h):
            gather_copy(h, plane, to_later(k)).wait_send()
            return 0

        def term_sent(k, _, h=h):
            term_copy(h, to_earlier(k), plane).wait_send()
            return 0

        lax.fori_loop(1, later, gather_sent, 0)
        lax.fori_loop(1, earlier, term_sent, 0)


def finish_kernel(
    part, pieces, shared_ref, gk_in, gv_in, q_out, k_out, v_out, gk_out, gv_out, kv, q_buf, k_buf, v_buf, load_sem, sem
):
    heads = pieces.shape[0]
    cols = shared_ref.shape[2]
    group = cols // HEAD_DIM
    loads = [
        pltpu.make_async_copy(pieces.at[h, 1:], kv.at[h], load_sem.at[0, h]) for h in range(heads)
    ]
    q_loads = [
        pltpu.make_async_copy(
            pieces.at[h, 0], q_buf.at[:, pl.ds(h * HEAD_DIM, HEAD_DIM)], load_sem.at[1, h]
        )
        for h in range(heads)
    ]
    copies = [
        pltpu.make_async_copy(gk_in, gk_out, sem.at[0]),
        pltpu.make_async_copy(gv_in, gv_out, sem.at[1]),
    ]
    for q_load, load in zip(q_loads, loads):
        q_load.start()
        load.start()
    for copy in copies:
        copy.start()
    for g in range(heads // group):
        for b in range(group):
            h = g * group + b
            q_loads[h].wait()
            loads[h].wait()
            for w, buf in ((0, k_buf), (1, v_buf)):
                for c in range(part):
                    rows = slice(c * SPAN, (c + 1) * SPAN)
                    at = w * part + c
                    add = shared_ref[g, at : at + 1, b * HEAD_DIM : (b + 1) * HEAD_DIM]
                    buf[rows, h * HEAD_DIM : (h + 1) * HEAD_DIM] = (
                        kv[h, w, rows].astype(F32) + add
                    ).astype(BF16)
        sl = pl.ds(g * cols, cols)
        for w, (buf, ref) in enumerate(((q_buf, q_out), (k_buf, k_out), (v_buf, v_out))):
            copy = pltpu.make_async_copy(
                buf.at[:, sl], ref.at[:, sl], sem.at[2 + 3 * g + w]
            )
            copy.start()
            copies.append(copy)
    for copy in copies:
        copy.wait()


def per_device(queries, keys, values, out_grad):
    count, cols = queries.shape
    nseq = lax.axis_size("seq")
    nhead = lax.axis_size("head")
    heads = cols // HEAD_DIM
    per_dev = count // SPAN
    total = per_dev * nseq
    tile = count // nhead
    part = per_dev // nhead
    steps = heads * nhead
    nplane = nseq // 2
    anyspace = pl.BlockSpec(memory_space=pl.ANY)
    hbm = pl.BlockSpec(memory_space=pltpu.HBM)
    vmem = pl.BlockSpec(memory_space=pltpu.VMEM)
    dma = pltpu.SemaphoreType.DMA
    pieces, grad_k, grad_v, shared = pl.pallas_call(
        functools.partial(main_kernel, nseq, nhead),
        out_shape=(
            jax.ShapeDtypeStruct((nhead * heads, 3, tile, HEAD_DIM), BF16),
            jax.ShapeDtypeStruct((per_dev, cols), F32),
            jax.ShapeDtypeStruct((per_dev, cols), F32),
            jax.ShapeDtypeStruct((nhead, 2 * part, cols), F32),
        ),
        in_specs=[hbm] * 4,
        out_specs=(anyspace, vmem, vmem, vmem),
        scratch_shapes=[pltpu.VMEM((count, cols), BF16)] * 4
        + [
            pltpu.VMEM((heads, nplane, 2, 2, per_dev, HEAD_DIM), BF16),
            pltpu.VMEM((HEAD_DIM, total), BF16),
            pltpu.VMEM((2, total, HEAD_DIM), F32),
            pltpu.VMEM((nplane, heads, 2, 2, per_dev, HEAD_DIM), BF16),
            pltpu.VMEM((nplane, heads, 2, 2, per_dev, HEAD_DIM), BF16),
            pltpu.VMEM((2, heads, 2, per_dev, HEAD_DIM), F32),
            pltpu.VMEM((heads, 2, per_dev, HEAD_DIM), F32),
            pltpu.VMEM((nhead, 2 * part, cols), F32),
            pltpu.VMEM((steps, 3, tile, HEAD_DIM), BF16),
            pltpu.VMEM((total, tile), F32),
            pltpu.VMEM((total, tile), F32),
            pltpu.VMEM((total, tile), F32),
            dma((4, nhead)),
            dma((heads,)),
            dma((heads,)),
            dma((heads, nplane)),
            dma((heads, nplane)),
            dma((heads, nplane)),
            dma((heads, nplane)),
            dma,
            dma,
            dma((steps,)),
            dma((nhead,)),
            dma((heads,)),
            dma((nhead,)),
            dma((nhead,)),
            dma,
        ],
        compiler_params=pltpu.CompilerParams(
            collective_id=0, has_side_effects=True, vmem_limit_bytes=53 * 1024 * 1024
        ),
        name="attend",
    )(queries, keys, values, out_grad)
    row = jax.ShapeDtypeStruct((tile, nhead * cols), BF16)
    block = jax.ShapeDtypeStruct((per_dev, cols), F32)
    query_grad, key_grad, value_grad, grad_k, grad_v = pl.pallas_call(
        functools.partial(finish_kernel, part),
        out_shape=(row, row, row, block, block),
        in_specs=[hbm, vmem, vmem, vmem],
        out_specs=(hbm,) * 5,
        scratch_shapes=[
            pltpu.VMEM((nhead * heads, 2, tile, HEAD_DIM), BF16),
            pltpu.VMEM((tile, nhead * cols), BF16),
            pltpu.VMEM((tile, nhead * cols), BF16),
            pltpu.VMEM((tile, nhead * cols), BF16),
            dma((2, nhead * heads)),
            dma((2 + 3 * nhead,)),
        ],
        compiler_params=pltpu.CompilerParams(vmem_limit_bytes=53 * 1024 * 1024),
        name="finish",
    )(pieces, shared, grad_k, grad_v)
    return (query_grad, key_grad, value_grad, grad_k, grad_v)


def solution(mesh):
    placed = (P("seq", "head"), P("seq", "head"), P("seq", "head"), P("seq", "head"))
    return jax.shard_map(
        per_device,
        mesh=mesh,
        in_specs=placed,
        out_specs=(
            P(("seq", "head"), None),
            P(("seq", "head"), None),
            P(("seq", "head"), None),
            P("seq", "head"),
            P("seq", "head"),
        ),
        check_vma=False,
    )
```

```python
import functools

import jax
import jax.numpy as jnp
from jax import lax
from jax.experimental import pallas as pl
from jax.experimental.pallas import tpu as pltpu
from jax.sharding import PartitionSpec as P

HEAD_DIM = 128
SPAN = 64
PLACES = 4
SLAB = 8
MESH = pl.DeviceIdType.MESH
LOG2E = 1.4426950408889634
F32 = jnp.float32
BF16 = jnp.bfloat16
NT = (((1,), (1,)), ((), ()))
NN = (((1,), (0,)), ((), ()))
TN = (((0,), (0,)), ((), ()))


def dot(a, b, dims):
    return lax.dot_general(a, b, dims, preferred_element_type=F32)


def tile_order(hd, j):
    chip = lax.rem(hd // 2 + 1 + j // 2, 2)
    core = lax.rem(lax.rem(hd, 2) + j + j // 2, 2)
    return chip * 2 + core


def main_kernel(
    nseq,
    nhead,
    q_hbm, k_hbm, v_hbm, d_hbm,
    out, gk_out, gv_out, shared,
    q_ref, k_ref, v_ref, d_ref,
    summ, summ_t, acc, term, rterm, own, other_own, sgs, stage, s_scr, e_scr, dp_scr,
    load_sem, xsend, xrecv, gsend, grecv, rsend, rrecv, psend, precv,
    asend, arecv, local_sem, ssend, srecv, own_sem,
):
    me = lax.axis_index("seq")
    hd = lax.axis_index("head")
    count = q_ref.shape[0]
    heads = q_ref.shape[1] // HEAD_DIM
    per_dev = count // SPAN
    total = per_dev * nseq
    tile = count // nhead
    scale = HEAD_DIM ** (-0.5)
    c2 = scale * LOG2E
    slab = me // SLAB
    side = lax.rem(me, SLAB) // PLACES
    plane = slab * PLACES + lax.rem(me, PLACES)
    nplane = nseq // 2
    partner = me + PLACES - 2 * PLACES * side

    def shard_at(p):
        return (p // PLACES) * SLAB + side * PLACES + lax.rem(p, PLACES)

    loads = [
        [
            pltpu.make_async_copy(
                src.at[c * tile : (c + 1) * tile], dst.at[c * tile : (c + 1) * tile], load_sem.at[i, c]
            )
            for c in range(nhead)
        ]
        for i, (src, dst) in enumerate(
            ((k_hbm, k_ref), (v_hbm, v_ref), (q_hbm, q_ref), (d_hbm, d_ref))
        )
    ]
    for group in loads:
        for load in group:
            load.start()
    summ[...] = jnp.zeros(summ.shape, summ.dtype)

    barrier = pltpu.get_barrier_semaphore()

    def greet(i, _):
        pl.semaphore_signal(
            barrier,
            inc=1,
            device_id={"seq": shard_at(lax.rem(plane + i, nplane))},
            device_id_type=MESH,
        )
        return 0

    lax.fori_loop(1, nplane, greet, 0)
    pl.semaphore_signal(barrier, inc=1, device_id={"seq": partner}, device_id_type=MESH)
    for i in range(1, nhead):
        for shard in (me, partner):
            pl.semaphore_signal(
                barrier,
                inc=1,
                device_id={"seq": shard, "head": lax.rem(hd + i, nhead)},
                device_id_type=MESH,
            )

    pool = (
        lax.broadcasted_iota(jnp.int32, (per_dev, count), 1) // SPAN
        == lax.broadcasted_iota(jnp.int32, (per_dev, count), 0)
    ).astype(BF16)
    for w, ref in ((0, k_ref), (1, v_ref)):
        for load in loads[w]:
            load.wait()
        mean = (dot(pool, ref[...], NN) * (1.0 / SPAN)).astype(BF16)
        for h in range(heads):
            summ[h, plane, side, w] = mean[:, h * HEAD_DIM : (h + 1) * HEAD_DIM]

    pl.semaphore_wait(barrier, nplane - 1 + 1 + 2 * (nhead - 1))

    def swap_copy(h, to):
        return pltpu.make_async_remote_copy(
            src_ref=summ.at[h, plane, to],
            dst_ref=summ.at[h, plane, to],
            send_sem=xsend.at[h],
            recv_sem=xrecv.at[h],
            device_id={"seq": partner},
            device_id_type=MESH,
        )

    def gather_copy(h, src, dst):
        return pltpu.make_async_remote_copy(
            src_ref=summ.at[h, src],
            dst_ref=summ.at[h, src],
            send_sem=gsend.at[h, dst],
            recv_sem=grecv.at[h, src],
            device_id={"seq": shard_at(dst)},
            device_id_type=MESH,
        )

    first = slab * PLACES
    later = nplane - first
    earlier = first + PLACES

    def to_later(k):
        return first + lax.rem(plane - first + k, later)

    def to_earlier(k):
        return lax.rem(plane + k, earlier)

    for h in range(heads):
        swap_copy(h, side).start()
    for h in range(heads):
        swap_copy(h, 1 - side).wait_recv()

        def gather_start(k, _, h=h):
            gather_copy(h, plane, to_later(k)).start()
            return 0

        lax.fori_loop(1, later, gather_start, 0)
    for group in loads[2:]:
        for load in group:
            load.wait()

    rows = 128
    nchunk = total // rows
    group = rows // (2 * per_dev)
    lane = lax.broadcasted_iota(jnp.int32, (SPAN, tile), 1)
    low_lane = lax.rem(lane, 2 * SPAN) < SPAN
    causal = lax.broadcasted_iota(jnp.int32, (SPAN, tile), 0) <= lax.rem(lane, SPAN)
    low128 = low_lane[:, : 2 * SPAN]

    def fold(x, op):
        parts = [x[8 * i : 8 * i + 8] for i in range(x.shape[0] // 8)]
        while len(parts) > 1:
            parts = [
                op(parts[i], parts[i + 1]) if i + 1 < len(parts) else parts[i]
                for i in range(0, len(parts), 2)
            ]
        return parts[0]

    def term_copy(h, dst, src):
        return pltpu.make_async_remote_copy(
            src_ref=term.at[dst, h],
            dst_ref=rterm.at[src, h],
            send_sem=rsend.at[h, dst],
            recv_sem=rrecv.at[h, src],
            device_id={"seq": shard_at(dst)},
            device_id_type=MESH,
        )

    def tile_copy(n, to):
        return pltpu.make_async_remote_copy(
            src_ref=stage.at[n],
            dst_ref=out.at[hd * heads + n // nhead],
            send_sem=asend.at[n],
            recv_sem=arecv.at[hd],
            device_id={"head": to},
            device_id_type=MESH,
        )

    def cross(m):
        return nhead * (m // 2) + lax.rem(m, 2)

    def send_cross(m):
        tile_copy(cross(m), tile_order(hd, lax.rem(m, 2))).start()

    def wait_cross(m):
        tile_copy(cross(m), tile_order(hd, lax.rem(m, 2))).wait_send()

    def step(n, _):
        h = n // nhead
        j = lax.rem(n, nhead)
        i = tile_order(hd, j)
        cols = pl.ds(pl.multiple_of(h * HEAD_DIM, HEAD_DIM), HEAD_DIM)
        trow = pl.ds(pl.multiple_of(i * tile, tile), tile)

        def sk(c):
            return summ[h, c * group : (c + 1) * group, :, 0].reshape(rows, HEAD_DIM)

        def sv(c):
            return summ[h, c * group : (c + 1) * group, :, 1].reshape(rows, HEAD_DIM)

        @pl.when(j == 0)
        def _():
            def gather_wait(k, _):
                gather_copy(h, to_earlier(k), plane).wait_recv()
                return 0

            lax.fori_loop(1, earlier, gather_wait, 0)
            for c in range(nchunk):
                summ_t[:, c * rows : (c + 1) * rows] = sk(c).astype(F32).T.astype(BF16)
            acc[...] = jnp.zeros(acc.shape, F32)

        qt = q_ref[trow, cols]
        kt = k_ref[trow, cols]
        vt = v_ref[trow, cols]
        dt = d_ref[trow, cols]

        def local(a, b):
            picked = []
            for p in range(tile // (2 * SPAN)):
                sl = slice(p * 2 * SPAN, (p + 1) * 2 * SPAN)
                full = dot(a[sl], b[sl], NT)
                picked.append(jnp.where(low128, full[:SPAN], full[SPAN:]))
            return jnp.concatenate(picked, axis=1)

        a_loc = jnp.where(causal, local(kt, qt), -jnp.inf)
        dp_loc = local(vt, dt)
        span_of = (
            me * per_dev
            + i * (tile // SPAN)
            + lax.broadcasted_iota(jnp.int32, (rows, tile), 1) // SPAN
        )
        place_row = lax.broadcasted_iota(jnp.int32, (rows, tile), 0)
        pair = place_row // per_dev
        row_id = (
            (lax.rem(pair, 2) * PLACES + pair // 2) * per_dev + lax.rem(place_row, per_dev)
        )
        top = fold(a_loc, jnp.maximum)
        for c in range(nchunk):
            s = dot(sk(c), qt, NT)
            s = jnp.where(row_id + c * rows < span_of, s, -jnp.inf)
            s_scr[c * rows : (c + 1) * rows] = s
            top = jnp.maximum(top, fold(s, jnp.maximum))
        top = jnp.max(top, axis=0, keepdims=True)
        base = top * c2

        e_loc = jnp.exp2(a_loc * c2 - base)
        mass = fold(e_loc, jnp.add)
        weighted = fold(e_loc * dp_loc, jnp.add)
        for c in range(nchunk):
            sl = slice(c * rows, (c + 1) * rows)
            dp = dot(sv(c), dt, NT)
            e = jnp.exp2(s_scr[sl] * c2 - base)
            e_scr[sl] = e
            dp_scr[sl] = dp
            mass = mass + fold(e, jnp.add)
            weighted = weighted + fold(e * dp, jnp.add)
        inv = 1.0 / jnp.sum(mass, axis=0, keepdims=True)
        delta = jnp.sum(weighted, axis=0, keepdims=True) * inv

        p_loc = e_loc * inv
        g_loc = p_loc * (dp_loc - delta)
        zero = jnp.zeros((SPAN, 2 * SPAN), F32)
        dqt_parts = []
        for p in range(tile // (2 * SPAN)):
            sl = slice(p * 2 * SPAN, (p + 1) * 2 * SPAN)
            g = g_loc[:, sl]
            w = p_loc[:, sl]
            g2 = jnp.concatenate(
                [jnp.where(low128, g, zero), jnp.where(low128, zero, g)], axis=0
            ).astype(BF16)
            w2 = jnp.concatenate(
                [jnp.where(low128, w, zero), jnp.where(low128, zero, w)], axis=0
            ).astype(BF16)
            stage[n, 1, sl] = (dot(g2, qt[sl], NN) * scale).astype(BF16)
            stage[n, 2, sl] = dot(w2, dt[sl], NN).astype(BF16)
            dqt_parts.append(dot(kt[sl], g2, TN))
        dqt = jnp.concatenate(dqt_parts, axis=1)
        for c in range(nchunk):
            sl = slice(c * rows, (c + 1) * rows)
            r = e_scr[sl] * inv
            g = (r * (dp_scr[sl] - delta)).astype(BF16)
            acc[0, sl] += dot(g, qt, NN)
            acc[1, sl] += dot(r.astype(BF16), dt, NN)
            dqt = dqt + dot(summ_t[:, sl], g, NN)
        stage[n, 0] = (dqt * scale).T.astype(BF16)

        @pl.when(n == 0)
        def _():
            send_cross(0)

        @pl.when(j == 1)
        def _():
            @pl.when(h >= 1)
            def _():
                wait_cross(h - 1)

            send_cross(h + 1)

        @pl.when(j == 2)
        def _():
            tile_copy(n, i).start()

        @pl.when(j == nhead - 1)
        def _():
            pltpu.make_async_copy(stage.at[n], out.at[hd * heads + h], local_sem.at[h]).start()
            mine = pl.ds(pl.multiple_of(plane * 2 * per_dev, 2 * per_dev), 2 * per_dev)
            for w in range(2):
                term[:, h, :, w] = acc[w].reshape(nplane, 2, per_dev, HEAD_DIM).astype(BF16)
                own[:, h, w] = acc[w, mine].reshape(2, per_dev, HEAD_DIM)

            def send_term(k, _):
                dst = to_earlier(k)
                term_copy(h, dst, plane).start()
                return 0

            lax.fori_loop(1, earlier, send_term, 0)

        return 0

    lax.fori_loop(0, heads * nhead, step, 0)

    send_cross(heads + 1)
    send_cross(heads + 2)
    for h in range(heads):

        def add_term(k, _, h=h):
            src = to_later(k)
            term_copy(h, plane, src).wait_recv()
            own[:, h] += rterm[src, h].astype(F32)
            return 0

        lax.fori_loop(1, later, add_term, 0)

    part = per_dev // nhead
    half = heads // 2

    def sums_of(which, w):
        factor = scale if w == 0 else 1.0
        return [own[which, h, w] * factor for h in range(heads)]

    def share_of(blocks, dst):
        rows_of = slice(dst * part, (dst + 1) * part)
        pieces = [
            jnp.concatenate([blocks[w][b * half + a][rows_of] for a in range(half)], axis=1)
            for w in range(2)
            for b in range(2)
        ]
        return (jnp.concatenate(pieces, axis=0) * (1.0 / SPAN)).astype(BF16)

    mine = [sums_of(side, w) for w in range(2)]
    theirs = [sums_of(1 - side, w) for w in range(2)]
    for w in range(2):
        for h in range(heads):
            other_own[0, h, w] = theirs[w][h].astype(BF16)
    partial = pltpu.make_async_remote_copy(
        src_ref=other_own.at[0],
        dst_ref=other_own.at[1],
        send_sem=psend,
        recv_sem=precv,
        device_id={"seq": partner},
        device_id_type=MESH,
    )
    partial.start()
    for dst in range(nhead):
        sgs[0, dst] = share_of(mine, dst)
        sgs[1, dst] = share_of(theirs, dst)

    def shared_copy(at, shard, from_side, src, dst):
        return pltpu.make_async_remote_copy(
            src_ref=sgs.at[at, dst],
            dst_ref=shared.at[from_side, src],
            send_sem=ssend.at[at, dst],
            recv_sem=srecv.at[from_side, src],
            device_id={"seq": shard, "head": dst},
            device_id_type=MESH,
        )

    for k in range(1, nhead):
        other = lax.rem(hd + k, nhead)
        shared_copy(1, partner, side, hd, other).start()
        shared_copy(0, me, side, hd, other).start()
    for m in range(heads + 3, 2 * heads):
        send_cross(m)
    keep = pltpu.make_async_copy(sgs.at[0, hd], shared.at[side, hd], own_sem)
    keep.start()
    keep.wait()
    partial.wait()
    arrived = [[other_own[1, h, w].astype(F32) for h in range(heads)] for w in range(2)]
    gk_out[...] = jnp.concatenate([mine[0][h] + arrived[0][h] for h in range(heads)], axis=1)
    gv_out[...] = jnp.concatenate([mine[1][h] + arrived[1][h] for h in range(heads)], axis=1)
    for dst in range(nhead):

        @pl.when(hd == dst)
        def _():
            shared[1 - side, dst] = share_of(arrived, dst)

    for k in range(1, nhead):
        other = lax.rem(hd + k, nhead)
        for at, shard in ((1, partner), (0, me)):
            shared_copy(at, shard, side, hd, other).wait_send()
        for from_side in range(2):
            shared_copy(0, me, from_side, other, other).wait_recv()
        pltpu.make_async_remote_copy(
            src_ref=stage.at[0],
            dst_ref=out.at[pl.ds(other * heads, heads)],
            send_sem=asend.at[0],
            recv_sem=arecv.at[other],
            device_id={"head": other},
            device_id_type=MESH,
        ).wait_recv()

    for m in range(heads - 1, 2 * heads):
        wait_cross(m)
    for h in range(heads):
        tile_copy(h * nhead + 2, tile_order(hd, 2)).wait_send()
    for h in range(heads):
        pltpu.make_async_copy(
            stage.at[h * nhead + nhead - 1], out.at[hd * heads + h], local_sem.at[h]
        ).wait()

    for h in range(heads):
        swap_copy(h, side).wait_send()

        def gather_sent(k, _, h=h):
            gather_copy(h, plane, to_later(k)).wait_send()
            return 0

        def term_sent(k, _, h=h):
            term_copy(h, to_earlier(k), plane).wait_send()
            return 0

        lax.fori_loop(1, later, gather_sent, 0)
        lax.fori_loop(1, earlier, term_sent, 0)


def finish_kernel(
    part, pieces, shared_ref, gk_in, gv_in, q_out, k_out, v_out, gk_out, gv_out, kv, q_buf, k_buf, v_buf, load_sem, sem
):
    heads = pieces.shape[0]
    cols = 2 * shared_ref.shape[3]
    group = cols // HEAD_DIM
    loads = [
        pltpu.make_async_copy(pieces.at[h, 1:], kv.at[h], load_sem.at[0, h]) for h in range(heads)
    ]
    q_loads = [
        pltpu.make_async_copy(
            pieces.at[h, 0], q_buf.at[:, pl.ds(h * HEAD_DIM, HEAD_DIM)], load_sem.at[1, h]
        )
        for h in range(heads)
    ]
    copies = [
        pltpu.make_async_copy(gk_in, gk_out, sem.at[0]),
        pltpu.make_async_copy(gv_in, gv_out, sem.at[1]),
    ]
    for q_load, load in zip(q_loads, loads):
        q_load.start()
        load.start()
    for copy in copies:
        copy.start()
    shares = [
        shared_ref[0, g].astype(F32) + shared_ref[1, g].astype(F32) for g in range(heads // group)
    ]
    for g in range(heads // group):
        for b in range(group):
            h = g * group + b
            q_loads[h].wait()
            loads[h].wait()
            for w, buf in ((0, k_buf), (1, v_buf)):
                for c in range(part):
                    rows = slice(c * SPAN, (c + 1) * SPAN)
                    at = (2 * w + b // 2) * part + c
                    sl = slice((b % 2) * HEAD_DIM, (b % 2 + 1) * HEAD_DIM)
                    add = shares[g][at : at + 1, sl]
                    buf[rows, h * HEAD_DIM : (h + 1) * HEAD_DIM] = (
                        kv[h, w, rows].astype(F32) + add
                    ).astype(BF16)
        sl = pl.ds(g * cols, cols)
        for w, (buf, ref) in enumerate(((q_buf, q_out), (k_buf, k_out), (v_buf, v_out))):
            copy = pltpu.make_async_copy(
                buf.at[:, sl], ref.at[:, sl], sem.at[2 + 3 * g + w]
            )
            copy.start()
            copies.append(copy)
    for copy in copies:
        copy.wait()


def per_device(queries, keys, values, out_grad):
    count, cols = queries.shape
    nseq = lax.axis_size("seq")
    nhead = lax.axis_size("head")
    heads = cols // HEAD_DIM
    per_dev = count // SPAN
    total = per_dev * nseq
    tile = count // nhead
    part = per_dev // nhead
    steps = heads * nhead
    nplane = nseq // 2
    anyspace = pl.BlockSpec(memory_space=pl.ANY)
    hbm = pl.BlockSpec(memory_space=pltpu.HBM)
    vmem = pl.BlockSpec(memory_space=pltpu.VMEM)
    dma = pltpu.SemaphoreType.DMA
    pieces, grad_k, grad_v, shared = pl.pallas_call(
        functools.partial(main_kernel, nseq, nhead),
        out_shape=(
            jax.ShapeDtypeStruct((nhead * heads, 3, tile, HEAD_DIM), BF16),
            jax.ShapeDtypeStruct((per_dev, cols), F32),
            jax.ShapeDtypeStruct((per_dev, cols), F32),
            jax.ShapeDtypeStruct((2, nhead, 4 * part, cols // 2), BF16),
        ),
        in_specs=[hbm] * 4,
        out_specs=(anyspace, vmem, vmem, vmem),
        scratch_shapes=[pltpu.VMEM((count, cols), BF16)] * 4
        + [
            pltpu.VMEM((heads, nplane, 2, 2, per_dev, HEAD_DIM), BF16),
            pltpu.VMEM((HEAD_DIM, total), BF16),
            pltpu.VMEM((2, total, HEAD_DIM), F32),
            pltpu.VMEM((nplane, heads, 2, 2, per_dev, HEAD_DIM), BF16),
            pltpu.VMEM((nplane, heads, 2, 2, per_dev, HEAD_DIM), BF16),
            pltpu.VMEM((2, heads, 2, per_dev, HEAD_DIM), F32),
            pltpu.VMEM((2, heads, 2, per_dev, HEAD_DIM), BF16),
            pltpu.VMEM((2, nhead, 4 * part, cols // 2), BF16),
            pltpu.VMEM((steps, 3, tile, HEAD_DIM), BF16),
            pltpu.VMEM((total, tile), F32),
            pltpu.VMEM((total, tile), F32),
            pltpu.VMEM((total, tile), F32),
            dma((4, nhead)),
            dma((heads,)),
            dma((heads,)),
            dma((heads, nplane)),
            dma((heads, nplane)),
            dma((heads, nplane)),
            dma((heads, nplane)),
            dma,
            dma,
            dma((steps,)),
            dma((nhead,)),
            dma((heads,)),
            dma((2, nhead)),
            dma((2, nhead)),
            dma,
        ],
        compiler_params=pltpu.CompilerParams(
            collective_id=0, has_side_effects=True, vmem_limit_bytes=53 * 1024 * 1024
        ),
        name="attend",
    )(queries, keys, values, out_grad)
    row = jax.ShapeDtypeStruct((tile, nhead * cols), BF16)
    block = jax.ShapeDtypeStruct((per_dev, cols), F32)
    query_grad, key_grad, value_grad, grad_k, grad_v = pl.pallas_call(
        functools.partial(finish_kernel, part),
        out_shape=(row, row, row, block, block),
        in_specs=[hbm, vmem, vmem, vmem],
        out_specs=(hbm,) * 5,
        scratch_shapes=[
            pltpu.VMEM((nhead * heads, 2, tile, HEAD_DIM), BF16),
            pltpu.VMEM((tile, nhead * cols), BF16),
            pltpu.VMEM((tile, nhead * cols), BF16),
            pltpu.VMEM((tile, nhead * cols), BF16),
            dma((2, nhead * heads)),
            dma((2 + 3 * nhead,)),
        ],
        compiler_params=pltpu.CompilerParams(vmem_limit_bytes=53 * 1024 * 1024),
        name="finish",
    )(pieces, shared, grad_k, grad_v)
    return (query_grad, key_grad, value_grad, grad_k, grad_v)


def solution(mesh):
    placed = (P("seq", "head"), P("seq", "head"), P("seq", "head"), P("seq", "head"))
    return jax.shard_map(
        per_device,
        mesh=mesh,
        in_specs=placed,
        out_specs=(
            P(("seq", "head"), None),
            P(("seq", "head"), None),
            P(("seq", "head"), None),
            P("seq", "head"),
            P("seq", "head"),
        ),
        check_vma=False,
    )
```

```python
import functools

import jax
import jax.numpy as jnp
from jax import lax
from jax.experimental import pallas as pl
from jax.experimental.pallas import tpu as pltpu
from jax.sharding import PartitionSpec as P

HEAD_DIM = 128
SPAN = 64
PLACES = 4
SLAB = 8
EARLY = 2
MESH = pl.DeviceIdType.MESH
LOG2E = 1.4426950408889634
F32 = jnp.float32
BF16 = jnp.bfloat16
NT = (((1,), (1,)), ((), ()))
NN = (((1,), (0,)), ((), ()))
TN = (((0,), (0,)), ((), ()))


def dot(a, b, dims):
    return lax.dot_general(a, b, dims, preferred_element_type=F32)


def main_kernel(
    nseq,
    nhead,
    q_hbm, k_hbm, v_hbm, d_hbm,
    out, gk_out, gv_out, shared, tri,
    q_ref, k_ref, v_ref, d_ref,
    sumk, sumv, summ_t, acc, term, rterm, own, other_own, sgs, stage, tri_stage, s_scr, dp_scr,
    load_sem, xsend, xrecv, gsend, grecv, rsend, rrecv, psend, precv,
    asend, arecv, local_sem, ssend, srecv, own_sem, esend, tsend, trecv,
):
    me = lax.axis_index("seq")
    hd = lax.axis_index("head")
    count = q_ref.shape[0]
    heads = q_ref.shape[1] // HEAD_DIM
    per_dev = count // SPAN
    total = per_dev * nseq
    tile = count // nhead
    scale = HEAD_DIM ** (-0.5)
    c2 = scale * LOG2E
    slab = me // SLAB
    side = lax.rem(me, SLAB) // PLACES
    place = lax.rem(me, PLACES)
    plane = slab * PLACES + place
    nplane = nseq // 2
    partner = me + PLACES - 2 * PLACES * side

    def shard_at(p):
        return (p // PLACES) * SLAB + side * PLACES + lax.rem(p, PLACES)

    loads = [
        [
            pltpu.make_async_copy(
                src.at[c * tile : (c + 1) * tile], dst.at[c * tile : (c + 1) * tile], load_sem.at[i, c]
            )
            for c in range(nhead)
        ]
        for i, (src, dst) in enumerate(
            ((k_hbm, k_ref), (v_hbm, v_ref), (q_hbm, q_ref), (d_hbm, d_ref))
        )
    ]
    for group in loads:
        for load in group:
            load.start()
    sumk[...] = jnp.zeros(sumk.shape, sumk.dtype)
    sumv[...] = jnp.zeros(sumv.shape, sumv.dtype)
    rterm[...] = jnp.zeros(rterm.shape, rterm.dtype)

    barrier = pltpu.get_barrier_semaphore()

    def greet(i, _):
        pl.semaphore_signal(
            barrier,
            inc=1,
            device_id={"seq": shard_at(lax.rem(plane + i, nplane))},
            device_id_type=MESH,
        )
        return 0

    lax.fori_loop(1, nplane, greet, 0)
    pl.semaphore_signal(barrier, inc=1, device_id={"seq": partner}, device_id_type=MESH)
    for i in range(1, nhead):
        for shard in (me, partner):
            pl.semaphore_signal(
                barrier,
                inc=1,
                device_id={"seq": shard, "head": lax.rem(hd + i, nhead)},
                device_id_type=MESH,
            )

    pool = (
        lax.broadcasted_iota(jnp.int32, (per_dev, count), 1) // SPAN
        == lax.broadcasted_iota(jnp.int32, (per_dev, count), 0)
    ).astype(BF16)
    for w, ref in ((0, k_ref), (1, v_ref)):
        for load in loads[w]:
            load.wait()
        mean = (dot(pool, ref[...], NN) * (1.0 / SPAN)).astype(BF16)
        for h in range(heads):
            block = mean[:, h * HEAD_DIM : (h + 1) * HEAD_DIM]
            if w == 0:
                sumk[h, slab, place, side] = block
            else:
                sumv[h, place, slab, side] = block

    pl.semaphore_wait(barrier, nplane - 1 + 1 + 2 * (nhead - 1))

    slabs = nplane // PLACES

    def swap_copy(w, to):
        ref = sumk.at[:, slab, place, to] if w == 0 else sumv.at[:, place, slab, to]
        return pltpu.make_async_remote_copy(
            src_ref=ref,
            dst_ref=ref,
            send_sem=xsend.at[w],
            recv_sem=xrecv.at[w],
            device_id={"seq": partner},
            device_id_type=MESH,
        )

    def gather_copy(kind, h, src, dst):
        ref = (
            sumk.at[h, slab, src],
            sumv.at[h, place, src],
            sumk.at[h, src],
            sumv.at[h, src],
        )[kind]
        to_place = kind in (0, 3)
        shard = slab * SLAB + side * PLACES + dst if to_place else dst * SLAB + side * PLACES + place
        return pltpu.make_async_remote_copy(
            src_ref=ref,
            dst_ref=ref,
            send_sem=gsend.at[kind, h, dst],
            recv_sem=grecv.at[kind, h, src],
            device_id={"seq": shard},
            device_id_type=MESH,
        )

    def gather_each(kind, h, what):
        def go(other, _):
            if what == "start":
                gather_copy(kind, h, mine_of, other).start()
            elif what == "sent":
                gather_copy(kind, h, mine_of, other).wait_send()
            else:
                gather_copy(kind, h, other, mine_of).wait_recv()
            return 0

        if kind in (0, 3):
            mine_of = place
            for k in range(1, PLACES):
                go(lax.rem(place + k, PLACES), 0)
        else:
            mine_of = slab
            if what == "arrived":
                lax.fori_loop(0, slab, go, 0)
            else:
                lax.fori_loop(slab + 1, slabs, go, 0)

    first = slab * PLACES
    later = nplane - first
    earlier = first + PLACES

    def to_later(k):
        return first + lax.rem(plane - first + k, later)

    def to_earlier(k):
        return lax.rem(plane + k, earlier)

    for w in range(2):
        swap_copy(w, side).start()
    for group in loads[2:]:
        for load in group:
            load.wait()

    plain = heads - EARLY

    other_chip = (1 - hd // 2) * 2

    def early_copy(e, j, w):
        ref = (q_ref, d_ref)[w]
        to = other_chip + j
        cols = slice((plain + e) * HEAD_DIM, (plain + e + 1) * HEAD_DIM)
        return pltpu.make_async_remote_copy(
            src_ref=ref.at[pl.ds(pl.multiple_of(to * tile, tile), tile), cols],
            dst_ref=out.at[hd * heads + plain + e, 1 + w],
            send_sem=esend.at[e, j, w],
            recv_sem=arecv.at[hd],
            device_id={"head": to},
            device_id_type=MESH,
        )

    early = [early_copy(e, j, w) for e in range(EARLY) for j in range(2) for w in range(2)]
    for copy in early:
        copy.start()
    for w in range(2):
        swap_copy(w, 1 - side).wait_recv()
    for h in range(heads):
        for kind in (0, 1):
            gather_each(kind, h, "start")
    for h in range(heads):
        for kind in (0, 1):
            gather_each(kind, h, "arrived")
            gather_each(kind + 2, h, "start")

    rows = 128
    nchunk = total // rows
    lane = lax.broadcasted_iota(jnp.int32, (SPAN, tile), 1)
    low_lane = lax.rem(lane, 2 * SPAN) < SPAN
    causal = lax.broadcasted_iota(jnp.int32, (SPAN, tile), 0) <= lax.rem(lane, SPAN)
    low128 = low_lane[:, : 2 * SPAN]
    diagonal = (lax.broadcasted_iota(jnp.int32, (SPAN, tile), 0) == lax.rem(lane, SPAN))[:, : 2 * SPAN]
    eye = (
        lax.broadcasted_iota(jnp.int32, (2 * SPAN, 2 * SPAN), 0)
        == lax.broadcasted_iota(jnp.int32, (2 * SPAN, 2 * SPAN), 1)
    ).astype(BF16)

    def fold(x, op):
        parts = [x[8 * i : 8 * i + 8] for i in range(x.shape[0] // 8)]
        while len(parts) > 1:
            parts = [
                op(parts[i], parts[i + 1]) if i + 1 < len(parts) else parts[i]
                for i in range(0, len(parts), 2)
            ]
        return parts[0]

    def term_copy(h, dst, src):
        return pltpu.make_async_remote_copy(
            src_ref=term.at[dst, h],
            dst_ref=rterm.at[src, h],
            send_sem=rsend.at[h, dst],
            recv_sem=rrecv.at[h, src],
            device_id={"seq": shard_at(dst)},
            device_id_type=MESH,
        )

    def tile_copy(h, to):
        return pltpu.make_async_remote_copy(
            src_ref=stage.at[h, to],
            dst_ref=out.at[hd * heads + h],
            send_sem=asend.at[h, to],
            recv_sem=arecv.at[hd],
            device_id={"head": to},
            device_id_type=MESH,
        )

    def cross_copies(m, packed):
        h = m // 2
        to = other_chip + lax.rem(m, 2)
        if not packed:
            return [tile_copy(h, to)]
        e = h - plain
        return [
            pltpu.make_async_remote_copy(
                src_ref=tri_stage.at[e, lax.rem(m, 2)],
                dst_ref=tri.at[lax.rem(hd, 2), e],
                send_sem=tsend.at[m - 2 * plain],
                recv_sem=trecv.at[lax.rem(hd, 2)],
                device_id={"head": to},
                device_id_type=MESH,
            ),
            pltpu.make_async_remote_copy(
                src_ref=stage.at[h, to, 0],
                dst_ref=out.at[hd * heads + h, 0],
                send_sem=asend.at[h, to],
                recv_sem=arecv.at[hd],
                device_id={"head": to},
                device_id_type=MESH,
            ),
        ]

    def send_cross(m):
        for packed in (False, True):

            @pl.when((m >= 2 * plain) == packed)
            def _():
                for copy in cross_copies(m, packed):
                    copy.start()

    def wait_cross(m):
        for packed in (False, True):

            @pl.when((m >= 2 * plain) == packed)
            def _():
                for copy in cross_copies(m, packed):
                    copy.wait_send()

    def add_terms(h):
        def term_wait(k, _):
            term_copy(h, plane, to_later(k)).wait_recv()
            return 0

        lax.fori_loop(1, later, term_wait, 0)
        total_own = own[:, h]
        for src in range(nplane):
            total_own = total_own + rterm[src, h].astype(F32)
        own[:, h] = total_own

    place_row = lax.broadcasted_iota(jnp.int32, (rows, tile), 0)
    pair_of = place_row // per_dev
    row_id = (
        (lax.rem(pair_of, 2) * PLACES + pair_of // 2) * per_dev + lax.rem(place_row, per_dev)
    )
    lane_span = lax.broadcasted_iota(jnp.int32, (rows, tile), 1) // SPAN
    zero = jnp.zeros((SPAN, 2 * SPAN), F32)

    def step(n, _):
        h = n // 2
        own_chip = lax.rem(n, 2)
        chip = lax.rem(hd // 2 + 1 + own_chip, 2)
        cols = pl.ds(pl.multiple_of(h * HEAD_DIM, HEAD_DIM), HEAD_DIM)

        def sk(c):
            return sumk[h, c].reshape(rows, HEAD_DIM)

        def sv(c):
            return sumv[h, :, c].reshape(rows, HEAD_DIM)

        @pl.when(own_chip == 0)
        def _():
            for kind in (2, 3):
                gather_each(kind, h, "arrived")
            for c in range(nchunk):
                summ_t[:, c * rows : (c + 1) * rows] = sk(c).astype(F32).T.astype(BF16)
            acc[...] = jnp.zeros(acc.shape, F32)

        def local(a, b):
            picked = []
            for p in range(tile // (2 * SPAN)):
                sl = slice(p * 2 * SPAN, (p + 1) * 2 * SPAN)
                full = dot(a[sl], b[sl], NT)
                picked.append(jnp.where(low128, full[:SPAN], full[SPAN:]))
            return jnp.concatenate(picked, axis=1)

        tri_at = jnp.where((h >= plain) & (own_chip == 0), h - plain, EARLY)
        q, k, v, d, base, top, inv, delta, p_loc, a_loc, dp_loc, dqt = ([None, None] for _ in range(12))

        def scores(t):
            trow = pl.ds(pl.multiple_of((chip * 2 + t) * tile, tile), tile)
            q[t], k[t], v[t], d[t] = (r[trow, cols] for r in (q_ref, k_ref, v_ref, d_ref))
            a_loc[t] = jnp.where(causal, local(k[t], q[t]), -jnp.inf)
            most = fold(a_loc[t], jnp.maximum)
            span_of = me * per_dev + (chip * 2 + t) * (tile // SPAN) + lane_span
            for c in range(nchunk):
                x = dot(sk(c), q[t], NT)
                x = jnp.where(row_id + c * rows < span_of, x, -jnp.inf)
                s_scr[t, c * rows : (c + 1) * rows] = x
                most = jnp.maximum(most, fold(x, jnp.maximum))
            base[t] = jnp.max(most, axis=0, keepdims=True) * c2

        def weights(t):
            dp_loc[t] = local(v[t], d[t])
            e_loc = jnp.exp2(a_loc[t] * c2 - base[t])
            mass = fold(e_loc, jnp.add)
            weighted = fold(e_loc * dp_loc[t], jnp.add)
            for c in range(nchunk):
                sl = slice(c * rows, (c + 1) * rows)
                dp = dot(sv(c), d[t], NT)
                e = jnp.exp2(s_scr[t, sl] * c2 - base[t])
                s_scr[t, sl] = e
                dp_scr[t, sl] = dp
                mass = mass + fold(e, jnp.add)
                weighted = weighted + fold(e * dp, jnp.add)
            inv[t] = 1.0 / jnp.sum(mass, axis=0, keepdims=True)
            delta[t] = jnp.sum(weighted, axis=0, keepdims=True) * inv[t]
            p_loc[t] = e_loc * inv[t]

        def local_grads(t):
            to = chip * 2 + t
            g_loc = p_loc[t] * (dp_loc[t] - delta[t])
            parts = []
            for p in range(tile // (2 * SPAN)):
                sl = slice(p * 2 * SPAN, (p + 1) * 2 * SPAN)
                g = g_loc[:, sl]
                w = p_loc[t][:, sl]
                g2 = jnp.concatenate(
                    [jnp.where(low128, g, zero), jnp.where(low128, zero, g)], axis=0
                ).astype(BF16)
                w2 = jnp.concatenate(
                    [jnp.where(low128, w, zero), jnp.where(low128, zero, w)], axis=0
                ).astype(BF16)
                stage[h, to, 1, sl] = (dot(g2, q[t][sl], NN) * scale).astype(BF16)
                stage[h, to, 2, sl] = dot(w2, d[t][sl], NN).astype(BF16)
                turned = dot(eye, w2, NT)
                turned = jnp.where(low128, turned[:SPAN], turned[SPAN:])
                tri_stage[tri_at, t, :SPAN, sl] = jnp.where(causal[:, sl], g, turned).astype(BF16)
                main = jnp.sum(jnp.where(diagonal, w, zero), axis=0, keepdims=True)
                tri_stage[tri_at, t, SPAN:, sl] = jnp.broadcast_to(main, (16, 2 * SPAN)).astype(BF16)
                parts.append(dot(k[t][sl], g2, TN))
            dqt[t] = jnp.concatenate(parts, axis=1)

        for t in range(2):
            scores(t)
        for t in range(2):
            weights(t)
        for t in range(2):
            local_grads(t)
        for c in range(nchunk):
            sl = slice(c * rows, (c + 1) * rows)
            for t in range(2):
                r = s_scr[t, sl] * inv[t]
                g = (r * (dp_scr[t, sl] - delta[t])).astype(BF16)
                add_k = dot(g, q[t], NN)
                add_v = dot(r.astype(BF16), d[t], NN)
                sum_k, sum_v = (add_k, add_v) if t == 0 else (sum_k + add_k, sum_v + add_v)
                dqt[t] = dqt[t] + dot(summ_t[:, sl], g, NN)
            acc[0, sl] += sum_k
            acc[1, sl] += sum_v
        for t in range(2):
            stage[h, chip * 2 + t, 0] = (dqt[t] * scale).T.astype(BF16)

        @pl.when(own_chip == 0)
        def _():
            @pl.when(h == 0)
            def _():
                send_cross(0)

            @pl.when(h >= 1)
            def _():
                wait_cross(h - 1)

            send_cross(h + 1)


        @pl.when(own_chip == 1)
        def _():
            tile_copy(h, hd + 1 - 2 * lax.rem(hd, 2)).start()
            pltpu.make_async_copy(stage.at[h, hd], out.at[hd * heads + h], local_sem.at[h]).start()
            mine = pl.ds(pl.multiple_of(plane * 2 * per_dev, 2 * per_dev), 2 * per_dev)
            for w in range(2):
                term[:, h, :, w] = acc[w].reshape(nplane, 2, per_dev, HEAD_DIM).astype(BF16)
                own[:, h, w] = acc[w, mine].reshape(2, per_dev, HEAD_DIM)

            def send_term(k, _):
                dst = to_earlier(k)
                term_copy(h, dst, plane).start()
                return 0

            lax.fori_loop(1, earlier, send_term, 0)

        return 0

    lax.fori_loop(0, heads * 2, step, 0)

    send_cross(heads + 1)
    send_cross(heads + 2)
    for h in range(heads):
        add_terms(h)

    part = per_dev // nhead
    half = heads // 2

    def sums_of(which, w):
        factor = scale if w == 0 else 1.0
        return [own[which, h, w] * factor for h in range(heads)]

    def share_of(blocks, dst):
        rows_of = slice(dst * part, (dst + 1) * part)
        pieces = [
            jnp.concatenate([blocks[w][b * half + a][rows_of] for a in range(half)], axis=1)
            for w in range(2)
            for b in range(2)
        ]
        return (jnp.concatenate(pieces, axis=0) * (1.0 / SPAN)).astype(BF16)

    mine = [sums_of(side, w) for w in range(2)]
    theirs = [sums_of(1 - side, w) for w in range(2)]
    for w in range(2):
        for h in range(heads):
            other_own[0, h, w] = theirs[w][h].astype(BF16)
    partial = pltpu.make_async_remote_copy(
        src_ref=other_own.at[0],
        dst_ref=other_own.at[1],
        send_sem=psend,
        recv_sem=precv,
        device_id={"seq": partner},
        device_id_type=MESH,
    )
    partial.start()
    for dst in range(nhead):
        sgs[0, dst] = share_of(mine, dst)
        sgs[1, dst] = share_of(theirs, dst)

    def shared_copy(at, shard, from_side, src, dst):
        return pltpu.make_async_remote_copy(
            src_ref=sgs.at[at, dst],
            dst_ref=shared.at[from_side, src],
            send_sem=ssend.at[at, dst],
            recv_sem=srecv.at[from_side, src],
            device_id={"seq": shard, "head": dst},
            device_id_type=MESH,
        )

    for k in range(1, nhead):
        other = lax.rem(hd + k, nhead)
        shared_copy(1, partner, side, hd, other).start()
        shared_copy(0, me, side, hd, other).start()
    for m in range(heads + 3, 2 * heads):
        send_cross(m)
    keep = pltpu.make_async_copy(sgs.at[0, hd], shared.at[side, hd], own_sem)
    keep.start()
    keep.wait()
    partial.wait()
    arrived = [[other_own[1, h, w].astype(F32) for h in range(heads)] for w in range(2)]
    gk_out[...] = jnp.concatenate([mine[0][h] + arrived[0][h] for h in range(heads)], axis=1)
    gv_out[...] = jnp.concatenate([mine[1][h] + arrived[1][h] for h in range(heads)], axis=1)
    for dst in range(nhead):

        @pl.when(hd == dst)
        def _():
            shared[1 - side, dst] = share_of(arrived, dst)

    for k in range(1, nhead):
        other = lax.rem(hd + k, nhead)
        for at, shard in ((1, partner), (0, me)):
            shared_copy(at, shard, side, hd, other).wait_send()
        for from_side in range(2):
            shared_copy(0, me, from_side, other, other).wait_recv()
        pltpu.make_async_remote_copy(
            src_ref=out.at[pl.ds(other * heads, heads)],
            dst_ref=out.at[pl.ds(other * heads, heads)],
            send_sem=asend.at[0, 0],
            recv_sem=arecv.at[other],
            device_id={"head": other},
            device_id_type=MESH,
        ).wait_recv()

    for copy in early:
        copy.wait_send()
    for m in range(heads - 1, 2 * heads):
        wait_cross(m)
    for c in range(2):
        pltpu.make_async_remote_copy(
            src_ref=tri.at[c],
            dst_ref=tri.at[c],
            send_sem=tsend.at[0],
            recv_sem=trecv.at[c],
            device_id={"head": other_chip},
            device_id_type=MESH,
        ).wait_recv()
    for h in range(heads):
        tile_copy(h, hd + 1 - 2 * lax.rem(hd, 2)).wait_send()
    for h in range(heads):
        pltpu.make_async_copy(stage.at[h, hd], out.at[hd * heads + h], local_sem.at[h]).wait()

    for w in range(2):
        swap_copy(w, side).wait_send()
    for h in range(heads):
        for kind in range(4):
            gather_each(kind, h, "sent")

        def term_sent(k, _, h=h):
            term_copy(h, to_earlier(k), plane).wait_send()
            return 0

        lax.fori_loop(1, earlier, term_sent, 0)


def finish_kernel(
    part, pieces, shared_ref, tri, gk_in, gv_in, q_out, k_out, v_out, gk_out, gv_out, kv, q_buf, k_buf, v_buf, load_sem, sem
):
    heads = pieces.shape[0]
    cols = 2 * shared_ref.shape[3]
    group = cols // HEAD_DIM
    loads = [
        pltpu.make_async_copy(pieces.at[h, 1:], kv.at[h], load_sem.at[0, h]) for h in range(heads)
    ]
    q_loads = [
        pltpu.make_async_copy(
            pieces.at[h, 0], q_buf.at[:, pl.ds(h * HEAD_DIM, HEAD_DIM)], load_sem.at[1, h]
        )
        for h in range(heads)
    ]
    copies = [
        pltpu.make_async_copy(gk_in, gk_out, sem.at[0]),
        pltpu.make_async_copy(gv_in, gv_out, sem.at[1]),
    ]
    for q_load, load in zip(q_loads, loads):
        q_load.start()
        load.start()
    for copy in copies:
        copy.start()
    chip = lax.axis_index("head") // 2
    lane = lax.broadcasted_iota(jnp.int32, (SPAN, 2 * SPAN), 1)
    low = lane < SPAN
    t_id = lax.rem(lane, SPAN)
    u_id = lax.broadcasted_iota(jnp.int32, (SPAN, 2 * SPAN), 0)
    shares = [
        shared_ref[0, g].astype(F32) + shared_ref[1, g].astype(F32) for g in range(heads // group)
    ]
    for g in range(heads // group):
        for b in range(group):
            h = g * group + b
            q_loads[h].wait()
            loads[h].wait()
            cols_of = slice(h * HEAD_DIM, (h + 1) * HEAD_DIM)

            def share(w, c, b=b, g=g):
                at = (2 * w + b // 2) * part + c
                sl = slice((b % 2) * HEAD_DIM, (b % 2 + 1) * HEAD_DIM)
                return shares[g][at : at + 1, sl]

            def as_sent(h=h, cols_of=cols_of, share=share):
                for w, buf in ((0, k_buf), (1, v_buf)):
                    for c in range(part):
                        rows = slice(c * SPAN, (c + 1) * SPAN)
                        buf[rows, cols_of] = (kv[h, w, rows].astype(F32) + share(w, c)).astype(BF16)

            def multiply(h=h, g=g, e=b - (group - EARLY), cols_of=cols_of, share=share):
                for p in range(part // 2):
                    rows = slice(p * 2 * SPAN, (p + 1) * 2 * SPAN)
                    block = tri[g % 2, e, :SPAN, rows].astype(F32)
                    main = tri[g % 2, e, SPAN : SPAN + 1, rows].astype(F32)
                    upper = jnp.where(u_id <= t_id, block, 0.0)
                    lower = jnp.where(u_id > t_id, block, jnp.where(u_id == t_id, main, 0.0))
                    for w, buf, x, dims, factor in (
                        (0, k_buf, upper, NN, HEAD_DIM ** (-0.5)),
                        (1, v_buf, lower, TN, 1.0),
                    ):
                        wide = jnp.concatenate(
                            [jnp.where(low, x, 0.0), jnp.where(low, 0.0, x)], axis=0
                        ).astype(BF16)
                        grad = dot(wide, kv[h, w, rows], dims) * factor
                        for c in range(2):
                            at = slice((2 * p + c) * SPAN, (2 * p + c + 1) * SPAN)
                            buf[at, cols_of] = (
                                grad[c * SPAN : (c + 1) * SPAN] + share(w, 2 * p + c)
                            ).astype(BF16)

            if b < group - EARLY:
                as_sent()
            else:
                pl.when(chip == g // 2)(as_sent)
                pl.when(chip != g // 2)(multiply)
        sl = pl.ds(g * cols, cols)
        for w, (buf, ref) in enumerate(((q_buf, q_out), (k_buf, k_out), (v_buf, v_out))):
            copy = pltpu.make_async_copy(
                buf.at[:, sl], ref.at[:, sl], sem.at[2 + 3 * g + w]
            )
            copy.start()
            copies.append(copy)
    for copy in copies:
        copy.wait()


def per_device(queries, keys, values, out_grad):
    count, cols = queries.shape
    nseq = lax.axis_size("seq")
    nhead = lax.axis_size("head")
    heads = cols // HEAD_DIM
    per_dev = count // SPAN
    total = per_dev * nseq
    tile = count // nhead
    part = per_dev // nhead
    nplane = nseq // 2
    anyspace = pl.BlockSpec(memory_space=pl.ANY)
    hbm = pl.BlockSpec(memory_space=pltpu.HBM)
    vmem = pl.BlockSpec(memory_space=pltpu.VMEM)
    dma = pltpu.SemaphoreType.DMA
    pieces, grad_k, grad_v, shared, tri = pl.pallas_call(
        functools.partial(main_kernel, nseq, nhead),
        out_shape=(
            jax.ShapeDtypeStruct((nhead * heads, 3, tile, HEAD_DIM), BF16),
            jax.ShapeDtypeStruct((per_dev, cols), F32),
            jax.ShapeDtypeStruct((per_dev, cols), F32),
            jax.ShapeDtypeStruct((2, nhead, 4 * part, cols // 2), BF16),
            jax.ShapeDtypeStruct((2, EARLY, SPAN + 16, tile), BF16),
        ),
        in_specs=[hbm] * 4,
        out_specs=(anyspace, vmem, vmem, vmem, vmem),
        scratch_shapes=[pltpu.VMEM((count, cols), BF16)] * 4
        + [
            pltpu.VMEM((heads, nplane // PLACES, PLACES, 2, per_dev, HEAD_DIM), BF16),
            pltpu.VMEM((heads, PLACES, nplane // PLACES, 2, per_dev, HEAD_DIM), BF16),
            pltpu.VMEM((HEAD_DIM, total), BF16),
            pltpu.VMEM((2, total, HEAD_DIM), F32),
            pltpu.VMEM((nplane, heads, 2, 2, per_dev, HEAD_DIM), BF16),
            pltpu.VMEM((nplane, heads, 2, 2, per_dev, HEAD_DIM), BF16),
            pltpu.VMEM((2, heads, 2, per_dev, HEAD_DIM), F32),
            pltpu.VMEM((2, heads, 2, per_dev, HEAD_DIM), BF16),
            pltpu.VMEM((2, nhead, 4 * part, cols // 2), BF16),
            pltpu.VMEM((heads, nhead, 3, tile, HEAD_DIM), BF16),
            pltpu.VMEM((EARLY + 1, 2, SPAN + 16, tile), BF16),
            pltpu.VMEM((2, total, tile), F32),
            pltpu.VMEM((2, total, tile), F32),
            dma((4, nhead)),
            dma((2,)),
            dma((2,)),
            dma((4, heads, PLACES)),
            dma((4, heads, PLACES)),
            dma((heads, nplane)),
            dma((heads, nplane)),
            dma,
            dma,
            dma((heads, nhead)),
            dma((nhead,)),
            dma((heads,)),
            dma((2, nhead)),
            dma((2, nhead)),
            dma,
            dma((EARLY, 2, 2)),
            dma((2 * EARLY,)),
            dma((2,)),
        ],
        compiler_params=pltpu.CompilerParams(
            collective_id=0, has_side_effects=True, vmem_limit_bytes=53 * 1024 * 1024
        ),
        name="attend",
    )(queries, keys, values, out_grad)
    row = jax.ShapeDtypeStruct((tile, nhead * cols), BF16)
    block = jax.ShapeDtypeStruct((per_dev, cols), F32)
    query_grad, key_grad, value_grad, grad_k, grad_v = pl.pallas_call(
        functools.partial(finish_kernel, part),
        out_shape=(row, row, row, block, block),
        in_specs=[hbm, vmem, vmem, vmem, vmem],
        out_specs=(hbm,) * 5,
        scratch_shapes=[
            pltpu.VMEM((nhead * heads, 2, tile, HEAD_DIM), BF16),
            pltpu.VMEM((tile, nhead * cols), BF16),
            pltpu.VMEM((tile, nhead * cols), BF16),
            pltpu.VMEM((tile, nhead * cols), BF16),
            dma((2, nhead * heads)),
            dma((2 + 3 * nhead,)),
        ],
        compiler_params=pltpu.CompilerParams(vmem_limit_bytes=53 * 1024 * 1024),
        name="finish",
    )(pieces, shared, tri, grad_k, grad_v)
    return (query_grad, key_grad, value_grad, grad_k, grad_v)


def solution(mesh):
    placed = (P("seq", "head"), P("seq", "head"), P("seq", "head"), P("seq", "head"))
    return jax.shard_map(
        per_device,
        mesh=mesh,
        in_specs=placed,
        out_specs=(
            P(("seq", "head"), None),
            P(("seq", "head"), None),
            P(("seq", "head"), None),
            P("seq", "head"),
            P("seq", "head"),
        ),
        check_vma=False,
    )
```

```python
import functools

import jax
import jax.numpy as jnp
from jax import lax
from jax.experimental import pallas as pl
from jax.experimental.pallas import tpu as pltpu
from jax.sharding import PartitionSpec as P

HEAD_DIM = 128
SPAN = 64
PLACES = 4
SLAB = 8
EARLY = 2
MESH = pl.DeviceIdType.MESH
LOG2E = 1.4426950408889634
F32 = jnp.float32
BF16 = jnp.bfloat16
NT = (((1,), (1,)), ((), ()))
NN = (((1,), (0,)), ((), ()))
TN = (((0,), (0,)), ((), ()))


def dot(a, b, dims):
    return lax.dot_general(a, b, dims, preferred_element_type=F32)


def main_kernel(
    nseq,
    nhead,
    q_hbm, k_hbm, v_hbm, d_hbm,
    out, gk_out, gv_out, shared, tri,
    q_ref, k_ref, v_ref, d_ref,
    sumk, sumv, summ_t, acc, term, rterm, own, other_own, sgs, stage, tri_stage, s_scr, dp_scr,
    load_sem, xsend, xrecv, gsend, grecv, rsend, rrecv, psend, precv,
    asend, arecv, local_sem, ssend, srecv, own_sem, esend, tsend, trecv,
):
    me = lax.axis_index("seq")
    hd = lax.axis_index("head")
    count = q_ref.shape[0]
    heads = q_ref.shape[1] // HEAD_DIM
    per_dev = count // SPAN
    total = per_dev * nseq
    tile = count // nhead
    scale = HEAD_DIM ** (-0.5)
    c2 = scale * LOG2E
    slab = me // SLAB
    side = lax.rem(me, SLAB) // PLACES
    place = lax.rem(me, PLACES)
    plane = slab * PLACES + place
    nplane = nseq // 2
    partner = me + PLACES - 2 * PLACES * side

    def shard_at(p):
        return (p // PLACES) * SLAB + side * PLACES + lax.rem(p, PLACES)

    loads = [
        [
            pltpu.make_async_copy(
                src.at[c * tile : (c + 1) * tile], dst.at[c * tile : (c + 1) * tile], load_sem.at[i, c]
            )
            for c in range(nhead)
        ]
        for i, (src, dst) in enumerate(
            ((k_hbm, k_ref), (v_hbm, v_ref), (q_hbm, q_ref), (d_hbm, d_ref))
        )
    ]
    for group in loads:
        for load in group:
            load.start()
    sumk[...] = jnp.zeros(sumk.shape, sumk.dtype)
    sumv[...] = jnp.zeros(sumv.shape, sumv.dtype)
    rterm[...] = jnp.zeros(rterm.shape, rterm.dtype)

    barrier = pltpu.get_barrier_semaphore()

    def greet(i, _):
        pl.semaphore_signal(
            barrier,
            inc=1,
            device_id={"seq": shard_at(lax.rem(plane + i, nplane))},
            device_id_type=MESH,
        )
        return 0

    lax.fori_loop(1, nplane, greet, 0)
    pl.semaphore_signal(barrier, inc=1, device_id={"seq": partner}, device_id_type=MESH)
    for k in range(1, PLACES):
        for p in (
            slab * PLACES + lax.rem(place + k, PLACES),
            lax.rem(slab + k, PLACES) * PLACES + place,
        ):
            pl.semaphore_signal(
                barrier,
                inc=1,
                device_id={"seq": shard_at(p) + partner - me},
                device_id_type=MESH,
            )
    for i in range(1, nhead):
        for shard in (me, partner):
            pl.semaphore_signal(
                barrier,
                inc=1,
                device_id={"seq": shard, "head": lax.rem(hd + i, nhead)},
                device_id_type=MESH,
            )

    pool = (
        lax.broadcasted_iota(jnp.int32, (per_dev, count), 1) // SPAN
        == lax.broadcasted_iota(jnp.int32, (per_dev, count), 0)
    ).astype(BF16)
    for w, ref in ((0, k_ref), (1, v_ref)):
        for load in loads[w]:
            load.wait()
        mean = (dot(pool, ref[...], NN) * (1.0 / SPAN)).astype(BF16)
        for h in range(heads):
            block = mean[:, h * HEAD_DIM : (h + 1) * HEAD_DIM]
            if w == 0:
                sumk[h, slab, place, side] = block
            else:
                sumv[h, place, slab, side] = block

    pl.semaphore_wait(barrier, nplane - 1 + 1 + 2 * (PLACES - 1) + 2 * (nhead - 1))

    slabs = nplane // PLACES

    def swap_copy(w, to):
        ref = sumk.at[1:, slab, place, to] if w == 0 else sumv.at[1:, place, slab, to]
        return pltpu.make_async_remote_copy(
            src_ref=ref,
            dst_ref=ref,
            send_sem=xsend.at[w],
            recv_sem=xrecv.at[w],
            device_id={"seq": partner},
            device_id_type=MESH,
        )

    def gather_copy(kind, h, src, dst):
        ref = (
            sumk.at[h, slab, src],
            sumv.at[h, place, src],
            sumk.at[h, src],
            sumv.at[h, src],
        )[kind]
        to_place = kind in (0, 3)
        shard = slab * SLAB + side * PLACES + dst if to_place else dst * SLAB + side * PLACES + place
        return pltpu.make_async_remote_copy(
            src_ref=ref,
            dst_ref=ref,
            send_sem=gsend.at[kind, h, dst],
            recv_sem=grecv.at[kind, h, src],
            device_id={"seq": shard},
            device_id_type=MESH,
        )

    def gather_each(kind, h, what):
        def go(other, _):
            if what == "start":
                gather_copy(kind, h, mine_of, other).start()
            elif what == "sent":
                gather_copy(kind, h, mine_of, other).wait_send()
            else:
                gather_copy(kind, h, other, mine_of).wait_recv()
            return 0

        if kind in (0, 3):
            mine_of = place
            for k in range(1, PLACES):
                go(lax.rem(place + k, PLACES), 0)
        else:
            mine_of = slab
            if what == "arrived":
                lax.fori_loop(0, slab, go, 0)
            else:
                lax.fori_loop(slab + 1, slabs, go, 0)

    first = slab * PLACES
    later = nplane - first
    earlier = first + PLACES

    def to_later(k):
        return first + lax.rem(plane - first + k, later)

    def to_earlier(k):
        return lax.rem(plane + k, earlier)

    def direct_copy(w, of, dst, across):
        ref = sumk.at[0, slab, place, of] if w == 0 else sumv.at[0, place, slab, of]
        p = slab * PLACES + dst if w == 0 else dst * PLACES + place
        return pltpu.make_async_remote_copy(
            src_ref=ref,
            dst_ref=ref,
            send_sem=gsend.at[w, 0, dst],
            recv_sem=grecv.at[w, 0, place if w == 0 else slab],
            device_id={"seq": shard_at(p) + across * (partner - me)},
            device_id_type=MESH,
        )

    for k in range(PLACES):
        for across in (1, 0):
            if k > 0 or across:
                direct_copy(0, side, lax.rem(place + k, PLACES), across).start()

    def direct_values(dst, _):
        direct_copy(1, side, dst, 1).start()

        @pl.when(dst > slab)
        def _():
            direct_copy(1, side, dst, 0).start()

        return 0

    lax.fori_loop(slab, slabs, direct_values, 0)
    for w in range(2):
        swap_copy(w, side).start()
    for group in loads[2:]:
        for load in group:
            load.wait()

    plain = heads - EARLY

    other_chip = (1 - hd // 2) * 2

    def goes_early(e, j):
        return e < EARLY - 1 or j == 0

    def early_copy(e, j, w):
        ref = (q_ref, d_ref)[w]
        to = other_chip + j
        cols = slice((plain + e) * HEAD_DIM, (plain + e + 1) * HEAD_DIM)
        return pltpu.make_async_remote_copy(
            src_ref=ref.at[pl.ds(pl.multiple_of(to * tile, tile), tile), cols],
            dst_ref=out.at[hd * heads + plain + e, 1 + w],
            send_sem=esend.at[e, j, w],
            recv_sem=arecv.at[hd],
            device_id={"head": to},
            device_id_type=MESH,
        )

    early = [early_copy(e, j, w) for e in range(EARLY) for j in range(2) for w in range(2) if goes_early(e, j)]
    for copy in early:
        copy.start()
    for kind in (0, 1):
        direct_copy(kind, 1 - side, place if kind == 0 else slab, 1).wait_recv()
        gather_each(kind, 0, "arrived")
        gather_each(kind + 2, 0, "start")
    for w in range(2):
        swap_copy(w, 1 - side).wait_recv()
    for h in range(1, heads):
        for kind in (0, 1):
            gather_each(kind, h, "start")
    for h in range(1, heads):
        for kind in (0, 1):
            gather_each(kind, h, "arrived")
            gather_each(kind + 2, h, "start")

    rows = 128
    nchunk = total // rows
    lane = lax.broadcasted_iota(jnp.int32, (SPAN, tile), 1)
    low_lane = lax.rem(lane, 2 * SPAN) < SPAN
    causal = lax.broadcasted_iota(jnp.int32, (SPAN, tile), 0) <= lax.rem(lane, SPAN)
    low128 = low_lane[:, : 2 * SPAN]
    diagonal = (lax.broadcasted_iota(jnp.int32, (SPAN, tile), 0) == lax.rem(lane, SPAN))[:, : 2 * SPAN]
    eye = (
        lax.broadcasted_iota(jnp.int32, (2 * SPAN, 2 * SPAN), 0)
        == lax.broadcasted_iota(jnp.int32, (2 * SPAN, 2 * SPAN), 1)
    ).astype(BF16)

    def fold(x, op):
        parts = [x[8 * i : 8 * i + 8] for i in range(x.shape[0] // 8)]
        while len(parts) > 1:
            parts = [
                op(parts[i], parts[i + 1]) if i + 1 < len(parts) else parts[i]
                for i in range(0, len(parts), 2)
            ]
        return parts[0]

    def term_copy(h, dst, src):
        return pltpu.make_async_remote_copy(
            src_ref=term.at[dst, h],
            dst_ref=rterm.at[src, h],
            send_sem=rsend.at[h, dst],
            recv_sem=rrecv.at[h, src],
            device_id={"seq": shard_at(dst)},
            device_id_type=MESH,
        )

    def tile_copy(h, to):
        return pltpu.make_async_remote_copy(
            src_ref=stage.at[h, to],
            dst_ref=out.at[hd * heads + h],
            send_sem=asend.at[h, to],
            recv_sem=arecv.at[hd],
            device_id={"head": to},
            device_id_type=MESH,
        )

    def cross_copies(m, packed):
        h = m // 2
        to = other_chip + lax.rem(m, 2)
        if not packed:
            return [tile_copy(h, to)]
        e = h - plain
        return [
            pltpu.make_async_remote_copy(
                src_ref=tri_stage.at[e, lax.rem(m, 2)],
                dst_ref=tri.at[lax.rem(hd, 2), e],
                send_sem=tsend.at[m - 2 * plain],
                recv_sem=trecv.at[lax.rem(hd, 2)],
                device_id={"head": to},
                device_id_type=MESH,
            ),
            pltpu.make_async_remote_copy(
                src_ref=stage.at[h, to, 0],
                dst_ref=out.at[hd * heads + h, 0],
                send_sem=asend.at[h, to],
                recv_sem=arecv.at[hd],
                device_id={"head": to},
                device_id_type=MESH,
            ),
        ]

    def send_cross(m):
        for packed in (False, True):

            @pl.when(((m >= 2 * plain) & (m < 2 * heads - 1)) == packed)
            def _():
                for copy in cross_copies(m, packed):
                    copy.start()

    def wait_cross(m):
        for packed in (False, True):

            @pl.when(((m >= 2 * plain) & (m < 2 * heads - 1)) == packed)
            def _():
                for copy in cross_copies(m, packed):
                    copy.wait_send()

    def add_terms(h):
        def term_wait(k, _):
            term_copy(h, plane, to_later(k)).wait_recv()
            return 0

        lax.fori_loop(1, later, term_wait, 0)
        total_own = own[:, h]
        for src in range(nplane):
            total_own = total_own + rterm[src, h].astype(F32)
        own[:, h] = total_own

    place_row = lax.broadcasted_iota(jnp.int32, (rows, tile), 0)
    pair_of = place_row // per_dev
    row_id = (
        (lax.rem(pair_of, 2) * PLACES + pair_of // 2) * per_dev + lax.rem(place_row, per_dev)
    )
    lane_span = lax.broadcasted_iota(jnp.int32, (rows, tile), 1) // SPAN
    zero = jnp.zeros((SPAN, 2 * SPAN), F32)

    def step(n, _):
        h = n // 2
        own_chip = lax.rem(n, 2)
        chip = lax.rem(hd // 2 + 1 + own_chip, 2)
        cols = pl.ds(pl.multiple_of(h * HEAD_DIM, HEAD_DIM), HEAD_DIM)

        def sk(c):
            return sumk[h, c].reshape(rows, HEAD_DIM)

        def sv(c):
            return sumv[h, :, c].reshape(rows, HEAD_DIM)

        @pl.when(own_chip == 0)
        def _():
            for kind in (2, 3):
                gather_each(kind, h, "arrived")
            for c in range(nchunk):
                summ_t[:, c * rows : (c + 1) * rows] = sk(c).astype(F32).T.astype(BF16)
            acc[...] = jnp.zeros(acc.shape, F32)

        def local(a, b):
            picked = []
            for p in range(tile // (2 * SPAN)):
                sl = slice(p * 2 * SPAN, (p + 1) * 2 * SPAN)
                full = dot(a[sl], b[sl], NT)
                picked.append(jnp.where(low128, full[:SPAN], full[SPAN:]))
            return jnp.concatenate(picked, axis=1)

        tri_at = jnp.where((h >= plain) & (own_chip == 0), h - plain, EARLY)
        q, k, v, d, base, top, inv, delta, p_loc, a_loc, dp_loc, dqt = ([None, None] for _ in range(12))

        def scores(t):
            trow = pl.ds(pl.multiple_of((chip * 2 + t) * tile, tile), tile)
            q[t], k[t], v[t], d[t] = (r[trow, cols] for r in (q_ref, k_ref, v_ref, d_ref))
            a_loc[t] = jnp.where(causal, local(k[t], q[t]), -jnp.inf)
            most = fold(a_loc[t], jnp.maximum)
            span_of = me * per_dev + (chip * 2 + t) * (tile // SPAN) + lane_span
            for c in range(nchunk):
                x = dot(sk(c), q[t], NT)
                x = jnp.where(row_id + c * rows < span_of, x, -jnp.inf)
                s_scr[t, c * rows : (c + 1) * rows] = x
                most = jnp.maximum(most, fold(x, jnp.maximum))
            base[t] = jnp.max(most, axis=0, keepdims=True) * c2

        def weights(t):
            dp_loc[t] = local(v[t], d[t])
            e_loc = jnp.exp2(a_loc[t] * c2 - base[t])
            mass = fold(e_loc, jnp.add)
            weighted = fold(e_loc * dp_loc[t], jnp.add)
            for c in range(nchunk):
                sl = slice(c * rows, (c + 1) * rows)
                dp = dot(sv(c), d[t], NT)
                e = jnp.exp2(s_scr[t, sl] * c2 - base[t])
                s_scr[t, sl] = e
                dp_scr[t, sl] = dp
                mass = mass + fold(e, jnp.add)
                weighted = weighted + fold(e * dp, jnp.add)
            inv[t] = 1.0 / jnp.sum(mass, axis=0, keepdims=True)
            delta[t] = jnp.sum(weighted, axis=0, keepdims=True) * inv[t]
            p_loc[t] = e_loc * inv[t]

        def local_grads(t):
            to = chip * 2 + t
            g_loc = p_loc[t] * (dp_loc[t] - delta[t])
            parts = []
            for p in range(tile // (2 * SPAN)):
                sl = slice(p * 2 * SPAN, (p + 1) * 2 * SPAN)
                g = g_loc[:, sl]
                w = p_loc[t][:, sl]
                g2 = jnp.concatenate(
                    [jnp.where(low128, g, zero), jnp.where(low128, zero, g)], axis=0
                ).astype(BF16)
                w2 = jnp.concatenate(
                    [jnp.where(low128, w, zero), jnp.where(low128, zero, w)], axis=0
                ).astype(BF16)
                stage[h, to, 1, sl] = (dot(g2, q[t][sl], NN) * scale).astype(BF16)
                stage[h, to, 2, sl] = dot(w2, d[t][sl], NN).astype(BF16)
                turned = dot(eye, w2, NT)
                turned = jnp.where(low128, turned[:SPAN], turned[SPAN:])
                tri_stage[tri_at, t, :SPAN, sl] = jnp.where(causal[:, sl], g, turned).astype(BF16)
                main = jnp.sum(jnp.where(diagonal, w, zero), axis=0, keepdims=True)
                tri_stage[tri_at, t, SPAN:, sl] = jnp.broadcast_to(main, (16, 2 * SPAN)).astype(BF16)
                parts.append(dot(k[t][sl], g2, TN))
            dqt[t] = jnp.concatenate(parts, axis=1)

        for t in range(2):
            scores(t)
        for t in range(2):
            weights(t)
        for t in range(2):
            local_grads(t)
        for c in range(nchunk):
            sl = slice(c * rows, (c + 1) * rows)
            for t in range(2):
                r = s_scr[t, sl] * inv[t]
                g = (r * (dp_scr[t, sl] - delta[t])).astype(BF16)
                add_k = dot(g, q[t], NN)
                add_v = dot(r.astype(BF16), d[t], NN)
                sum_k, sum_v = (add_k, add_v) if t == 0 else (sum_k + add_k, sum_v + add_v)
                dqt[t] = dqt[t] + dot(summ_t[:, sl], g, NN)
            acc[0, sl] += sum_k
            acc[1, sl] += sum_v
        for t in range(2):
            stage[h, chip * 2 + t, 0] = (dqt[t] * scale).T.astype(BF16)

        @pl.when(own_chip == 0)
        def _():
            @pl.when(h == 0)
            def _():
                send_cross(0)

            @pl.when(h >= 1)
            def _():
                wait_cross(h - 1)

            send_cross(h + 1)


        @pl.when(own_chip == 1)
        def _():
            tile_copy(h, hd + 1 - 2 * lax.rem(hd, 2)).start()
            pltpu.make_async_copy(stage.at[h, hd], out.at[hd * heads + h], local_sem.at[h]).start()
            mine = pl.ds(pl.multiple_of(plane * 2 * per_dev, 2 * per_dev), 2 * per_dev)
            for w in range(2):
                term[:, h, :, w] = acc[w].reshape(nplane, 2, per_dev, HEAD_DIM).astype(BF16)
                own[:, h, w] = acc[w, mine].reshape(2, per_dev, HEAD_DIM)

            def send_term(k, _):
                dst = to_earlier(k)
                term_copy(h, dst, plane).start()
                return 0

            lax.fori_loop(1, earlier, send_term, 0)

        return 0

    lax.fori_loop(0, heads * 2, step, 0)

    send_cross(heads + 1)
    send_cross(heads + 2)
    for h in range(heads):
        add_terms(h)

    part = per_dev // nhead
    half = heads // 2

    def sums_of(which, w):
        factor = scale if w == 0 else 1.0
        return [own[which, h, w] * factor for h in range(heads)]

    def share_of(blocks, dst):
        rows_of = slice(dst * part, (dst + 1) * part)
        pieces = [
            jnp.concatenate([blocks[w][b * half + a][rows_of] for a in range(half)], axis=1)
            for w in range(2)
            for b in range(2)
        ]
        return (jnp.concatenate(pieces, axis=0) * (1.0 / SPAN)).astype(BF16)

    mine = [sums_of(side, w) for w in range(2)]
    theirs = [sums_of(1 - side, w) for w in range(2)]
    for w in range(2):
        for h in range(heads):
            other_own[0, h, w] = theirs[w][h].astype(BF16)
    partial = pltpu.make_async_remote_copy(
        src_ref=other_own.at[0],
        dst_ref=other_own.at[1],
        send_sem=psend,
        recv_sem=precv,
        device_id={"seq": partner},
        device_id_type=MESH,
    )
    partial.start()
    for dst in range(nhead):
        sgs[0, dst] = share_of(mine, dst)
        sgs[1, dst] = share_of(theirs, dst)

    def shared_copy(at, shard, from_side, src, dst):
        return pltpu.make_async_remote_copy(
            src_ref=sgs.at[at, dst],
            dst_ref=shared.at[from_side, src],
            send_sem=ssend.at[at, dst],
            recv_sem=srecv.at[from_side, src],
            device_id={"seq": shard, "head": dst},
            device_id_type=MESH,
        )

    for k in range(1, nhead):
        other = lax.rem(hd + k, nhead)
        shared_copy(1, partner, side, hd, other).start()
        shared_copy(0, me, side, hd, other).start()
    for m in range(heads + 3, 2 * heads):
        send_cross(m)
    keep = pltpu.make_async_copy(sgs.at[0, hd], shared.at[side, hd], own_sem)
    keep.start()
    keep.wait()
    partial.wait()
    arrived = [[other_own[1, h, w].astype(F32) for h in range(heads)] for w in range(2)]
    gk_out[...] = jnp.concatenate([mine[0][h] + arrived[0][h] for h in range(heads)], axis=1)
    gv_out[...] = jnp.concatenate([mine[1][h] + arrived[1][h] for h in range(heads)], axis=1)
    for dst in range(nhead):

        @pl.when(hd == dst)
        def _():
            shared[1 - side, dst] = share_of(arrived, dst)

    for k in range(1, nhead):
        other = lax.rem(hd + k, nhead)
        for at, shard in ((1, partner), (0, me)):
            shared_copy(at, shard, side, hd, other).wait_send()
        for from_side in range(2):
            shared_copy(0, me, from_side, other, other).wait_recv()
        pltpu.make_async_remote_copy(
            src_ref=out.at[pl.ds(other * heads, heads)],
            dst_ref=out.at[pl.ds(other * heads, heads)],
            send_sem=asend.at[0, 0],
            recv_sem=arecv.at[other],
            device_id={"head": other},
            device_id_type=MESH,
        ).wait_recv()

    for copy in early:
        copy.wait_send()
    for m in range(heads - 1, 2 * heads):
        wait_cross(m)
    for c in range(2):
        for core, blocks in ((0, EARLY), (1, EARLY - 1)):

            @pl.when(lax.rem(hd, 2) == core)
            def _():
                pltpu.make_async_remote_copy(
                    src_ref=tri.at[c, :blocks],
                    dst_ref=tri.at[c, :blocks],
                    send_sem=tsend.at[0],
                    recv_sem=trecv.at[c],
                    device_id={"head": other_chip},
                    device_id_type=MESH,
                ).wait_recv()

    for h in range(heads):
        tile_copy(h, hd + 1 - 2 * lax.rem(hd, 2)).wait_send()
    for h in range(heads):
        pltpu.make_async_copy(stage.at[h, hd], out.at[hd * heads + h], local_sem.at[h]).wait()

    for w in range(2):
        swap_copy(w, side).wait_send()
        direct_copy(w, side, place if w == 0 else slab, 1).wait_send()
    for h in range(heads):
        for kind in range(4):
            gather_each(kind, h, "sent")

        def term_sent(k, _, h=h):
            term_copy(h, to_earlier(k), plane).wait_send()
            return 0

        lax.fori_loop(1, earlier, term_sent, 0)


def finish_kernel(
    part, pieces, shared_ref, tri, gk_in, gv_in, q_out, k_out, v_out, gk_out, gv_out, kv, q_buf, k_buf, v_buf, load_sem, sem
):
    heads = pieces.shape[0]
    cols = 2 * shared_ref.shape[3]
    group = cols // HEAD_DIM
    loads = [
        pltpu.make_async_copy(
            pieces.at[g * group : (g + 1) * group], kv.at[g * group : (g + 1) * group], load_sem.at[g]
        )
        for g in range(heads // group)
    ]
    copies = [
        pltpu.make_async_copy(gk_in, gk_out, sem.at[0]),
        pltpu.make_async_copy(gv_in, gv_out, sem.at[1]),
    ]
    for load in loads:
        load.start()
    for copy in copies:
        copy.start()
    chip = lax.axis_index("head") // 2
    core = lax.rem(lax.axis_index("head"), 2)
    lane = lax.broadcasted_iota(jnp.int32, (SPAN, 2 * SPAN), 1)
    low = lane < SPAN
    t_id = lax.rem(lane, SPAN)
    u_id = lax.broadcasted_iota(jnp.int32, (SPAN, 2 * SPAN), 0)
    shares = [
        shared_ref[0, g].astype(F32) + shared_ref[1, g].astype(F32) for g in range(heads // group)
    ]
    for g in range(heads // group):
        loads[g].wait()
        for b in range(group):
            h = g * group + b
            cols_of = slice(h * HEAD_DIM, (h + 1) * HEAD_DIM)
            q_buf[:, cols_of] = kv[h, 0]

            def share(w, c, b=b, g=g):
                at = (2 * w + b // 2) * part + c
                sl = slice((b % 2) * HEAD_DIM, (b % 2 + 1) * HEAD_DIM)
                return shares[g][at : at + 1, sl]

            def as_sent(h=h, cols_of=cols_of, share=share):
                for w, buf in ((0, k_buf), (1, v_buf)):
                    for c in range(part):
                        rows = slice(c * SPAN, (c + 1) * SPAN)
                        buf[rows, cols_of] = (kv[h, 1 + w, rows].astype(F32) + share(w, c)).astype(BF16)

            def multiply(h=h, g=g, e=b - (group - EARLY), cols_of=cols_of, share=share):
                for p in range(part // 2):
                    rows = slice(p * 2 * SPAN, (p + 1) * 2 * SPAN)
                    block = tri[g % 2, e, :SPAN, rows].astype(F32)
                    main = tri[g % 2, e, SPAN : SPAN + 1, rows].astype(F32)
                    upper = jnp.where(u_id <= t_id, block, 0.0)
                    lower = jnp.where(u_id > t_id, block, jnp.where(u_id == t_id, main, 0.0))
                    for w, buf, x, dims, factor in (
                        (0, k_buf, upper, NN, HEAD_DIM ** (-0.5)),
                        (1, v_buf, lower, TN, 1.0),
                    ):
                        wide = jnp.concatenate(
                            [jnp.where(low, x, 0.0), jnp.where(low, 0.0, x)], axis=0
                        ).astype(BF16)
                        grad = dot(wide, kv[h, 1 + w, rows], dims) * factor
                        for c in range(2):
                            at = slice((2 * p + c) * SPAN, (2 * p + c + 1) * SPAN)
                            buf[at, cols_of] = (
                                grad[c * SPAN : (c + 1) * SPAN] + share(w, 2 * p + c)
                            ).astype(BF16)

            if b < group - EARLY:
                as_sent()
            else:
                packed = chip != g // 2
                if b == group - 1:
                    packed = packed & (core == 0)
                pl.when(jnp.logical_not(packed))(as_sent)
                pl.when(packed)(multiply)
        sl = pl.ds(g * cols, cols)
        for w, (buf, ref) in enumerate(((q_buf, q_out), (k_buf, k_out), (v_buf, v_out))):
            copy = pltpu.make_async_copy(
                buf.at[:, sl], ref.at[:, sl], sem.at[2 + 3 * g + w]
            )
            copy.start()
            copies.append(copy)
    for copy in copies:
        copy.wait()


def per_device(queries, keys, values, out_grad):
    count, cols = queries.shape
    nseq = lax.axis_size("seq")
    nhead = lax.axis_size("head")
    heads = cols // HEAD_DIM
    per_dev = count // SPAN
    total = per_dev * nseq
    tile = count // nhead
    part = per_dev // nhead
    nplane = nseq // 2
    anyspace = pl.BlockSpec(memory_space=pl.ANY)
    hbm = pl.BlockSpec(memory_space=pltpu.HBM)
    vmem = pl.BlockSpec(memory_space=pltpu.VMEM)
    dma = pltpu.SemaphoreType.DMA
    pieces, grad_k, grad_v, shared, tri = pl.pallas_call(
        functools.partial(main_kernel, nseq, nhead),
        out_shape=(
            jax.ShapeDtypeStruct((nhead * heads, 3, tile, HEAD_DIM), BF16),
            jax.ShapeDtypeStruct((per_dev, cols), F32),
            jax.ShapeDtypeStruct((per_dev, cols), F32),
            jax.ShapeDtypeStruct((2, nhead, 4 * part, cols // 2), BF16),
            jax.ShapeDtypeStruct((2, EARLY, SPAN + 16, tile), BF16),
        ),
        in_specs=[hbm] * 4,
        out_specs=(anyspace, vmem, vmem, vmem, vmem),
        scratch_shapes=[pltpu.VMEM((count, cols), BF16)] * 4
        + [
            pltpu.VMEM((heads, nplane // PLACES, PLACES, 2, per_dev, HEAD_DIM), BF16),
            pltpu.VMEM((heads, PLACES, nplane // PLACES, 2, per_dev, HEAD_DIM), BF16),
            pltpu.VMEM((HEAD_DIM, total), BF16),
            pltpu.VMEM((2, total, HEAD_DIM), F32),
            pltpu.VMEM((nplane, heads, 2, 2, per_dev, HEAD_DIM), BF16),
            pltpu.VMEM((nplane, heads, 2, 2, per_dev, HEAD_DIM), BF16),
            pltpu.VMEM((2, heads, 2, per_dev, HEAD_DIM), F32),
            pltpu.VMEM((2, heads, 2, per_dev, HEAD_DIM), BF16),
            pltpu.VMEM((2, nhead, 4 * part, cols // 2), BF16),
            pltpu.VMEM((heads, nhead, 3, tile, HEAD_DIM), BF16),
            pltpu.VMEM((EARLY + 1, 2, SPAN + 16, tile), BF16),
            pltpu.VMEM((2, total, tile), F32),
            pltpu.VMEM((2, total, tile), F32),
            dma((4, nhead)),
            dma((2,)),
            dma((2,)),
            dma((4, heads, PLACES)),
            dma((4, heads, PLACES)),
            dma((heads, nplane)),
            dma((heads, nplane)),
            dma,
            dma,
            dma((heads, nhead)),
            dma((nhead,)),
            dma((heads,)),
            dma((2, nhead)),
            dma((2, nhead)),
            dma,
            dma((EARLY, 2, 2)),
            dma((2 * EARLY,)),
            dma((2,)),
        ],
        compiler_params=pltpu.CompilerParams(
            collective_id=0, has_side_effects=True, vmem_limit_bytes=53 * 1024 * 1024
        ),
        name="attend",
    )(queries, keys, values, out_grad)
    row = jax.ShapeDtypeStruct((tile, nhead * cols), BF16)
    block = jax.ShapeDtypeStruct((per_dev, cols), F32)
    query_grad, key_grad, value_grad, grad_k, grad_v = pl.pallas_call(
        functools.partial(finish_kernel, part),
        out_shape=(row, row, row, block, block),
        in_specs=[hbm, vmem, vmem, vmem, vmem],
        out_specs=(hbm,) * 5,
        scratch_shapes=[
            pltpu.VMEM((nhead * heads, 3, tile, HEAD_DIM), BF16),
            pltpu.VMEM((tile, nhead * cols), BF16),
            pltpu.VMEM((tile, nhead * cols), BF16),
            pltpu.VMEM((tile, nhead * cols), BF16),
            dma((nhead,)),
            dma((2 + 3 * nhead,)),
        ],
        compiler_params=pltpu.CompilerParams(vmem_limit_bytes=53 * 1024 * 1024),
        name="finish",
    )(pieces, shared, tri, grad_k, grad_v)
    return (query_grad, key_grad, value_grad, grad_k, grad_v)


def solution(mesh):
    placed = (P("seq", "head"), P("seq", "head"), P("seq", "head"), P("seq", "head"))
    return jax.shard_map(
        per_device,
        mesh=mesh,
        in_specs=placed,
        out_specs=(
            P(("seq", "head"), None),
            P(("seq", "head"), None),
            P(("seq", "head"), None),
            P("seq", "head"),
            P("seq", "head"),
        ),
        check_vma=False,
    )
```

```python
import functools

import jax
import jax.numpy as jnp
from jax import lax
from jax.experimental import pallas as pl
from jax.experimental.pallas import tpu as pltpu
from jax.sharding import PartitionSpec as P

HEAD_DIM = 128
SPAN = 64
PLACES = 4
SLAB = 8
EARLY = 2
MESH = pl.DeviceIdType.MESH
LOG2E = 1.4426950408889634
F32 = jnp.float32
BF16 = jnp.bfloat16
NT = (((1,), (1,)), ((), ()))
NN = (((1,), (0,)), ((), ()))
TN = (((0,), (0,)), ((), ()))


def dot(a, b, dims):
    return lax.dot_general(a, b, dims, preferred_element_type=F32)


def main_kernel(
    nseq,
    nhead,
    q_hbm, k_hbm, v_hbm, d_hbm,
    out, gk_out, gv_out, shared, tri,
    q_ref, k_ref, v_ref, d_ref,
    sumk, sumv, summ_t, acc, term, rterm, own, other_own, sgs, stage, tri_stage, s_scr, dp_scr,
    load_sem, xsend, xrecv, gsend, grecv, rsend, rrecv, psend, precv,
    asend, arecv, local_sem, ssend, srecv, own_sem, esend, tsend, trecv,
):
    me = lax.axis_index("seq")
    hd = lax.axis_index("head")
    count = q_ref.shape[0]
    heads = q_ref.shape[1] // HEAD_DIM
    per_dev = count // SPAN
    total = per_dev * nseq
    tile = count // nhead
    scale = HEAD_DIM ** (-0.5)
    c2 = scale * LOG2E
    slab = me // SLAB
    side = lax.rem(me, SLAB) // PLACES
    place = lax.rem(me, PLACES)
    plane = slab * PLACES + place
    nplane = nseq // 2
    partner = me + PLACES - 2 * PLACES * side

    def shard_at(p):
        return (p // PLACES) * SLAB + side * PLACES + lax.rem(p, PLACES)

    loads = [
        [
            pltpu.make_async_copy(
                src.at[c * tile : (c + 1) * tile], dst.at[c * tile : (c + 1) * tile], load_sem.at[i, c]
            )
            for c in range(nhead)
        ]
        for i, (src, dst) in enumerate(
            ((k_hbm, k_ref), (v_hbm, v_ref), (q_hbm, q_ref), (d_hbm, d_ref))
        )
    ]
    for group in loads:
        for load in group:
            load.start()
    sumk[...] = jnp.zeros(sumk.shape, sumk.dtype)
    sumv[...] = jnp.zeros(sumv.shape, sumv.dtype)
    rterm[...] = jnp.zeros(rterm.shape, rterm.dtype)

    barrier = pltpu.get_barrier_semaphore()

    def greet(i, _):
        pl.semaphore_signal(
            barrier,
            inc=1,
            device_id={"seq": shard_at(lax.rem(plane + i, nplane))},
            device_id_type=MESH,
        )
        return 0

    lax.fori_loop(1, nplane, greet, 0)
    pl.semaphore_signal(barrier, inc=1, device_id={"seq": partner}, device_id_type=MESH)
    for k in range(1, PLACES):
        for p in (
            slab * PLACES + lax.rem(place + k, PLACES),
            lax.rem(slab + k, PLACES) * PLACES + place,
        ):
            pl.semaphore_signal(
                barrier,
                inc=1,
                device_id={"seq": shard_at(p) + partner - me},
                device_id_type=MESH,
            )
    for i in range(1, nhead):
        for shard in (me, partner):
            pl.semaphore_signal(
                barrier,
                inc=1,
                device_id={"seq": shard, "head": lax.rem(hd + i, nhead)},
                device_id_type=MESH,
            )

    pool = (
        lax.broadcasted_iota(jnp.int32, (per_dev, count), 1) // SPAN
        == lax.broadcasted_iota(jnp.int32, (per_dev, count), 0)
    ).astype(BF16)
    for w, ref in ((0, k_ref), (1, v_ref)):
        for load in loads[w]:
            load.wait()
        mean = (dot(pool, ref[...], NN) * (1.0 / SPAN)).astype(BF16)
        for h in range(heads):
            block = mean[:, h * HEAD_DIM : (h + 1) * HEAD_DIM]
            if w == 0:
                sumk[h, slab, place, side] = block
            else:
                sumv[h, place, slab, side] = block

    pl.semaphore_wait(barrier, nplane - 1 + 1 + 2 * (PLACES - 1) + 2 * (nhead - 1))

    slabs = nplane // PLACES

    def swap_copy(w, to):
        ref = sumk.at[1:, slab, place, to] if w == 0 else sumv.at[1:, place, slab, to]
        return pltpu.make_async_remote_copy(
            src_ref=ref,
            dst_ref=ref,
            send_sem=xsend.at[w],
            recv_sem=xrecv.at[w],
            device_id={"seq": partner},
            device_id_type=MESH,
        )

    def gather_copy(kind, h, src, dst):
        ref = (
            sumk.at[h, slab, src],
            sumv.at[h, place, src],
            sumk.at[h, src],
            sumv.at[h, src],
        )[kind]
        to_place = kind in (0, 3)
        shard = slab * SLAB + side * PLACES + dst if to_place else dst * SLAB + side * PLACES + place
        return pltpu.make_async_remote_copy(
            src_ref=ref,
            dst_ref=ref,
            send_sem=gsend.at[kind, h, dst],
            recv_sem=grecv.at[kind, h, src],
            device_id={"seq": shard},
            device_id_type=MESH,
        )

    def gather_each(kind, h, what):
        def go(other, _):
            if what == "start":
                gather_copy(kind, h, mine_of, other).start()
            elif what == "sent":
                gather_copy(kind, h, mine_of, other).wait_send()
            else:
                gather_copy(kind, h, other, mine_of).wait_recv()
            return 0

        if kind in (0, 3):
            mine_of = place
            for k in range(1, PLACES):
                go(lax.rem(place + k, PLACES), 0)
        else:
            mine_of = slab
            if what == "arrived":
                lax.fori_loop(0, slab, go, 0)
            else:
                lax.fori_loop(slab + 1, slabs, go, 0)

    first = slab * PLACES
    later = nplane - first
    earlier = first + PLACES

    def to_later(k):
        return first + lax.rem(plane - first + k, later)

    def to_earlier(k):
        return lax.rem(plane + k, earlier)

    def direct_copy(w, of, dst, across):
        ref = sumk.at[0, slab, place, of] if w == 0 else sumv.at[0, place, slab, of]
        p = slab * PLACES + dst if w == 0 else dst * PLACES + place
        return pltpu.make_async_remote_copy(
            src_ref=ref,
            dst_ref=ref,
            send_sem=gsend.at[w, 0, dst],
            recv_sem=grecv.at[w, 0, place if w == 0 else slab],
            device_id={"seq": shard_at(p) + across * (partner - me)},
            device_id_type=MESH,
        )

    for k in range(PLACES):
        for across in (1, 0):
            if k > 0 or across:
                direct_copy(0, side, lax.rem(place + k, PLACES), across).start()

    def direct_values(dst, _):
        direct_copy(1, side, dst, 1).start()

        @pl.when(dst > slab)
        def _():
            direct_copy(1, side, dst, 0).start()

        return 0

    lax.fori_loop(slab, slabs, direct_values, 0)
    for w in range(2):
        swap_copy(w, side).start()
    for group in loads[2:]:
        for load in group:
            load.wait()

    plain = heads - EARLY

    other_chip = (1 - hd // 2) * 2

    def goes_early(e, j):
        return e < EARLY - 1 or j == 0

    def early_copy(e, j, w):
        ref = (q_ref, d_ref)[w]
        to = other_chip + j
        cols = slice((plain + e) * HEAD_DIM, (plain + e + 1) * HEAD_DIM)
        return pltpu.make_async_remote_copy(
            src_ref=ref.at[pl.ds(pl.multiple_of(to * tile, tile), tile), cols],
            dst_ref=out.at[hd * heads + plain + e, 1 + w],
            send_sem=esend.at[e, j, w],
            recv_sem=arecv.at[hd],
            device_id={"head": to},
            device_id_type=MESH,
        )

    early = [early_copy(e, j, w) for e in range(EARLY) for j in range(2) for w in range(2) if goes_early(e, j)]
    for copy in early:
        copy.start()
    for kind in (0, 1):
        direct_copy(kind, 1 - side, place if kind == 0 else slab, 1).wait_recv()
        gather_each(kind, 0, "arrived")
        gather_each(kind + 2, 0, "start")
    for w in range(2):
        swap_copy(w, 1 - side).wait_recv()
    for h in range(1, heads):
        for kind in (0, 1):
            gather_each(kind, h, "start")
    for h in range(1, heads):
        for kind in (0, 1):
            gather_each(kind, h, "arrived")
            gather_each(kind + 2, h, "start")

    rows = 128
    nchunk = total // rows
    lane = lax.broadcasted_iota(jnp.int32, (SPAN, tile), 1)
    low_lane = lax.rem(lane, 2 * SPAN) < SPAN
    causal = lax.broadcasted_iota(jnp.int32, (SPAN, tile), 0) <= lax.rem(lane, SPAN)
    low128 = low_lane[:, : 2 * SPAN]
    diagonal = (lax.broadcasted_iota(jnp.int32, (SPAN, tile), 0) == lax.rem(lane, SPAN))[:, : 2 * SPAN]
    eye = (
        lax.broadcasted_iota(jnp.int32, (2 * SPAN, 2 * SPAN), 0)
        == lax.broadcasted_iota(jnp.int32, (2 * SPAN, 2 * SPAN), 1)
    ).astype(BF16)

    def fold(x, op):
        parts = [x[8 * i : 8 * i + 8] for i in range(x.shape[0] // 8)]
        while len(parts) > 1:
            parts = [
                op(parts[i], parts[i + 1]) if i + 1 < len(parts) else parts[i]
                for i in range(0, len(parts), 2)
            ]
        return parts[0]

    def term_copy(h, dst, src):
        return pltpu.make_async_remote_copy(
            src_ref=term.at[dst, h],
            dst_ref=rterm.at[src, h],
            send_sem=rsend.at[h, dst],
            recv_sem=rrecv.at[h, src],
            device_id={"seq": shard_at(dst)},
            device_id_type=MESH,
        )

    def tile_copy(h, to):
        return pltpu.make_async_remote_copy(
            src_ref=stage.at[h, to],
            dst_ref=out.at[hd * heads + h],
            send_sem=asend.at[h, to],
            recv_sem=arecv.at[hd],
            device_id={"head": to},
            device_id_type=MESH,
        )

    def cross_copies(m, packed):
        h = m // 2
        to = other_chip + lax.rem(m, 2)
        if not packed:
            return [tile_copy(h, to)]
        e = h - plain
        return [
            pltpu.make_async_remote_copy(
                src_ref=tri_stage.at[e, lax.rem(m, 2)],
                dst_ref=tri.at[lax.rem(hd, 2), e],
                send_sem=tsend.at[m - 2 * plain],
                recv_sem=trecv.at[lax.rem(hd, 2)],
                device_id={"head": to},
                device_id_type=MESH,
            ),
            pltpu.make_async_remote_copy(
                src_ref=stage.at[h, to, 0],
                dst_ref=out.at[hd * heads + h, 0],
                send_sem=asend.at[h, to],
                recv_sem=arecv.at[hd],
                device_id={"head": to},
                device_id_type=MESH,
            ),
        ]

    def send_cross(m):
        for packed in (False, True):

            @pl.when(((m >= 2 * plain) & (m < 2 * heads - 1)) == packed)
            def _():
                for copy in cross_copies(m, packed):
                    copy.start()

    def wait_cross(m):
        for packed in (False, True):

            @pl.when(((m >= 2 * plain) & (m < 2 * heads - 1)) == packed)
            def _():
                for copy in cross_copies(m, packed):
                    copy.wait_send()

    def add_terms(h):
        def term_wait(k, _):
            term_copy(h, plane, to_later(k)).wait_recv()
            return 0

        lax.fori_loop(1, later, term_wait, 0)
        total_own = own[:, h]
        for src in range(nplane):
            total_own = total_own + rterm[src, h].astype(F32)
        own[:, h] = total_own

    place_row = lax.broadcasted_iota(jnp.int32, (rows, tile), 0)
    pair_of = place_row // per_dev
    row_id = (
        (lax.rem(pair_of, 2) * PLACES + pair_of // 2) * per_dev + lax.rem(place_row, per_dev)
    )
    lane_span = lax.broadcasted_iota(jnp.int32, (rows, tile), 1) // SPAN
    zero = jnp.zeros((SPAN, 2 * SPAN), F32)

    def step(n, _):
        h = n // 2
        own_chip = lax.rem(n, 2)
        chip = lax.rem(hd // 2 + 1 + own_chip, 2)
        cols = pl.ds(pl.multiple_of(h * HEAD_DIM, HEAD_DIM), HEAD_DIM)

        def sk(c):
            return sumk[h, c].reshape(rows, HEAD_DIM)

        def sv(c):
            return sumv[h, :, c].reshape(rows, HEAD_DIM)

        @pl.when(own_chip == 0)
        def _():
            for kind in (2, 3):
                gather_each(kind, h, "arrived")
            for c in range(nchunk):
                summ_t[:, c * rows : (c + 1) * rows] = sk(c).astype(F32).T.astype(BF16)
            acc[...] = jnp.zeros(acc.shape, F32)

        def local(a, b):
            picked = []
            for p in range(tile // (2 * SPAN)):
                sl = slice(p * 2 * SPAN, (p + 1) * 2 * SPAN)
                full = dot(a[sl], b[sl], NT)
                picked.append(jnp.where(low128, full[:SPAN], full[SPAN:]))
            return jnp.concatenate(picked, axis=1)

        tri_at = jnp.where((h >= plain) & (own_chip == 0), h - plain, EARLY)
        q, k, v, d, base, top, inv, delta, p_loc, a_loc, dp_loc, dqt = ([None, None] for _ in range(12))

        def scores(t):
            trow = pl.ds(pl.multiple_of((chip * 2 + t) * tile, tile), tile)
            q[t], k[t], v[t], d[t] = (r[trow, cols] for r in (q_ref, k_ref, v_ref, d_ref))
            a_loc[t] = jnp.where(causal, local(k[t], q[t]), -jnp.inf)
            most = fold(a_loc[t], jnp.maximum)
            span_of = me * per_dev + (chip * 2 + t) * (tile // SPAN) + lane_span
            for c in range(nchunk):
                x = dot(sk(c), q[t], NT)
                x = jnp.where(row_id + c * rows < span_of, x, -jnp.inf)
                s_scr[t, c * rows : (c + 1) * rows] = x
                most = jnp.maximum(most, fold(x, jnp.maximum))
            base[t] = jnp.max(most, axis=0, keepdims=True) * c2

        def weights(t):
            dp_loc[t] = local(v[t], d[t])
            e_loc = jnp.exp2(a_loc[t] * c2 - base[t])
            mass = fold(e_loc, jnp.add)
            weighted = fold(e_loc * dp_loc[t], jnp.add)
            for c in range(nchunk):
                sl = slice(c * rows, (c + 1) * rows)
                dp = dot(sv(c), d[t], NT)
                e = jnp.exp2(s_scr[t, sl] * c2 - base[t])
                s_scr[t, sl] = e
                dp_scr[t, sl] = dp
                mass = mass + fold(e, jnp.add)
                weighted = weighted + fold(e * dp, jnp.add)
            inv[t] = 1.0 / jnp.sum(mass, axis=0, keepdims=True)
            delta[t] = jnp.sum(weighted, axis=0, keepdims=True) * inv[t]
            p_loc[t] = e_loc * inv[t]

        def local_grads(t):
            to = chip * 2 + t
            g_loc = p_loc[t] * (dp_loc[t] - delta[t])
            parts = []
            for p in range(tile // (2 * SPAN)):
                sl = slice(p * 2 * SPAN, (p + 1) * 2 * SPAN)
                g = g_loc[:, sl]
                w = p_loc[t][:, sl]
                g2 = jnp.concatenate(
                    [jnp.where(low128, g, zero), jnp.where(low128, zero, g)], axis=0
                ).astype(BF16)
                w2 = jnp.concatenate(
                    [jnp.where(low128, w, zero), jnp.where(low128, zero, w)], axis=0
                ).astype(BF16)
                stage[h, to, 1, sl] = (dot(g2, q[t][sl], NN) * scale).astype(BF16)
                stage[h, to, 2, sl] = dot(w2, d[t][sl], NN).astype(BF16)
                turned = dot(eye, w2, NT)
                turned = jnp.where(low128, turned[:SPAN], turned[SPAN:])
                tri_stage[tri_at, t, :SPAN, sl] = jnp.where(causal[:, sl], g, turned).astype(BF16)
                main = jnp.sum(jnp.where(diagonal, w, zero), axis=0, keepdims=True)
                tri_stage[tri_at, t, SPAN:, sl] = jnp.broadcast_to(main, (16, 2 * SPAN)).astype(BF16)
                parts.append(dot(k[t][sl], g2, TN))
            dqt[t] = jnp.concatenate(parts, axis=1)

        for t in range(2):
            scores(t)
        for t in range(2):
            weights(t)
        for t in range(2):
            local_grads(t)
        for c in range(nchunk):
            sl = slice(c * rows, (c + 1) * rows)
            for t in range(2):
                r = s_scr[t, sl] * inv[t]
                g = (r * (dp_scr[t, sl] - delta[t])).astype(BF16)
                add_k = dot(g, q[t], NN)
                add_v = dot(r.astype(BF16), d[t], NN)
                sum_k, sum_v = (add_k, add_v) if t == 0 else (sum_k + add_k, sum_v + add_v)
                dqt[t] = dqt[t] + dot(summ_t[:, sl], g, NN)
            acc[0, sl] += sum_k
            acc[1, sl] += sum_v
        for t in range(2):
            stage[h, chip * 2 + t, 0] = (dqt[t] * scale).T.astype(BF16)

        @pl.when(own_chip == 0)
        def _():
            @pl.when(h == 0)
            def _():
                send_cross(0)

            @pl.when(h >= 1)
            def _():
                wait_cross(h - 1)

            send_cross(h + 1)


        @pl.when(own_chip == 1)
        def _():
            tile_copy(h, hd + 1 - 2 * lax.rem(hd, 2)).start()
            pltpu.make_async_copy(stage.at[h, hd], out.at[hd * heads + h], local_sem.at[h]).start()
            mine = pl.ds(pl.multiple_of(plane * 2 * per_dev, 2 * per_dev), 2 * per_dev)
            for w in range(2):
                term[:, h, :, w] = acc[w].reshape(nplane, 2, per_dev, HEAD_DIM).astype(BF16)
                own[:, h, w] = acc[w, mine].reshape(2, per_dev, HEAD_DIM)

            def send_term(k, _):
                dst = to_earlier(k)
                term_copy(h, dst, plane).start()
                return 0

            lax.fori_loop(1, earlier, send_term, 0)

        return 0

    lax.fori_loop(0, heads * 2, step, 0)

    send_cross(heads + 1)
    send_cross(heads + 2)
    for h in range(heads):
        add_terms(h)

    part = per_dev // nhead
    half = heads // 2

    def sums_of(which, w):
        factor = scale if w == 0 else 1.0
        return [own[which, h, w] * factor for h in range(heads)]

    def share_of(blocks, dst):
        rows_of = slice(dst * part, (dst + 1) * part)
        pieces = [
            jnp.concatenate([blocks[w][b * half + a][rows_of] for a in range(half)], axis=1)
            for w in range(2)
            for b in range(2)
        ]
        return (jnp.concatenate(pieces, axis=0) * (1.0 / SPAN)).astype(BF16)

    mine = [sums_of(side, w) for w in range(2)]
    theirs = [sums_of(1 - side, w) for w in range(2)]
    for w in range(2):
        for h in range(heads):
            other_own[0, h, w] = theirs[w][h].astype(BF16)
    partial = pltpu.make_async_remote_copy(
        src_ref=other_own.at[0],
        dst_ref=other_own.at[1],
        send_sem=psend,
        recv_sem=precv,
        device_id={"seq": partner},
        device_id_type=MESH,
    )
    partial.start()
    for dst in range(nhead):
        sgs[0, dst] = share_of(mine, dst)
        sgs[1, dst] = share_of(theirs, dst)

    def shared_copy(at, shard, from_side, src, dst):
        return pltpu.make_async_remote_copy(
            src_ref=sgs.at[at, dst],
            dst_ref=shared.at[from_side, src],
            send_sem=ssend.at[at, dst],
            recv_sem=srecv.at[from_side, src],
            device_id={"seq": shard, "head": dst},
            device_id_type=MESH,
        )

    for k in range(1, nhead):
        other = lax.rem(hd + k, nhead)
        shared_copy(1, partner, side, hd, other).start()
        shared_copy(0, me, side, hd, other).start()
    for m in range(heads + 3, 2 * heads):
        send_cross(m)
    keep = pltpu.make_async_copy(sgs.at[0, hd], shared.at[side, hd], own_sem)
    keep.start()
    keep.wait()
    partial.wait()
    arrived = [[other_own[1, h, w].astype(F32) for h in range(heads)] for w in range(2)]
    gk_out[...] = jnp.concatenate([mine[0][h] + arrived[0][h] for h in range(heads)], axis=1)
    gv_out[...] = jnp.concatenate([mine[1][h] + arrived[1][h] for h in range(heads)], axis=1)
    for dst in range(nhead):

        @pl.when(hd == dst)
        def _():
            shared[1 - side, dst] = share_of(arrived, dst)

    for k in range(1, nhead):
        other = lax.rem(hd + k, nhead)
        for at, shard in ((1, partner), (0, me)):
            shared_copy(at, shard, side, hd, other).wait_send()
        for from_side in range(2):
            shared_copy(0, me, from_side, other, other).wait_recv()
        pltpu.make_async_remote_copy(
            src_ref=out.at[pl.ds(other * heads, heads)],
            dst_ref=out.at[pl.ds(other * heads, heads)],
            send_sem=asend.at[0, 0],
            recv_sem=arecv.at[other],
            device_id={"head": other},
            device_id_type=MESH,
        ).wait_recv()

    for copy in early:
        copy.wait_send()
    for m in range(heads - 1, 2 * heads):
        wait_cross(m)
    for c in range(2):
        for core, blocks in ((0, EARLY), (1, EARLY - 1)):

            @pl.when(lax.rem(hd, 2) == core)
            def _():
                pltpu.make_async_remote_copy(
                    src_ref=tri.at[c, :blocks],
                    dst_ref=tri.at[c, :blocks],
                    send_sem=tsend.at[0],
                    recv_sem=trecv.at[c],
                    device_id={"head": other_chip},
                    device_id_type=MESH,
                ).wait_recv()

    for h in range(heads):
        tile_copy(h, hd + 1 - 2 * lax.rem(hd, 2)).wait_send()
    for h in range(heads):
        pltpu.make_async_copy(stage.at[h, hd], out.at[hd * heads + h], local_sem.at[h]).wait()

    for w in range(2):
        swap_copy(w, side).wait_send()
        direct_copy(w, side, place if w == 0 else slab, 1).wait_send()
    for h in range(heads):
        for kind in range(4):
            gather_each(kind, h, "sent")

        def term_sent(k, _, h=h):
            term_copy(h, to_earlier(k), plane).wait_send()
            return 0

        lax.fori_loop(1, earlier, term_sent, 0)


def finish_kernel(
    part, pieces, shared_ref, tri, gk_in, gv_in, q_out, k_out, v_out, gk_out, gv_out, q_buf, k_buf, v_buf, sem
):
    heads = pieces.shape[0]
    cols = 2 * shared_ref.shape[3]
    group = cols // HEAD_DIM
    copies = [
        pltpu.make_async_copy(gk_in, gk_out, sem.at[0]),
        pltpu.make_async_copy(gv_in, gv_out, sem.at[1]),
    ]
    for copy in copies:
        copy.start()
    chip = lax.axis_index("head") // 2
    core = lax.rem(lax.axis_index("head"), 2)
    lane = lax.broadcasted_iota(jnp.int32, (SPAN, 2 * SPAN), 1)
    low = lane < SPAN
    t_id = lax.rem(lane, SPAN)
    u_id = lax.broadcasted_iota(jnp.int32, (SPAN, 2 * SPAN), 0)
    shares = [
        shared_ref[0, g].astype(F32) + shared_ref[1, g].astype(F32) for g in range(heads // group)
    ]
    for g in range(heads // group):
        for b in range(group):
            h = g * group + b
            cols_of = slice(h * HEAD_DIM, (h + 1) * HEAD_DIM)
            q_buf[:, cols_of] = pieces[h, 0]

            def share(w, c, b=b, g=g):
                at = (2 * w + b // 2) * part + c
                sl = slice((b % 2) * HEAD_DIM, (b % 2 + 1) * HEAD_DIM)
                return shares[g][at : at + 1, sl]

            def as_sent(h=h, cols_of=cols_of, share=share):
                for w, buf in ((0, k_buf), (1, v_buf)):
                    for c in range(part):
                        rows = slice(c * SPAN, (c + 1) * SPAN)
                        buf[rows, cols_of] = (pieces[h, 1 + w, rows].astype(F32) + share(w, c)).astype(BF16)

            def multiply(h=h, g=g, e=b - (group - EARLY), cols_of=cols_of, share=share):
                for p in range(part // 2):
                    rows = slice(p * 2 * SPAN, (p + 1) * 2 * SPAN)
                    block = tri[g % 2, e, :SPAN, rows].astype(F32)
                    main = tri[g % 2, e, SPAN : SPAN + 1, rows].astype(F32)
                    upper = jnp.where(u_id <= t_id, block, 0.0)
                    lower = jnp.where(u_id > t_id, block, jnp.where(u_id == t_id, main, 0.0))
                    for w, buf, x, dims, factor in (
                        (0, k_buf, upper, NN, HEAD_DIM ** (-0.5)),
                        (1, v_buf, lower, TN, 1.0),
                    ):
                        wide = jnp.concatenate(
                            [jnp.where(low, x, 0.0), jnp.where(low, 0.0, x)], axis=0
                        ).astype(BF16)
                        grad = dot(wide, pieces[h, 1 + w, rows], dims) * factor
                        for c in range(2):
                            at = slice((2 * p + c) * SPAN, (2 * p + c + 1) * SPAN)
                            buf[at, cols_of] = (
                                grad[c * SPAN : (c + 1) * SPAN] + share(w, 2 * p + c)
                            ).astype(BF16)

            if b < group - EARLY:
                as_sent()
            else:
                packed = chip != g // 2
                if b == group - 1:
                    packed = packed & (core == 0)
                pl.when(jnp.logical_not(packed))(as_sent)
                pl.when(packed)(multiply)
        sl = pl.ds(g * cols, cols)
        for w, (buf, ref) in enumerate(((q_buf, q_out), (k_buf, k_out), (v_buf, v_out))):
            copy = pltpu.make_async_copy(
                buf.at[:, sl], ref.at[:, sl], sem.at[2 + 3 * g + w]
            )
            copy.start()
            copies.append(copy)
    for copy in copies:
        copy.wait()


def per_device(queries, keys, values, out_grad):
    count, cols = queries.shape
    nseq = lax.axis_size("seq")
    nhead = lax.axis_size("head")
    heads = cols // HEAD_DIM
    per_dev = count // SPAN
    total = per_dev * nseq
    tile = count // nhead
    part = per_dev // nhead
    nplane = nseq // 2
    anyspace = pl.BlockSpec(memory_space=pl.ANY)
    hbm = pl.BlockSpec(memory_space=pltpu.HBM)
    vmem = pl.BlockSpec(memory_space=pltpu.VMEM)
    dma = pltpu.SemaphoreType.DMA
    pieces, grad_k, grad_v, shared, tri = pl.pallas_call(
        functools.partial(main_kernel, nseq, nhead),
        out_shape=(
            pltpu.VMEM((nhead * heads, 3, tile, HEAD_DIM), BF16),
            jax.ShapeDtypeStruct((per_dev, cols), F32),
            jax.ShapeDtypeStruct((per_dev, cols), F32),
            jax.ShapeDtypeStruct((2, nhead, 4 * part, cols // 2), BF16),
            jax.ShapeDtypeStruct((2, EARLY, SPAN + 16, tile), BF16),
        ),
        in_specs=[hbm] * 4,
        out_specs=(vmem, vmem, vmem, vmem, vmem),
        scratch_shapes=[pltpu.VMEM((count, cols), BF16)] * 4
        + [
            pltpu.VMEM((heads, nplane // PLACES, PLACES, 2, per_dev, HEAD_DIM), BF16),
            pltpu.VMEM((heads, PLACES, nplane // PLACES, 2, per_dev, HEAD_DIM), BF16),
            pltpu.VMEM((HEAD_DIM, total), BF16),
            pltpu.VMEM((2, total, HEAD_DIM), F32),
            pltpu.VMEM((nplane, heads, 2, 2, per_dev, HEAD_DIM), BF16),
            pltpu.VMEM((nplane, heads, 2, 2, per_dev, HEAD_DIM), BF16),
            pltpu.VMEM((2, heads, 2, per_dev, HEAD_DIM), F32),
            pltpu.VMEM((2, heads, 2, per_dev, HEAD_DIM), BF16),
            pltpu.VMEM((2, nhead, 4 * part, cols // 2), BF16),
            pltpu.VMEM((heads, nhead, 3, tile, HEAD_DIM), BF16),
            pltpu.VMEM((EARLY + 1, 2, SPAN + 16, tile), BF16),
            pltpu.VMEM((2, total, tile), F32),
            pltpu.VMEM((2, total, tile), F32),
            dma((4, nhead)),
            dma((2,)),
            dma((2,)),
            dma((4, heads, PLACES)),
            dma((4, heads, PLACES)),
            dma((heads, nplane)),
            dma((heads, nplane)),
            dma,
            dma,
            dma((heads, nhead)),
            dma((nhead,)),
            dma((heads,)),
            dma((2, nhead)),
            dma((2, nhead)),
            dma,
            dma((EARLY, 2, 2)),
            dma((2 * EARLY,)),
            dma((2,)),
        ],
        compiler_params=pltpu.CompilerParams(
            collective_id=0, has_side_effects=True, vmem_limit_bytes=50 * 1024 * 1024
        ),
        name="attend",
    )(queries, keys, values, out_grad)
    row = jax.ShapeDtypeStruct((tile, nhead * cols), BF16)
    block = jax.ShapeDtypeStruct((per_dev, cols), F32)
    query_grad, key_grad, value_grad, grad_k, grad_v = pl.pallas_call(
        functools.partial(finish_kernel, part),
        out_shape=(row, row, row, block, block),
        in_specs=[vmem, vmem, vmem, vmem, vmem],
        out_specs=(hbm,) * 5,
        scratch_shapes=[
            pltpu.VMEM((tile, nhead * cols), BF16),
            pltpu.VMEM((tile, nhead * cols), BF16),
            pltpu.VMEM((tile, nhead * cols), BF16),
            dma((2 + 3 * nhead,)),
        ],
        compiler_params=pltpu.CompilerParams(vmem_limit_bytes=50 * 1024 * 1024),
        name="finish",
    )(pieces, shared, tri, grad_k, grad_v)
    return (query_grad, key_grad, value_grad, grad_k, grad_v)


def solution(mesh):
    placed = (P("seq", "head"), P("seq", "head"), P("seq", "head"), P("seq", "head"))
    return jax.shard_map(
        per_device,
        mesh=mesh,
        in_specs=placed,
        out_specs=(
            P(("seq", "head"), None),
            P(("seq", "head"), None),
            P(("seq", "head"), None),
            P("seq", "head"),
            P("seq", "head"),
        ),
        check_vma=False,
    )
```

```python
import functools

import jax
import jax.numpy as jnp
from jax import lax
from jax.experimental import pallas as pl
from jax.experimental.pallas import tpu as pltpu
from jax.sharding import PartitionSpec as P

HEAD_DIM = 128
SPAN = 64
PLACES = 4
SLAB = 8
EARLY = 2
MESH = pl.DeviceIdType.MESH
LOG2E = 1.4426950408889634
F32 = jnp.float32
BF16 = jnp.bfloat16
NT = (((1,), (1,)), ((), ()))
NN = (((1,), (0,)), ((), ()))
TN = (((0,), (0,)), ((), ()))


def dot(a, b, dims):
    return lax.dot_general(a, b, dims, preferred_element_type=F32)


def main_kernel(
    nseq,
    nhead,
    q_hbm, k_hbm, v_hbm, d_hbm,
    out, gk_out, gv_out, shared, tri,
    q_ref, k_ref, v_ref, d_ref,
    sumk, sumv, summ_t, acc, term, rterm, own, other_own, sgs, stage, tri_stage, s_scr, dp_scr,
    load_sem, xsend, xrecv, gsend, grecv, rsend, rrecv, psend, precv,
    asend, arecv, local_sem, ssend, srecv, own_sem, esend, tsend, trecv,
):
    me = lax.axis_index("seq")
    hd = lax.axis_index("head")
    count = q_ref.shape[0]
    heads = q_ref.shape[1] // HEAD_DIM
    per_dev = count // SPAN
    total = per_dev * nseq
    tile = count // nhead
    scale = HEAD_DIM ** (-0.5)
    c2 = scale * LOG2E
    slab = me // SLAB
    side = lax.rem(me, SLAB) // PLACES
    place = lax.rem(me, PLACES)
    plane = slab * PLACES + place
    nplane = nseq // 2
    partner = me + PLACES - 2 * PLACES * side

    def shard_at(p):
        return (p // PLACES) * SLAB + side * PLACES + lax.rem(p, PLACES)

    loads = [
        [
            pltpu.make_async_copy(
                src.at[c * tile : (c + 1) * tile], dst.at[c * tile : (c + 1) * tile], load_sem.at[i, c]
            )
            for c in range(nhead)
        ]
        for i, (src, dst) in enumerate(
            ((k_hbm, k_ref), (v_hbm, v_ref), (q_hbm, q_ref), (d_hbm, d_ref))
        )
    ]
    for group in loads:
        for load in group:
            load.start()
    sumk[...] = jnp.zeros(sumk.shape, sumk.dtype)
    sumv[...] = jnp.zeros(sumv.shape, sumv.dtype)
    rterm[...] = jnp.zeros(rterm.shape, rterm.dtype)

    barrier = pltpu.get_barrier_semaphore()

    def greet(i, _):
        pl.semaphore_signal(
            barrier,
            inc=1,
            device_id={"seq": shard_at(lax.rem(plane + i, nplane))},
            device_id_type=MESH,
        )
        return 0

    lax.fori_loop(1, nplane, greet, 0)
    pl.semaphore_signal(barrier, inc=1, device_id={"seq": partner}, device_id_type=MESH)
    for k in range(1, PLACES):
        for p in (
            slab * PLACES + lax.rem(place + k, PLACES),
            lax.rem(slab + k, PLACES) * PLACES + place,
        ):
            pl.semaphore_signal(
                barrier,
                inc=1,
                device_id={"seq": shard_at(p) + partner - me},
                device_id_type=MESH,
            )
    for i in range(1, nhead):
        for shard in (me, partner):
            pl.semaphore_signal(
                barrier,
                inc=1,
                device_id={"seq": shard, "head": lax.rem(hd + i, nhead)},
                device_id_type=MESH,
            )

    pool = (
        lax.broadcasted_iota(jnp.int32, (per_dev, count), 1) // SPAN
        == lax.broadcasted_iota(jnp.int32, (per_dev, count), 0)
    ).astype(BF16)
    for w, ref in ((0, k_ref), (1, v_ref)):
        for load in loads[w]:
            load.wait()
        mean = (dot(pool, ref[...], NN) * (1.0 / SPAN)).astype(BF16)
        for h in range(heads):
            block = mean[:, h * HEAD_DIM : (h + 1) * HEAD_DIM]
            if w == 0:
                sumk[h, slab, place, side] = block
            else:
                sumv[h, place, slab, side] = block

    pl.semaphore_wait(barrier, nplane - 1 + 1 + 2 * (PLACES - 1) + 2 * (nhead - 1))

    slabs = nplane // PLACES

    def swap_copy(w, to):
        ref = sumk.at[1:, slab, place, to] if w == 0 else sumv.at[1:, place, slab, to]
        return pltpu.make_async_remote_copy(
            src_ref=ref,
            dst_ref=ref,
            send_sem=xsend.at[w],
            recv_sem=xrecv.at[w],
            device_id={"seq": partner},
            device_id_type=MESH,
        )

    def gather_copy(kind, h, src, dst):
        ref = (
            sumk.at[h, slab, src],
            sumv.at[h, place, src],
            sumk.at[h, src],
            sumv.at[h, src],
        )[kind]
        to_place = kind in (0, 3)
        shard = slab * SLAB + side * PLACES + dst if to_place else dst * SLAB + side * PLACES + place
        return pltpu.make_async_remote_copy(
            src_ref=ref,
            dst_ref=ref,
            send_sem=gsend.at[kind, h, dst],
            recv_sem=grecv.at[kind, h, src],
            device_id={"seq": shard},
            device_id_type=MESH,
        )

    def gather_each(kind, h, what):
        def go(other, _):
            if what == "start":
                gather_copy(kind, h, mine_of, other).start()
            elif what == "sent":
                gather_copy(kind, h, mine_of, other).wait_send()
            else:
                gather_copy(kind, h, other, mine_of).wait_recv()
            return 0

        if kind in (0, 3):
            mine_of = place
            for k in range(1, PLACES):
                go(lax.rem(place + k, PLACES), 0)
        else:
            mine_of = slab
            if what == "arrived":
                lax.fori_loop(0, slab, go, 0)
            else:
                lax.fori_loop(slab + 1, slabs, go, 0)

    first = slab * PLACES
    later = nplane - first
    earlier = first + PLACES

    def to_later(k):
        return first + lax.rem(plane - first + k, later)

    def to_earlier(k):
        return lax.rem(plane + k, earlier)

    def direct_copy(w, of, dst, across):
        ref = sumk.at[0, slab, place, of] if w == 0 else sumv.at[0, place, slab, of]
        p = slab * PLACES + dst if w == 0 else dst * PLACES + place
        return pltpu.make_async_remote_copy(
            src_ref=ref,
            dst_ref=ref,
            send_sem=gsend.at[w, 0, dst],
            recv_sem=grecv.at[w, 0, place if w == 0 else slab],
            device_id={"seq": shard_at(p) + across * (partner - me)},
            device_id_type=MESH,
        )

    for k in range(PLACES):
        for across in (1, 0):
            if k > 0 or across:
                direct_copy(0, side, lax.rem(place + k, PLACES), across).start()

    def direct_values(dst, _):
        direct_copy(1, side, dst, 1).start()

        @pl.when(dst > slab)
        def _():
            direct_copy(1, side, dst, 0).start()

        return 0

    lax.fori_loop(slab, slabs, direct_values, 0)
    for w in range(2):
        swap_copy(w, side).start()
    for group in loads[2:]:
        for load in group:
            load.wait()

    plain = heads - EARLY

    other_chip = (1 - hd // 2) * 2

    def goes_early(e, j):
        return e < EARLY - 1 or j == 0

    def early_copy(e, j, w):
        ref = (q_ref, d_ref)[w]
        to = other_chip + j
        cols = slice((plain + e) * HEAD_DIM, (plain + e + 1) * HEAD_DIM)
        return pltpu.make_async_remote_copy(
            src_ref=ref.at[pl.ds(pl.multiple_of(to * tile, tile), tile), cols],
            dst_ref=out.at[hd * heads + plain + e, 1 + w],
            send_sem=esend.at[e, j, w],
            recv_sem=arecv.at[hd],
            device_id={"head": to},
            device_id_type=MESH,
        )

    early = [early_copy(e, j, w) for e in range(EARLY) for j in range(2) for w in range(2) if goes_early(e, j)]
    for copy in early:
        copy.start()
    for kind in (0, 1):
        direct_copy(kind, 1 - side, place if kind == 0 else slab, 1).wait_recv()
        gather_each(kind, 0, "arrived")
        gather_each(kind + 2, 0, "start")
    for w in range(2):
        swap_copy(w, 1 - side).wait_recv()
    for h in range(1, heads):
        for kind in (0, 1):
            gather_each(kind, h, "start")
    for h in range(1, heads):
        for kind in (0, 1):
            gather_each(kind, h, "arrived")
            gather_each(kind + 2, h, "start")

    rows = 128
    nchunk = total // rows
    lane = lax.broadcasted_iota(jnp.int32, (SPAN, tile), 1)
    low_lane = lax.rem(lane, 2 * SPAN) < SPAN
    causal = lax.broadcasted_iota(jnp.int32, (SPAN, tile), 0) <= lax.rem(lane, SPAN)
    low128 = low_lane[:, : 2 * SPAN]
    diagonal = (lax.broadcasted_iota(jnp.int32, (SPAN, tile), 0) == lax.rem(lane, SPAN))[:, : 2 * SPAN]
    eye = (
        lax.broadcasted_iota(jnp.int32, (2 * SPAN, 2 * SPAN), 0)
        == lax.broadcasted_iota(jnp.int32, (2 * SPAN, 2 * SPAN), 1)
    ).astype(BF16)

    def fold(x, op):
        parts = [x[8 * i : 8 * i + 8] for i in range(x.shape[0] // 8)]
        while len(parts) > 1:
            parts = [
                op(parts[i], parts[i + 1]) if i + 1 < len(parts) else parts[i]
                for i in range(0, len(parts), 2)
            ]
        return parts[0]

    def term_copy(h, dst, src):
        return pltpu.make_async_remote_copy(
            src_ref=term.at[dst, h],
            dst_ref=rterm.at[src, h],
            send_sem=rsend.at[h, dst],
            recv_sem=rrecv.at[h, src],
            device_id={"seq": shard_at(dst)},
            device_id_type=MESH,
        )

    def tile_copy(h, to):
        return pltpu.make_async_remote_copy(
            src_ref=stage.at[h, to],
            dst_ref=out.at[hd * heads + h],
            send_sem=asend.at[h, to],
            recv_sem=arecv.at[hd],
            device_id={"head": to},
            device_id_type=MESH,
        )

    def cross_copies(m, packed):
        h = m // 2
        to = other_chip + lax.rem(m, 2)
        if not packed:
            return [tile_copy(h, to)]
        e = h - plain
        return [
            pltpu.make_async_remote_copy(
                src_ref=tri_stage.at[e, lax.rem(m, 2)],
                dst_ref=tri.at[lax.rem(hd, 2), e],
                send_sem=tsend.at[m - 2 * plain],
                recv_sem=trecv.at[lax.rem(hd, 2)],
                device_id={"head": to},
                device_id_type=MESH,
            ),
            pltpu.make_async_remote_copy(
                src_ref=stage.at[h, to, 0],
                dst_ref=out.at[hd * heads + h, 0],
                send_sem=asend.at[h, to],
                recv_sem=arecv.at[hd],
                device_id={"head": to},
                device_id_type=MESH,
            ),
        ]

    def send_cross(m):
        for packed in (False, True):

            @pl.when(((m >= 2 * plain) & (m < 2 * heads - 1)) == packed)
            def _():
                for copy in cross_copies(m, packed):
                    copy.start()

    def wait_cross(m):
        for packed in (False, True):

            @pl.when(((m >= 2 * plain) & (m < 2 * heads - 1)) == packed)
            def _():
                for copy in cross_copies(m, packed):
                    copy.wait_send()

    def add_terms(h):
        def term_wait(k, _):
            term_copy(h, plane, to_later(k)).wait_recv()
            return 0

        lax.fori_loop(1, later, term_wait, 0)
        total_own = own[:, h]
        for src in range(nplane):
            total_own = total_own + rterm[src, h].astype(F32)
        own[:, h] = total_own

    place_row = lax.broadcasted_iota(jnp.int32, (rows, tile), 0)
    pair_of = place_row // per_dev
    row_id = (
        (lax.rem(pair_of, 2) * PLACES + pair_of // 2) * per_dev + lax.rem(place_row, per_dev)
    )
    lane_span = lax.broadcasted_iota(jnp.int32, (rows, tile), 1) // SPAN
    zero = jnp.zeros((SPAN, 2 * SPAN), F32)

    def step(n, _):
        h = n // 2
        own_chip = lax.rem(n, 2)
        chip = lax.rem(hd // 2 + 1 + own_chip, 2)
        cols = pl.ds(pl.multiple_of(h * HEAD_DIM, HEAD_DIM), HEAD_DIM)

        def sk(c):
            return sumk[h, c].reshape(rows, HEAD_DIM)

        def sv(c):
            return sumv[h, :, c].reshape(rows, HEAD_DIM)

        @pl.when(own_chip == 0)
        def _():
            for kind in (2, 3):
                gather_each(kind, h, "arrived")
            for c in range(nchunk):
                summ_t[:, c * rows : (c + 1) * rows] = sk(c).astype(F32).T.astype(BF16)
            acc[...] = jnp.zeros(acc.shape, F32)

        def local(a, b):
            picked = []
            for p in range(tile // (2 * SPAN)):
                sl = slice(p * 2 * SPAN, (p + 1) * 2 * SPAN)
                full = dot(a[sl], b[sl], NT)
                picked.append(jnp.where(low128, full[:SPAN], full[SPAN:]))
            return jnp.concatenate(picked, axis=1)

        tri_at = jnp.where((h >= plain) & (own_chip == 0), h - plain, EARLY)
        q, k, v, d, base, top, inv, delta, p_loc, a_loc, dp_loc, dqt = ([None, None] for _ in range(12))

        def scores(t):
            trow = pl.ds(pl.multiple_of((chip * 2 + t) * tile, tile), tile)
            q[t], k[t], v[t], d[t] = (r[trow, cols] for r in (q_ref, k_ref, v_ref, d_ref))
            a_loc[t] = jnp.where(causal, local(k[t], q[t]), -jnp.inf)
            most = fold(a_loc[t], jnp.maximum)
            span_of = me * per_dev + (chip * 2 + t) * (tile // SPAN) + lane_span
            for c in range(nchunk):
                x = dot(sk(c), q[t], NT)
                x = jnp.where(row_id + c * rows < span_of, x, -jnp.inf)
                s_scr[t, c * rows : (c + 1) * rows] = x
                most = jnp.maximum(most, fold(x, jnp.maximum))
            base[t] = jnp.max(most, axis=0, keepdims=True) * c2

        def weights(t):
            dp_loc[t] = local(v[t], d[t])
            e_loc = jnp.exp2(a_loc[t] * c2 - base[t])
            mass = fold(e_loc, jnp.add)
            weighted = fold(e_loc * dp_loc[t], jnp.add)
            for c in range(nchunk):
                sl = slice(c * rows, (c + 1) * rows)
                dp = dot(sv(c), d[t], NT)
                e = jnp.exp2(s_scr[t, sl] * c2 - base[t])
                s_scr[t, sl] = e
                dp_scr[t, sl] = dp
                mass = mass + fold(e, jnp.add)
                weighted = weighted + fold(e * dp, jnp.add)
            inv[t] = 1.0 / jnp.sum(mass, axis=0, keepdims=True)
            delta[t] = jnp.sum(weighted, axis=0, keepdims=True) * inv[t]
            p_loc[t] = e_loc * inv[t]

        def local_grads(t):
            to = chip * 2 + t
            g_loc = p_loc[t] * (dp_loc[t] - delta[t])
            parts = []
            for p in range(tile // (2 * SPAN)):
                sl = slice(p * 2 * SPAN, (p + 1) * 2 * SPAN)
                g = g_loc[:, sl]
                w = p_loc[t][:, sl]
                g2 = jnp.concatenate(
                    [jnp.where(low128, g, zero), jnp.where(low128, zero, g)], axis=0
                ).astype(BF16)
                w2 = jnp.concatenate(
                    [jnp.where(low128, w, zero), jnp.where(low128, zero, w)], axis=0
                ).astype(BF16)
                stage[h, to, 1, sl] = (dot(g2, q[t][sl], NN) * scale).astype(BF16)
                stage[h, to, 2, sl] = dot(w2, d[t][sl], NN).astype(BF16)
                turned = dot(eye, w2, NT)
                turned = jnp.where(low128, turned[:SPAN], turned[SPAN:])
                tri_stage[tri_at, t, :SPAN, sl] = jnp.where(causal[:, sl], g, turned).astype(BF16)
                main = jnp.sum(jnp.where(diagonal, w, zero), axis=0, keepdims=True)
                tri_stage[tri_at, t, SPAN:, sl] = jnp.broadcast_to(main, (16, 2 * SPAN)).astype(BF16)
                parts.append(dot(k[t][sl], g2, TN))
            dqt[t] = jnp.concatenate(parts, axis=1)

        for t in range(2):
            scores(t)
        for t in range(2):
            weights(t)
        for t in range(2):
            local_grads(t)
        for c in range(nchunk):
            sl = slice(c * rows, (c + 1) * rows)
            for t in range(2):
                r = s_scr[t, sl] * inv[t]
                g = (r * (dp_scr[t, sl] - delta[t])).astype(BF16)
                add_k = dot(g, q[t], NN)
                add_v = dot(r.astype(BF16), d[t], NN)
                sum_k, sum_v = (add_k, add_v) if t == 0 else (sum_k + add_k, sum_v + add_v)
                dqt[t] = dqt[t] + dot(summ_t[:, sl], g, NN)
            acc[0, sl] += sum_k
            acc[1, sl] += sum_v
        for t in range(2):
            stage[h, chip * 2 + t, 0] = (dqt[t] * scale).T.astype(BF16)

        @pl.when(own_chip == 0)
        def _():
            @pl.when(h == 0)
            def _():
                send_cross(0)

            @pl.when(h >= 1)
            def _():
                wait_cross(h - 1)

            send_cross(h + 1)


        @pl.when(own_chip == 1)
        def _():
            tile_copy(h, hd + 1 - 2 * lax.rem(hd, 2)).start()
            pltpu.make_async_copy(stage.at[h, hd], out.at[hd * heads + h], local_sem.at[h]).start()
            mine = pl.ds(pl.multiple_of(plane * 2 * per_dev, 2 * per_dev), 2 * per_dev)
            for w in range(2):
                term[:, h, :, w] = acc[w].reshape(nplane, 2, per_dev, HEAD_DIM).astype(BF16)
                own[:, h, w] = acc[w, mine].reshape(2, per_dev, HEAD_DIM)

            def send_term(k, _):
                dst = to_earlier(k)
                term_copy(h, dst, plane).start()
                return 0

            lax.fori_loop(1, earlier, send_term, 0)

        return 0

    lax.fori_loop(0, heads * 2, step, 0)

    send_cross(heads + 1)
    send_cross(heads + 2)
    for h in range(heads):
        add_terms(h)

    part = per_dev // nhead
    half = heads // 2

    def sums_of(which, w):
        factor = scale if w == 0 else 1.0
        return [own[which, h, w] * factor for h in range(heads)]

    def share_of(blocks, dst):
        rows_of = slice(dst * part, (dst + 1) * part)
        pieces = [
            jnp.concatenate([blocks[w][b * half + a][rows_of] for a in range(half)], axis=1)
            for w in range(2)
            for b in range(2)
        ]
        return (jnp.concatenate(pieces, axis=0) * (1.0 / SPAN)).astype(BF16)

    mine = [sums_of(side, w) for w in range(2)]
    theirs = [sums_of(1 - side, w) for w in range(2)]
    for w in range(2):
        for h in range(heads):
            other_own[0, h, w] = theirs[w][h].astype(BF16)
    partial = pltpu.make_async_remote_copy(
        src_ref=other_own.at[0],
        dst_ref=other_own.at[1],
        send_sem=psend,
        recv_sem=precv,
        device_id={"seq": partner},
        device_id_type=MESH,
    )
    partial.start()
    for dst in range(nhead):
        sgs[0, dst] = share_of(mine, dst)
        sgs[1, dst] = share_of(theirs, dst)

    def shared_copy(at, shard, from_side, src, dst):
        return pltpu.make_async_remote_copy(
            src_ref=sgs.at[at, dst],
            dst_ref=shared.at[from_side, src],
            send_sem=ssend.at[at, dst],
            recv_sem=srecv.at[from_side, src],
            device_id={"seq": shard, "head": dst},
            device_id_type=MESH,
        )

    for k in range(1, nhead):
        other = lax.rem(hd + k, nhead)
        shared_copy(1, partner, side, hd, other).start()
        shared_copy(0, me, side, hd, other).start()
    for m in range(heads + 3, 2 * heads):
        send_cross(m)
    keep = pltpu.make_async_copy(sgs.at[0, hd], shared.at[side, hd], own_sem)
    keep.start()
    keep.wait()
    partial.wait()
    arrived = [[other_own[1, h, w].astype(F32) for h in range(heads)] for w in range(2)]
    gk_out[...] = jnp.concatenate([mine[0][h] + arrived[0][h] for h in range(heads)], axis=1)
    gv_out[...] = jnp.concatenate([mine[1][h] + arrived[1][h] for h in range(heads)], axis=1)
    for dst in range(nhead):

        @pl.when(hd == dst)
        def _():
            shared[1 - side, dst] = share_of(arrived, dst)

    for k in range(1, nhead):
        other = lax.rem(hd + k, nhead)
        for at, shard in ((1, partner), (0, me)):
            shared_copy(at, shard, side, hd, other).wait_send()
        for from_side in range(2):
            shared_copy(0, me, from_side, other, other).wait_recv()
        pltpu.make_async_remote_copy(
            src_ref=out.at[pl.ds(other * heads, heads)],
            dst_ref=out.at[pl.ds(other * heads, heads)],
            send_sem=asend.at[0, 0],
            recv_sem=arecv.at[other],
            device_id={"head": other},
            device_id_type=MESH,
        ).wait_recv()

    for copy in early:
        copy.wait_send()
    for m in range(heads - 1, 2 * heads):
        wait_cross(m)
    for c in range(2):
        for core, blocks in ((0, EARLY), (1, EARLY - 1)):

            @pl.when(lax.rem(hd, 2) == core)
            def _():
                pltpu.make_async_remote_copy(
                    src_ref=tri.at[c, :blocks],
                    dst_ref=tri.at[c, :blocks],
                    send_sem=tsend.at[0],
                    recv_sem=trecv.at[c],
                    device_id={"head": other_chip},
                    device_id_type=MESH,
                ).wait_recv()

    for h in range(heads):
        tile_copy(h, hd + 1 - 2 * lax.rem(hd, 2)).wait_send()
    for h in range(heads):
        pltpu.make_async_copy(stage.at[h, hd], out.at[hd * heads + h], local_sem.at[h]).wait()

    for w in range(2):
        swap_copy(w, side).wait_send()
        direct_copy(w, side, place if w == 0 else slab, 1).wait_send()
    for h in range(heads):
        for kind in range(4):
            gather_each(kind, h, "sent")

        def term_sent(k, _, h=h):
            term_copy(h, to_earlier(k), plane).wait_send()
            return 0

        lax.fori_loop(1, earlier, term_sent, 0)


def finish_kernel(
    part, pieces, shared_ref, tri, gk_in, gv_in, q_out, k_out, v_out, gk_out, gv_out, k_buf, v_buf, sem
):
    heads = pieces.shape[0]
    cols = 2 * shared_ref.shape[3]
    group = cols // HEAD_DIM
    copies = [
        pltpu.make_async_copy(gk_in, gk_out, sem.at[0]),
        pltpu.make_async_copy(gv_in, gv_out, sem.at[1]),
    ]
    for h in range(heads):
        copies.append(
            pltpu.make_async_copy(
                pieces.at[h, 0], q_out.at[:, pl.ds(h * HEAD_DIM, HEAD_DIM)], sem.at[2 + h]
            )
        )
    for copy in copies:
        copy.start()
    chip = lax.axis_index("head") // 2
    core = lax.rem(lax.axis_index("head"), 2)
    head_of = [lax.rem(2 * (1 - chip) + g, heads // group) for g in range(heads // group)]
    lane = lax.broadcasted_iota(jnp.int32, (SPAN, 2 * SPAN), 1)
    low = lane < SPAN
    t_id = lax.rem(lane, SPAN)
    u_id = lax.broadcasted_iota(jnp.int32, (SPAN, 2 * SPAN), 0)
    shares = [
        shared_ref[0, g].astype(F32) + shared_ref[1, g].astype(F32) for g in head_of
    ]
    for g in range(heads // group):
        for b in range(group):
            h = g * group + b
            slot = head_of[g] * group + b
            cols_of = slice(h * HEAD_DIM, (h + 1) * HEAD_DIM)

            def share(w, c, b=b, g=g):
                at = (2 * w + b // 2) * part + c
                sl = slice((b % 2) * HEAD_DIM, (b % 2 + 1) * HEAD_DIM)
                return shares[g][at : at + 1, sl]

            def as_sent(slot=slot, cols_of=cols_of, share=share):
                for w, buf in ((0, k_buf), (1, v_buf)):
                    for c in range(part):
                        rows = slice(c * SPAN, (c + 1) * SPAN)
                        buf[rows, cols_of] = (pieces[slot, 1 + w, rows].astype(F32) + share(w, c)).astype(BF16)

            def multiply(slot=slot, g=g, e=b - (group - EARLY), cols_of=cols_of, share=share):
                for p in range(part // 2):
                    rows = slice(p * 2 * SPAN, (p + 1) * 2 * SPAN)
                    block = tri[g, e, :SPAN, rows].astype(F32)
                    main = tri[g, e, SPAN : SPAN + 1, rows].astype(F32)
                    upper = jnp.where(u_id <= t_id, block, 0.0)
                    lower = jnp.where(u_id > t_id, block, jnp.where(u_id == t_id, main, 0.0))
                    for w, buf, x, dims, factor in (
                        (0, k_buf, upper, NN, HEAD_DIM ** (-0.5)),
                        (1, v_buf, lower, TN, 1.0),
                    ):
                        wide = jnp.concatenate(
                            [jnp.where(low, x, 0.0), jnp.where(low, 0.0, x)], axis=0
                        ).astype(BF16)
                        grad = dot(wide, pieces[slot, 1 + w, rows], dims) * factor
                        for c in range(2):
                            at = slice((2 * p + c) * SPAN, (2 * p + c + 1) * SPAN)
                            buf[at, cols_of] = (
                                grad[c * SPAN : (c + 1) * SPAN] + share(w, 2 * p + c)
                            ).astype(BF16)

            if g > 1 or b < group - EARLY:
                as_sent()
            elif b < group - 1:
                multiply()
            else:
                pl.when(core != 0)(as_sent)
                pl.when(core == 0)(multiply)
        sl = pl.ds(g * cols, cols)
        for w, (buf, ref) in enumerate(((k_buf, k_out), (v_buf, v_out))):
            copy = pltpu.make_async_copy(
                buf.at[:, sl],
                ref.at[:, pl.ds(pl.multiple_of(head_of[g] * cols, cols), cols)],
                sem.at[2 + heads + 2 * g + w]
            )
            copy.start()
            copies.append(copy)
    for copy in copies:
        copy.wait()


def per_device(queries, keys, values, out_grad):
    count, cols = queries.shape
    nseq = lax.axis_size("seq")
    nhead = lax.axis_size("head")
    heads = cols // HEAD_DIM
    per_dev = count // SPAN
    total = per_dev * nseq
    tile = count // nhead
    part = per_dev // nhead
    nplane = nseq // 2
    anyspace = pl.BlockSpec(memory_space=pl.ANY)
    hbm = pl.BlockSpec(memory_space=pltpu.HBM)
    vmem = pl.BlockSpec(memory_space=pltpu.VMEM)
    dma = pltpu.SemaphoreType.DMA
    pieces, grad_k, grad_v, shared, tri = pl.pallas_call(
        functools.partial(main_kernel, nseq, nhead),
        out_shape=(
            pltpu.VMEM((nhead * heads, 3, tile, HEAD_DIM), BF16),
            jax.ShapeDtypeStruct((per_dev, cols), F32),
            jax.ShapeDtypeStruct((per_dev, cols), F32),
            jax.ShapeDtypeStruct((2, nhead, 4 * part, cols // 2), BF16),
            jax.ShapeDtypeStruct((2, EARLY, SPAN + 16, tile), BF16),
        ),
        in_specs=[hbm] * 4,
        out_specs=(vmem, vmem, vmem, vmem, vmem),
        scratch_shapes=[pltpu.VMEM((count, cols), BF16)] * 4
        + [
            pltpu.VMEM((heads, nplane // PLACES, PLACES, 2, per_dev, HEAD_DIM), BF16),
            pltpu.VMEM((heads, PLACES, nplane // PLACES, 2, per_dev, HEAD_DIM), BF16),
            pltpu.VMEM((HEAD_DIM, total), BF16),
            pltpu.VMEM((2, total, HEAD_DIM), F32),
            pltpu.VMEM((nplane, heads, 2, 2, per_dev, HEAD_DIM), BF16),
            pltpu.VMEM((nplane, heads, 2, 2, per_dev, HEAD_DIM), BF16),
            pltpu.VMEM((2, heads, 2, per_dev, HEAD_DIM), F32),
            pltpu.VMEM((2, heads, 2, per_dev, HEAD_DIM), BF16),
            pltpu.VMEM((2, nhead, 4 * part, cols // 2), BF16),
            pltpu.VMEM((heads, nhead, 3, tile, HEAD_DIM), BF16),
            pltpu.VMEM((EARLY + 1, 2, SPAN + 16, tile), BF16),
            pltpu.VMEM((2, total, tile), F32),
            pltpu.VMEM((2, total, tile), F32),
            dma((4, nhead)),
            dma((2,)),
            dma((2,)),
            dma((4, heads, PLACES)),
            dma((4, heads, PLACES)),
            dma((heads, nplane)),
            dma((heads, nplane)),
            dma,
            dma,
            dma((heads, nhead)),
            dma((nhead,)),
            dma((heads,)),
            dma((2, nhead)),
            dma((2, nhead)),
            dma,
            dma((EARLY, 2, 2)),
            dma((2 * EARLY,)),
            dma((2,)),
        ],
        compiler_params=pltpu.CompilerParams(
            collective_id=0, has_side_effects=True, vmem_limit_bytes=50 * 1024 * 1024
        ),
        name="attend",
    )(queries, keys, values, out_grad)
    row = jax.ShapeDtypeStruct((tile, nhead * cols), BF16)
    block = jax.ShapeDtypeStruct((per_dev, cols), F32)
    query_grad, key_grad, value_grad, grad_k, grad_v = pl.pallas_call(
        functools.partial(finish_kernel, part),
        out_shape=(row, row, row, block, block),
        in_specs=[vmem, vmem, vmem, vmem, vmem],
        out_specs=(hbm,) * 5,
        scratch_shapes=[
            pltpu.VMEM((tile, nhead * cols), BF16),
            pltpu.VMEM((tile, nhead * cols), BF16),
            dma((2 + nhead * heads + 2 * nhead,)),
        ],
        compiler_params=pltpu.CompilerParams(vmem_limit_bytes=50 * 1024 * 1024),
        name="finish",
    )(pieces, shared, tri, grad_k, grad_v)
    return (query_grad, key_grad, value_grad, grad_k, grad_v)


def solution(mesh):
    placed = (P("seq", "head"), P("seq", "head"), P("seq", "head"), P("seq", "head"))
    return jax.shard_map(
        per_device,
        mesh=mesh,
        in_specs=placed,
        out_specs=(
            P(("seq", "head"), None),
            P(("seq", "head"), None),
            P(("seq", "head"), None),
            P("seq", "head"),
            P("seq", "head"),
        ),
        check_vma=False,
    )
```

```python
import functools

import jax
import jax.numpy as jnp
from jax import lax
from jax.experimental import pallas as pl
from jax.experimental.pallas import tpu as pltpu
from jax.sharding import PartitionSpec as P

HEAD_DIM = 128
SPAN = 64
PLACES = 4
SLAB = 8
EARLY = 2
MESH = pl.DeviceIdType.MESH
LOG2E = 1.4426950408889634
F32 = jnp.float32
BF16 = jnp.bfloat16
NT = (((1,), (1,)), ((), ()))
NN = (((1,), (0,)), ((), ()))
TN = (((0,), (0,)), ((), ()))


def dot(a, b, dims):
    return lax.dot_general(a, b, dims, preferred_element_type=F32)


def main_kernel(
    nseq,
    nhead,
    q_hbm, k_hbm, v_hbm, d_hbm,
    out, gk_out, gv_out, shared, tri,
    q_ref, k_ref, v_ref, d_ref,
    sumk, sumv, summ_t, acc, term, rterm, own, other_own, sgs, stage, tri_stage, s_scr, dp_scr,
    load_sem, xsend, xrecv, gsend, grecv, rsend, rrecv, psend, precv,
    asend, arecv, local_sem, ssend, srecv, own_sem, esend, tsend, trecv,
):
    me = lax.axis_index("seq")
    hd = lax.axis_index("head")
    count = q_ref.shape[0]
    heads = q_ref.shape[1] // HEAD_DIM
    per_dev = count // SPAN
    total = per_dev * nseq
    tile = count // nhead
    scale = HEAD_DIM ** (-0.5)
    c2 = scale * LOG2E
    slab = me // SLAB
    side = lax.rem(me, SLAB) // PLACES
    place = lax.rem(me, PLACES)
    plane = slab * PLACES + place
    nplane = nseq // 2
    partner = me + PLACES - 2 * PLACES * side

    def shard_at(p):
        return (p // PLACES) * SLAB + side * PLACES + lax.rem(p, PLACES)

    loads = [
        [
            pltpu.make_async_copy(
                src.at[c * tile : (c + 1) * tile], dst.at[c * tile : (c + 1) * tile], load_sem.at[i, c]
            )
            for c in range(nhead)
        ]
        for i, (src, dst) in enumerate(
            ((k_hbm, k_ref), (v_hbm, v_ref), (q_hbm, q_ref), (d_hbm, d_ref))
        )
    ]
    for group in loads:
        for load in group:
            load.start()
    sumk[...] = jnp.zeros(sumk.shape, sumk.dtype)
    sumv[...] = jnp.zeros(sumv.shape, sumv.dtype)
    rterm[...] = jnp.zeros(rterm.shape, rterm.dtype)

    barrier = pltpu.get_barrier_semaphore()

    def greet(i, _):
        pl.semaphore_signal(
            barrier,
            inc=1,
            device_id={"seq": shard_at(lax.rem(plane + i, nplane))},
            device_id_type=MESH,
        )
        return 0

    lax.fori_loop(1, nplane, greet, 0)
    pl.semaphore_signal(barrier, inc=1, device_id={"seq": partner}, device_id_type=MESH)
    for k in range(1, PLACES):
        for p in (
            slab * PLACES + lax.rem(place + k, PLACES),
            lax.rem(slab + k, PLACES) * PLACES + place,
        ):
            pl.semaphore_signal(
                barrier,
                inc=1,
                device_id={"seq": shard_at(p) + partner - me},
                device_id_type=MESH,
            )
    for i in range(1, nhead):
        for shard in (me, partner):
            pl.semaphore_signal(
                barrier,
                inc=1,
                device_id={"seq": shard, "head": lax.rem(hd + i, nhead)},
                device_id_type=MESH,
            )

    pool = (
        lax.broadcasted_iota(jnp.int32, (per_dev, count), 1) // SPAN
        == lax.broadcasted_iota(jnp.int32, (per_dev, count), 0)
    ).astype(BF16)
    for w, ref in ((0, k_ref), (1, v_ref)):
        for load in loads[w]:
            load.wait()
        mean = (dot(pool, ref[...], NN) * (1.0 / SPAN)).astype(BF16)
        for h in range(heads):
            block = mean[:, h * HEAD_DIM : (h + 1) * HEAD_DIM]
            if w == 0:
                sumk[h, slab, place, side] = block
            else:
                sumv[h, place, slab, side] = block

    pl.semaphore_wait(barrier, nplane - 1 + 1 + 2 * (PLACES - 1) + 2 * (nhead - 1))

    slabs = nplane // PLACES

    def swap_copy(w, to):
        ref = sumk.at[1:, slab, place, to] if w == 0 else sumv.at[1:, place, slab, to]
        return pltpu.make_async_remote_copy(
            src_ref=ref,
            dst_ref=ref,
            send_sem=xsend.at[w],
            recv_sem=xrecv.at[w],
            device_id={"seq": partner},
            device_id_type=MESH,
        )

    def gather_copy(kind, h, src, dst):
        ref = (
            sumk.at[h, slab, src],
            sumv.at[h, place, src],
            sumk.at[h, src],
            sumv.at[h, src],
        )[kind]
        to_place = kind in (0, 3)
        shard = slab * SLAB + side * PLACES + dst if to_place else dst * SLAB + side * PLACES + place
        return pltpu.make_async_remote_copy(
            src_ref=ref,
            dst_ref=ref,
            send_sem=gsend.at[kind, h, dst],
            recv_sem=grecv.at[kind, h, src],
            device_id={"seq": shard},
            device_id_type=MESH,
        )

    def gather_each(kind, h, what):
        def go(other, _):
            if what == "start":
                gather_copy(kind, h, mine_of, other).start()
            elif what == "sent":
                gather_copy(kind, h, mine_of, other).wait_send()
            else:
                gather_copy(kind, h, other, mine_of).wait_recv()
            return 0

        if kind in (0, 3):
            mine_of = place
            for k in range(1, PLACES):
                go(lax.rem(place + k, PLACES), 0)
        else:
            mine_of = slab
            if what == "arrived":
                lax.fori_loop(0, slab, go, 0)
            else:
                lax.fori_loop(slab + 1, slabs, go, 0)

    first = slab * PLACES
    later = nplane - first
    earlier = first + PLACES

    def to_later(k):
        return first + lax.rem(plane - first + k, later)

    def to_earlier(k):
        return lax.rem(plane + k, earlier)

    def direct_copy(w, of, dst, across):
        ref = sumk.at[0, slab, place, of] if w == 0 else sumv.at[0, place, slab, of]
        p = slab * PLACES + dst if w == 0 else dst * PLACES + place
        return pltpu.make_async_remote_copy(
            src_ref=ref,
            dst_ref=ref,
            send_sem=gsend.at[w, 0, dst],
            recv_sem=grecv.at[w, 0, place if w == 0 else slab],
            device_id={"seq": shard_at(p) + across * (partner - me)},
            device_id_type=MESH,
        )

    for k in range(PLACES):
        for across in (1, 0):
            if k > 0 or across:
                direct_copy(0, side, lax.rem(place + k, PLACES), across).start()

    def direct_values(dst, _):
        direct_copy(1, side, dst, 1).start()

        @pl.when(dst > slab)
        def _():
            direct_copy(1, side, dst, 0).start()

        return 0

    lax.fori_loop(slab, slabs, direct_values, 0)
    for w in range(2):
        swap_copy(w, side).start()
    for group in loads[2:]:
        for load in group:
            load.wait()

    plain = heads - EARLY

    other_chip = (1 - hd // 2) * 2

    def goes_early(e, j):
        return e < EARLY - 1 or j == 0

    def early_copy(e, j, w):
        ref = (q_ref, d_ref)[w]
        to = other_chip + j
        cols = slice((plain + e) * HEAD_DIM, (plain + e + 1) * HEAD_DIM)
        return pltpu.make_async_remote_copy(
            src_ref=ref.at[pl.ds(pl.multiple_of(to * tile, tile), tile), cols],
            dst_ref=out.at[hd * heads + plain + e, 1 + w],
            send_sem=esend.at[e, j, w],
            recv_sem=arecv.at[hd],
            device_id={"head": to},
            device_id_type=MESH,
        )

    early = [early_copy(e, j, w) for e in range(EARLY) for j in range(2) for w in range(2) if goes_early(e, j)]
    for copy in early:
        copy.start()
    for kind in (0, 1):
        direct_copy(kind, 1 - side, place if kind == 0 else slab, 1).wait_recv()
        gather_each(kind, 0, "arrived")
        gather_each(kind + 2, 0, "start")
    for w in range(2):
        swap_copy(w, 1 - side).wait_recv()
    for h in range(1, heads):
        for kind in (0, 1):
            gather_each(kind, h, "start")
    for h in range(1, heads):
        for kind in (0, 1):
            gather_each(kind, h, "arrived")
            gather_each(kind + 2, h, "start")

    rows = 128
    nchunk = total // rows
    lane = lax.broadcasted_iota(jnp.int32, (SPAN, tile), 1)
    low_lane = lax.rem(lane, 2 * SPAN) < SPAN
    causal = lax.broadcasted_iota(jnp.int32, (SPAN, tile), 0) <= lax.rem(lane, SPAN)
    low128 = low_lane[:, : 2 * SPAN]
    diagonal = (lax.broadcasted_iota(jnp.int32, (SPAN, tile), 0) == lax.rem(lane, SPAN))[:, : 2 * SPAN]
    eye = (
        lax.broadcasted_iota(jnp.int32, (2 * SPAN, 2 * SPAN), 0)
        == lax.broadcasted_iota(jnp.int32, (2 * SPAN, 2 * SPAN), 1)
    ).astype(BF16)

    def fold(x, op):
        parts = [x[8 * i : 8 * i + 8] for i in range(x.shape[0] // 8)]
        while len(parts) > 1:
            parts = [
                op(parts[i], parts[i + 1]) if i + 1 < len(parts) else parts[i]
                for i in range(0, len(parts), 2)
            ]
        return parts[0]

    def term_copy(h, dst, src):
        return pltpu.make_async_remote_copy(
            src_ref=term.at[dst, h],
            dst_ref=rterm.at[src, h],
            send_sem=rsend.at[h, dst],
            recv_sem=rrecv.at[h, src],
            device_id={"seq": shard_at(dst)},
            device_id_type=MESH,
        )

    def tile_copy(h, to):
        return pltpu.make_async_remote_copy(
            src_ref=stage.at[h, to],
            dst_ref=out.at[hd * heads + h],
            send_sem=asend.at[h, to],
            recv_sem=arecv.at[hd],
            device_id={"head": to},
            device_id_type=MESH,
        )

    def cross_copies(m, packed):
        h = m // 2
        to = other_chip + lax.rem(m, 2)
        if not packed:
            return [tile_copy(h, to)]
        e = h - plain
        return [
            pltpu.make_async_remote_copy(
                src_ref=tri_stage.at[e, lax.rem(m, 2)],
                dst_ref=tri.at[lax.rem(hd, 2), e],
                send_sem=tsend.at[m - 2 * plain],
                recv_sem=trecv.at[lax.rem(hd, 2)],
                device_id={"head": to},
                device_id_type=MESH,
            ),
            pltpu.make_async_remote_copy(
                src_ref=stage.at[h, to, 0],
                dst_ref=out.at[hd * heads + h, 0],
                send_sem=asend.at[h, to],
                recv_sem=arecv.at[hd],
                device_id={"head": to},
                device_id_type=MESH,
            ),
        ]

    def send_cross(m):
        for packed in (False, True):

            @pl.when(((m >= 2 * plain) & (m < 2 * heads - 1)) == packed)
            def _():
                for copy in cross_copies(m, packed):
                    copy.start()

    def wait_cross(m):
        for packed in (False, True):

            @pl.when(((m >= 2 * plain) & (m < 2 * heads - 1)) == packed)
            def _():
                for copy in cross_copies(m, packed):
                    copy.wait_send()

    def add_terms(h):
        def term_wait(k, _):
            term_copy(h, plane, to_later(k)).wait_recv()
            return 0

        lax.fori_loop(1, later, term_wait, 0)
        total_own = own[:, h]
        for src in range(nplane):
            total_own = total_own + rterm[src, h].astype(F32)
        own[:, h] = total_own

    place_row = lax.broadcasted_iota(jnp.int32, (rows, tile), 0)
    pair_of = place_row // per_dev
    row_id = (
        (lax.rem(pair_of, 2) * PLACES + pair_of // 2) * per_dev + lax.rem(place_row, per_dev)
    )
    lane_span = lax.broadcasted_iota(jnp.int32, (rows, tile), 1) // SPAN
    zero = jnp.zeros((SPAN, 2 * SPAN), F32)

    def step(n, _):
        h = n // 2
        own_chip = lax.rem(n, 2)
        chip = lax.rem(hd // 2 + 1 + own_chip, 2)
        cols = pl.ds(pl.multiple_of(h * HEAD_DIM, HEAD_DIM), HEAD_DIM)

        def sk(c):
            return sumk[h, c].reshape(rows, HEAD_DIM)

        def sv(c):
            return sumv[h, :, c].reshape(rows, HEAD_DIM)

        @pl.when(own_chip == 0)
        def _():
            for kind in (2, 3):
                gather_each(kind, h, "arrived")
            for c in range(nchunk):
                summ_t[:, c * rows : (c + 1) * rows] = sk(c).astype(F32).T.astype(BF16)
            acc[...] = jnp.zeros(acc.shape, F32)

        def local(a, b):
            picked = []
            for p in range(tile // (2 * SPAN)):
                sl = slice(p * 2 * SPAN, (p + 1) * 2 * SPAN)
                full = dot(a[sl], b[sl], NT)
                picked.append(jnp.where(low128, full[:SPAN], full[SPAN:]))
            return jnp.concatenate(picked, axis=1)

        tri_at = jnp.where((h >= plain) & (own_chip == 0), h - plain, EARLY)
        q, k, v, d, base, top, inv, delta, p_loc, a_loc, dp_loc, dqt = ([None, None] for _ in range(12))

        def scores(t):
            trow = pl.ds(pl.multiple_of((chip * 2 + t) * tile, tile), tile)
            q[t], k[t], v[t], d[t] = (r[trow, cols] for r in (q_ref, k_ref, v_ref, d_ref))
            a_loc[t] = jnp.where(causal, local(k[t], q[t]), -jnp.inf)
            most = fold(a_loc[t], jnp.maximum)
            span_of = me * per_dev + (chip * 2 + t) * (tile // SPAN) + lane_span
            for c in range(nchunk):
                x = dot(sk(c), q[t], NT)
                x = jnp.where(row_id + c * rows < span_of, x, -jnp.inf)
                s_scr[t, c * rows : (c + 1) * rows] = x
                most = jnp.maximum(most, fold(x, jnp.maximum))
            base[t] = jnp.max(most, axis=0, keepdims=True) * c2

        def weights(t):
            dp_loc[t] = local(v[t], d[t])
            e_loc = jnp.exp2(a_loc[t] * c2 - base[t])
            mass = fold(e_loc, jnp.add)
            weighted = fold(e_loc * dp_loc[t], jnp.add)
            for c in range(nchunk):
                sl = slice(c * rows, (c + 1) * rows)
                dp = dot(sv(c), d[t], NT)
                e = jnp.exp2(s_scr[t, sl] * c2 - base[t])
                s_scr[t, sl] = e
                dp_scr[t, sl] = dp
                mass = mass + fold(e, jnp.add)
                weighted = weighted + fold(e * dp, jnp.add)
            inv[t] = 1.0 / jnp.sum(mass, axis=0, keepdims=True)
            delta[t] = jnp.sum(weighted, axis=0, keepdims=True) * inv[t]
            p_loc[t] = e_loc * inv[t]

        def local_grads(t):
            to = chip * 2 + t
            g_loc = p_loc[t] * (dp_loc[t] - delta[t])
            parts = []
            for p in range(tile // (2 * SPAN)):
                sl = slice(p * 2 * SPAN, (p + 1) * 2 * SPAN)
                g = g_loc[:, sl]
                w = p_loc[t][:, sl]
                g2 = jnp.concatenate(
                    [jnp.where(low128, g, zero), jnp.where(low128, zero, g)], axis=0
                ).astype(BF16)
                w2 = jnp.concatenate(
                    [jnp.where(low128, w, zero), jnp.where(low128, zero, w)], axis=0
                ).astype(BF16)
                stage[h, to, 1, sl] = (dot(g2, q[t][sl], NN) * scale).astype(BF16)
                stage[h, to, 2, sl] = dot(w2, d[t][sl], NN).astype(BF16)
                turned = dot(eye, w2, NT)
                turned = jnp.where(low128, turned[:SPAN], turned[SPAN:])
                tri_stage[tri_at, t, :SPAN, sl] = jnp.where(causal[:, sl], g, turned).astype(BF16)
                main = jnp.sum(jnp.where(diagonal, w, zero), axis=0, keepdims=True)
                tri_stage[tri_at, t, SPAN:, sl] = jnp.broadcast_to(main, (16, 2 * SPAN)).astype(BF16)
                parts.append(dot(k[t][sl], g2, TN))
            dqt[t] = jnp.concatenate(parts, axis=1)

        for t in range(2):
            scores(t)
        for t in range(2):
            weights(t)
        for t in range(2):
            local_grads(t)
        for c in range(nchunk):
            sl = slice(c * rows, (c + 1) * rows)
            for t in range(2):
                r = s_scr[t, sl] * inv[t]
                g = (r * (dp_scr[t, sl] - delta[t])).astype(BF16)
                add_k = dot(g, q[t], NN)
                add_v = dot(r.astype(BF16), d[t], NN)
                sum_k, sum_v = (add_k, add_v) if t == 0 else (sum_k + add_k, sum_v + add_v)
                dqt[t] = dqt[t] + dot(summ_t[:, sl], g, NN)
            acc[0, sl] += sum_k
            acc[1, sl] += sum_v
        for t in range(2):
            stage[h, chip * 2 + t, 0] = (dqt[t] * scale).T.astype(BF16)

        @pl.when(own_chip == 0)
        def _():
            @pl.when(h == 0)
            def _():
                send_cross(0)

            @pl.when(h >= 1)
            def _():
                wait_cross(h - 1)

            send_cross(h + 1)

            @pl.when(h >= 2)
            def _():
                add_terms(h - 2)


        @pl.when(own_chip == 1)
        def _():
            tile_copy(h, hd + 1 - 2 * lax.rem(hd, 2)).start()
            pltpu.make_async_copy(stage.at[h, hd], out.at[hd * heads + h], local_sem.at[h]).start()
            mine = pl.ds(pl.multiple_of(plane * 2 * per_dev, 2 * per_dev), 2 * per_dev)
            for w in range(2):
                term[:, h, :, w] = acc[w].reshape(nplane, 2, per_dev, HEAD_DIM).astype(BF16)
                own[:, h, w] = acc[w, mine].reshape(2, per_dev, HEAD_DIM)

            def send_term(k, _):
                dst = to_earlier(k)
                term_copy(h, dst, plane).start()
                return 0

            lax.fori_loop(1, earlier, send_term, 0)

        return 0

    lax.fori_loop(0, heads * 2, step, 0)

    send_cross(heads + 1)
    send_cross(heads + 2)
    for h in range(heads - 2, heads):
        add_terms(h)

    part = per_dev // nhead
    half = heads // 2

    def sums_of(which, w):
        factor = scale if w == 0 else 1.0
        return [own[which, h, w] * factor for h in range(heads)]

    def share_of(blocks, dst):
        rows_of = slice(dst * part, (dst + 1) * part)
        pieces = [
            jnp.concatenate([blocks[w][b * half + a][rows_of] for a in range(half)], axis=1)
            for w in range(2)
            for b in range(2)
        ]
        return (jnp.concatenate(pieces, axis=0) * (1.0 / SPAN)).astype(BF16)

    mine = [sums_of(side, w) for w in range(2)]
    theirs = [sums_of(1 - side, w) for w in range(2)]
    for w in range(2):
        for h in range(heads):
            other_own[0, h, w] = theirs[w][h].astype(BF16)
    partial = pltpu.make_async_remote_copy(
        src_ref=other_own.at[0],
        dst_ref=other_own.at[1],
        send_sem=psend,
        recv_sem=precv,
        device_id={"seq": partner},
        device_id_type=MESH,
    )
    partial.start()
    for dst in range(nhead):
        sgs[0, dst] = share_of(mine, dst)
        sgs[1, dst] = share_of(theirs, dst)

    def shared_copy(at, shard, from_side, src, dst):
        return pltpu.make_async_remote_copy(
            src_ref=sgs.at[at, dst],
            dst_ref=shared.at[from_side, src],
            send_sem=ssend.at[at, dst],
            recv_sem=srecv.at[from_side, src],
            device_id={"seq": shard, "head": dst},
            device_id_type=MESH,
        )

    for k in range(1, nhead):
        other = lax.rem(hd + k, nhead)
        shared_copy(1, partner, side, hd, other).start()
        shared_copy(0, me, side, hd, other).start()
    for m in range(heads + 3, 2 * heads):
        send_cross(m)
    keep = pltpu.make_async_copy(sgs.at[0, hd], shared.at[side, hd], own_sem)
    keep.start()
    keep.wait()
    partial.wait()
    arrived = [[other_own[1, h, w].astype(F32) for h in range(heads)] for w in range(2)]
    gk_out[...] = jnp.concatenate([mine[0][h] + arrived[0][h] for h in range(heads)], axis=1)
    gv_out[...] = jnp.concatenate([mine[1][h] + arrived[1][h] for h in range(heads)], axis=1)
    for dst in range(nhead):

        @pl.when(hd == dst)
        def _():
            shared[1 - side, dst] = share_of(arrived, dst)

    for k in range(1, nhead):
        other = lax.rem(hd + k, nhead)
        for at, shard in ((1, partner), (0, me)):
            shared_copy(at, shard, side, hd, other).wait_send()
        for from_side in range(2):
            shared_copy(0, me, from_side, other, other).wait_recv()
        pltpu.make_async_remote_copy(
            src_ref=out.at[pl.ds(other * heads, heads)],
            dst_ref=out.at[pl.ds(other * heads, heads)],
            send_sem=asend.at[0, 0],
            recv_sem=arecv.at[other],
            device_id={"head": other},
            device_id_type=MESH,
        ).wait_recv()

    for copy in early:
        copy.wait_send()
    for m in range(heads - 1, 2 * heads):
        wait_cross(m)
    for c in range(2):
        for core, blocks in ((0, EARLY), (1, EARLY - 1)):

            @pl.when(lax.rem(hd, 2) == core)
            def _():
                pltpu.make_async_remote_copy(
                    src_ref=tri.at[c, :blocks],
                    dst_ref=tri.at[c, :blocks],
                    send_sem=tsend.at[0],
                    recv_sem=trecv.at[c],
                    device_id={"head": other_chip},
                    device_id_type=MESH,
                ).wait_recv()

    for h in range(heads):
        tile_copy(h, hd + 1 - 2 * lax.rem(hd, 2)).wait_send()
    for h in range(heads):
        pltpu.make_async_copy(stage.at[h, hd], out.at[hd * heads + h], local_sem.at[h]).wait()

    for w in range(2):
        swap_copy(w, side).wait_send()
        direct_copy(w, side, place if w == 0 else slab, 1).wait_send()
    for h in range(heads):
        for kind in range(4):
            gather_each(kind, h, "sent")

        def term_sent(k, _, h=h):
            term_copy(h, to_earlier(k), plane).wait_send()
            return 0

        lax.fori_loop(1, earlier, term_sent, 0)


def finish_kernel(
    part, pieces, shared_ref, tri, gk_in, gv_in, q_out, k_out, v_out, gk_out, gv_out, k_buf, v_buf, sem
):
    heads = pieces.shape[0]
    cols = 2 * shared_ref.shape[3]
    group = cols // HEAD_DIM
    copies = [
        pltpu.make_async_copy(gk_in, gk_out, sem.at[0]),
        pltpu.make_async_copy(gv_in, gv_out, sem.at[1]),
    ]
    for h in range(heads):
        copies.append(
            pltpu.make_async_copy(
                pieces.at[h, 0], q_out.at[:, pl.ds(h * HEAD_DIM, HEAD_DIM)], sem.at[2 + h]
            )
        )
    for copy in copies:
        copy.start()
    chip = lax.axis_index("head") // 2
    core = lax.rem(lax.axis_index("head"), 2)
    head_of = [lax.rem(2 * (1 - chip) + g, heads // group) for g in range(heads // group)]
    lane = lax.broadcasted_iota(jnp.int32, (SPAN, 2 * SPAN), 1)
    low = lane < SPAN
    t_id = lax.rem(lane, SPAN)
    u_id = lax.broadcasted_iota(jnp.int32, (SPAN, 2 * SPAN), 0)
    shares = [
        shared_ref[0, g].astype(F32) + shared_ref[1, g].astype(F32) for g in head_of
    ]
    for g in range(heads // group):
        for b in range(group):
            h = g * group + b
            slot = head_of[g] * group + b
            cols_of = slice(h * HEAD_DIM, (h + 1) * HEAD_DIM)

            def share(w, c, b=b, g=g):
                at = (2 * w + b // 2) * part + c
                sl = slice((b % 2) * HEAD_DIM, (b % 2 + 1) * HEAD_DIM)
                return shares[g][at : at + 1, sl]

            def as_sent(slot=slot, cols_of=cols_of, share=share):
                for w, buf in ((0, k_buf), (1, v_buf)):
                    for c in range(part):
                        rows = slice(c * SPAN, (c + 1) * SPAN)
                        buf[rows, cols_of] = (pieces[slot, 1 + w, rows].astype(F32) + share(w, c)).astype(BF16)

            def multiply(slot=slot, g=g, e=b - (group - EARLY), cols_of=cols_of, share=share):
                for p in range(part // 2):
                    rows = slice(p * 2 * SPAN, (p + 1) * 2 * SPAN)
                    block = tri[g, e, :SPAN, rows].astype(F32)
                    main = tri[g, e, SPAN : SPAN + 1, rows].astype(F32)
                    upper = jnp.where(u_id <= t_id, block, 0.0)
                    lower = jnp.where(u_id > t_id, block, jnp.where(u_id == t_id, main, 0.0))
                    for w, buf, x, dims, factor in (
                        (0, k_buf, upper, NN, HEAD_DIM ** (-0.5)),
                        (1, v_buf, lower, TN, 1.0),
                    ):
                        wide = jnp.concatenate(
                            [jnp.where(low, x, 0.0), jnp.where(low, 0.0, x)], axis=0
                        ).astype(BF16)
                        grad = dot(wide, pieces[slot, 1 + w, rows], dims) * factor
                        for c in range(2):
                            at = slice((2 * p + c) * SPAN, (2 * p + c + 1) * SPAN)
                            buf[at, cols_of] = (
                                grad[c * SPAN : (c + 1) * SPAN] + share(w, 2 * p + c)
                            ).astype(BF16)

            if g > 1 or b < group - EARLY:
                as_sent()
            elif b < group - 1:
                multiply()
            else:
                pl.when(core != 0)(as_sent)
                pl.when(core == 0)(multiply)
        sl = pl.ds(g * cols, cols)
        for w, (buf, ref) in enumerate(((k_buf, k_out), (v_buf, v_out))):
            copy = pltpu.make_async_copy(
                buf.at[:, sl],
                ref.at[:, pl.ds(pl.multiple_of(head_of[g] * cols, cols), cols)],
                sem.at[2 + heads + 2 * g + w]
            )
            copy.start()
            copies.append(copy)
    for copy in copies:
        copy.wait()


def per_device(queries, keys, values, out_grad):
    count, cols = queries.shape
    nseq = lax.axis_size("seq")
    nhead = lax.axis_size("head")
    heads = cols // HEAD_DIM
    per_dev = count // SPAN
    total = per_dev * nseq
    tile = count // nhead
    part = per_dev // nhead
    nplane = nseq // 2
    anyspace = pl.BlockSpec(memory_space=pl.ANY)
    hbm = pl.BlockSpec(memory_space=pltpu.HBM)
    vmem = pl.BlockSpec(memory_space=pltpu.VMEM)
    dma = pltpu.SemaphoreType.DMA
    pieces, grad_k, grad_v, shared, tri = pl.pallas_call(
        functools.partial(main_kernel, nseq, nhead),
        out_shape=(
            pltpu.VMEM((nhead * heads, 3, tile, HEAD_DIM), BF16),
            jax.ShapeDtypeStruct((per_dev, cols), F32),
            jax.ShapeDtypeStruct((per_dev, cols), F32),
            jax.ShapeDtypeStruct((2, nhead, 4 * part, cols // 2), BF16),
            jax.ShapeDtypeStruct((2, EARLY, SPAN + 16, tile), BF16),
        ),
        in_specs=[hbm] * 4,
        out_specs=(vmem, vmem, vmem, vmem, vmem),
        scratch_shapes=[pltpu.VMEM((count, cols), BF16)] * 4
        + [
            pltpu.VMEM((heads, nplane // PLACES, PLACES, 2, per_dev, HEAD_DIM), BF16),
            pltpu.VMEM((heads, PLACES, nplane // PLACES, 2, per_dev, HEAD_DIM), BF16),
            pltpu.VMEM((HEAD_DIM, total), BF16),
            pltpu.VMEM((2, total, HEAD_DIM), F32),
            pltpu.VMEM((nplane, heads, 2, 2, per_dev, HEAD_DIM), BF16),
            pltpu.VMEM((nplane, heads, 2, 2, per_dev, HEAD_DIM), BF16),
            pltpu.VMEM((2, heads, 2, per_dev, HEAD_DIM), F32),
            pltpu.VMEM((2, heads, 2, per_dev, HEAD_DIM), BF16),
            pltpu.VMEM((2, nhead, 4 * part, cols // 2), BF16),
            pltpu.VMEM((heads, nhead, 3, tile, HEAD_DIM), BF16),
            pltpu.VMEM((EARLY + 1, 2, SPAN + 16, tile), BF16),
            pltpu.VMEM((2, total, tile), F32),
            pltpu.VMEM((2, total, tile), F32),
            dma((4, nhead)),
            dma((2,)),
            dma((2,)),
            dma((4, heads, PLACES)),
            dma((4, heads, PLACES)),
            dma((heads, nplane)),
            dma((heads, nplane)),
            dma,
            dma,
            dma((heads, nhead)),
            dma((nhead,)),
            dma((heads,)),
            dma((2, nhead)),
            dma((2, nhead)),
            dma,
            dma((EARLY, 2, 2)),
            dma((2 * EARLY,)),
            dma((2,)),
        ],
        compiler_params=pltpu.CompilerParams(
            collective_id=0, has_side_effects=True, vmem_limit_bytes=50 * 1024 * 1024
        ),
        name="attend",
    )(queries, keys, values, out_grad)
    row = jax.ShapeDtypeStruct((tile, nhead * cols), BF16)
    block = jax.ShapeDtypeStruct((per_dev, cols), F32)
    query_grad, key_grad, value_grad, grad_k, grad_v = pl.pallas_call(
        functools.partial(finish_kernel, part),
        out_shape=(row, row, row, block, block),
        in_specs=[vmem, vmem, vmem, vmem, vmem],
        out_specs=(hbm,) * 5,
        scratch_shapes=[
            pltpu.VMEM((tile, nhead * cols), BF16),
            pltpu.VMEM((tile, nhead * cols), BF16),
            dma((2 + nhead * heads + 2 * nhead,)),
        ],
        compiler_params=pltpu.CompilerParams(vmem_limit_bytes=50 * 1024 * 1024),
        name="finish",
    )(pieces, shared, tri, grad_k, grad_v)
    return (query_grad, key_grad, value_grad, grad_k, grad_v)


def solution(mesh):
    placed = (P("seq", "head"), P("seq", "head"), P("seq", "head"), P("seq", "head"))
    return jax.shard_map(
        per_device,
        mesh=mesh,
        in_specs=placed,
        out_specs=(
            P(("seq", "head"), None),
            P(("seq", "head"), None),
            P(("seq", "head"), None),
            P("seq", "head"),
            P("seq", "head"),
        ),
        check_vma=False,
    )
```
